128 devices in a mesh: gx: 16 (over y, x), gy: 8 (over z, core).
Axes of the slice: x: 4, y: 4, z: 4, core: 2. Of those that a mesh axis runs over, the one named last changes fastest.
Arguments:
- tracer: float32 [12, 960, 5760], P(None, 'gy', 'gx'), may hold values from -6 to 6
- east_velocity: float32 [12, 960, 5760], P(None, 'gy', 'gx'), may hold values from -3 to 3
- north_velocity: float32 [12, 960, 5760], P(None, 'gy', 'gx'), may hold values from -3 to 3
- kmt: int32 [960, 5760], P('gy', 'gx'), may hold values from 0 to 12, as said below
- block_mask: int32 [16, 64], P('gy', 'gx'), may hold values 0 or 1
- surface_forcing: float32 [960, 5760], P('gy', 'gx'), may hold values from -6 to 6
Outputs:
- updated: float32 [12, 960, 5760], P(None, 'gy', 'gx')
- sea_level: float32 [960, 5760], P('gy', 'gx')
- residual: float32 [960, 5760], P('gy', 'gx')
The draws below stay inside these ranges and needn't reach their ends.
Inputs may be any that keep to these rules, and one draw needn't show every extreme that they name: `kmt`: zero on the grid's first and last rows.
All inputs are finite; a program needn't handle non-finite values. No bound on the sum of `block_mask` on one device may be relied on, other than what follows from the above.
Results may differ from the reference program's by a relative error of at most 0.0003.
Values sent between devices are 32-bit elements; how exact they have to be, the bound alone decides.
No kernel may reach another device: no remote copies, remote signals or barrier semaphores. Data moves between devices by JAX's collectives and lax.ppermute only.
A program may use at most 128 MiB of HBM per device.

```python
import math
import jax
import jax.numpy as jnp
from jax import lax

BSX = 90
BSY = 60
KL = 12
ITERS = 8
NBX = 64
NBY = 16
NX = 5760
NY = 960


def draw_kmt(key, part):
    key = jax.random.fold_in(key, 7)
    raw = jax.random.randint(key, (NY, NX), -(KL // 2), KL + 1)
    rows = jnp.arange(NY)[:, None]
    inner = (rows > 0) & (rows < NY - 1)
    return jnp.where(inner, jnp.maximum(raw, 0), 0).astype(jnp.int32)


def with_ends(result, stream_key, least, largest):
    dims = result.shape
    place = [jax.random.randint(jax.random.fold_in(stream_key, axis), (), 0, dims[axis]) for axis in range(len(dims))]
    result = result.at[tuple(place)].set(least)
    longest = dims.index(max(dims))
    place[longest] = (place[longest] + 1) % dims[longest]
    return result.at[tuple(place)].set(largest)


def block_levels(key, dims, split, least, high):
    loudness, own = 1.0, jax.random.fold_in(key, 6)
    for axis_at, shards_of in split:
        draws = jnp.exp(jax.random.uniform(jax.random.fold_in(own, axis_at), (shards_of,), jnp.float32, least / len(split), high / len(split)))
        loudness = loudness * jnp.repeat(draws, dims[axis_at] // shards_of).reshape([-1 if axis == axis_at else 1 for axis in range(len(dims))])
    return loudness


def normal_values(rng, extent, width, reach, pieces=(), held_as=jnp.bfloat16):
    drawn = width * jax.random.normal(rng, extent, jnp.float32)
    if pieces:
        drawn = drawn * block_levels(rng, extent, pieces, -0.22, 0.18)
    return jnp.clip(drawn, -reach, reach).astype(held_as)


def setup_inputs(seed: int = 0) -> dict:
    keys = jax.random.split(jax.random.key(seed), 7)
    return {
        "tracer": normal_values(keys[0], (KL, NY, NX), 1.0, 6.0, ((1, 8), (2, 16)), jnp.float32),
        "east_velocity": normal_values(keys[1], (KL, NY, NX), 0.5, 3.0, ((1, 8), (2, 16)), jnp.float32),
        "north_velocity": normal_values(keys[2], (KL, NY, NX), 0.5, 3.0, ((1, 8), (2, 16)), jnp.float32),
        "kmt": draw_kmt(jax.random.fold_in(keys[6], 71), 0),
        "block_mask": with_ends((jax.random.randint(keys[4], (NBY, NBX), 0, 4) < 3).astype(jnp.int32), jax.random.fold_in(keys[4], 1), 0, 1),
        "surface_forcing": normal_values(keys[5], (NY, NX), 1.0, 6.0, ((0, 8), (1, 16)), jnp.float32),
    }


DT_STEP = 0.2
KAPPA_H = 0.2
KAPPA_V = 0.3
SHIFT = 0.002

def tracer_update(tracer_pad, east_pad, north_pad, ocean_pad):
    middle_rows = tracer_pad[:, 1:-1, :]
    east_rows = east_pad[:, 1:-1, :]
    ocean_rows = ocean_pad[:, 1:-1, :]
    open_east = ocean_rows[:, :, :-1] * ocean_rows[:, :, 1:]
    flux_east = (KAPPA_H * (middle_rows[:, :, 1:] - middle_rows[:, :, :-1]) - east_rows[:, :, :-1] * 0.5 * (middle_rows[:, :, :-1] + middle_rows[:, :, 1:])) * open_east
    middle_cols = tracer_pad[:, :, 1:-1]
    north_cols = north_pad[:, :, 1:-1]
    ocean_cols = ocean_pad[:, :, 1:-1]
    open_north = ocean_cols[:, :-1, :] * ocean_cols[:, 1:, :]
    flux_north = (KAPPA_H * (middle_cols[:, 1:, :] - middle_cols[:, :-1, :]) - north_cols[:, :-1, :] * 0.5 * (middle_cols[:, :-1, :] + middle_cols[:, 1:, :])) * open_north
    horizontal = flux_east[:, :, 1:] - flux_east[:, :, :-1] + flux_north[:, 1:, :] - flux_north[:, :-1, :]
    center = tracer_pad[:, 1:-1, 1:-1]
    ocean = ocean_pad[:, 1:-1, 1:-1]
    flux_down = KAPPA_V * (center[1:] - center[:-1]) * (ocean[:-1] * ocean[1:])
    vertical = jnp.pad(flux_down, ((0, 1), (0, 0), (0, 0))) - jnp.pad(flux_down, ((1, 0), (0, 0), (0, 0)))
    return center + DT_STEP * ocean * (horizontal + vertical)

def face_weights(depth_pad, wet_pad):
    wet_rows = wet_pad[1:-1, :]
    depth_rows = depth_pad[1:-1, :]
    east_face = wet_rows[:, :-1] * wet_rows[:, 1:] * 0.5 * (depth_rows[:, :-1] + depth_rows[:, 1:])
    wet_cols = wet_pad[:, 1:-1]
    depth_cols = depth_pad[:, 1:-1]
    north_face = wet_cols[:-1, :] * wet_cols[1:, :] * 0.5 * (depth_cols[:-1, :] + depth_cols[1:, :])
    depth = depth_pad[1:-1, 1:-1]
    wet = wet_pad[1:-1, 1:-1]
    diagonal = SHIFT * depth + east_face[:, 1:] + east_face[:, :-1] + north_face[1:, :] + north_face[:-1, :]
    diagonal = jnp.where(wet > 0.5, diagonal, jnp.float32(1.0))
    return (east_face, north_face, diagonal)

def apply_operator(field_pad, east_face, north_face, diagonal):
    center = field_pad[1:-1, 1:-1]
    beside = east_face[:, 1:] * field_pad[1:-1, 2:] + east_face[:, :-1] * field_pad[1:-1, :-2]
    beside = beside + north_face[1:, :] * field_pad[2:, 1:-1] + north_face[:-1, :] * field_pad[:-2, 1:-1]
    return diagonal * center - beside

def wrap_three(array):
    return jnp.pad(array, ((0, 0), (1, 1), (1, 1)), mode='wrap')

def reference(tracer, east_velocity, north_velocity, kmt, block_mask, surface_forcing):
    keep = jnp.repeat(jnp.repeat(block_mask, BSY, axis=0), BSX, axis=1)
    levels = kmt * keep
    levels_pad = jnp.pad(levels, 1, mode='wrap')
    ocean_pad = (jnp.arange(KL, dtype=jnp.int32)[:, None, None] < levels_pad[None]).astype(jnp.float32)
    updated = tracer_update(wrap_three(tracer), wrap_three(east_velocity), wrap_three(north_velocity), ocean_pad)
    thick = 1.0 + 0.5 * jnp.arange(KL).astype(jnp.float32) / KL
    depth_pad = lax.optimization_barrier(jnp.sum(thick[:, None, None] * ocean_pad, axis=0))
    wet_pad = (levels_pad > 0).astype(jnp.float32)
    column = lax.optimization_barrier(jnp.sum(thick[:, None, None] * ocean_pad[:, 1:-1, 1:-1] * updated, axis=0)) / math.sqrt(KL)
    rhs = wet_pad[1:-1, 1:-1] * (column + surface_forcing)
    east_face, north_face, diagonal = face_weights(depth_pad, wet_pad)
    sea_level = jnp.zeros_like(rhs)
    residual = rhs
    precond = residual / diagonal
    direction = precond
    norm_now = jnp.sum(residual * precond)
    for step in range(ITERS):
        image = apply_operator(jnp.pad(direction, 1, mode='wrap'), east_face, north_face, diagonal)
        alpha = norm_now / jnp.sum(direction * image)
        sea_level = sea_level + alpha * direction
        residual = residual - alpha * image
        precond = residual / diagonal
        norm_next = jnp.sum(residual * precond)
        direction = precond + norm_next / norm_now * direction
        norm_now = norm_next
    return (updated, sea_level, residual)
```

```python
import math

import jax
import jax.numpy as jnp
from jax import lax
from jax.experimental import pallas as pl
from jax.experimental.pallas import tpu as pltpu
from jax.sharding import PartitionSpec as P

BSX = 90
BSY = 60
KL = 12
ITERS = 8

DT_STEP = 0.2
KAPPA_H = 0.2
KAPPA_V = 0.3
SHIFT = 0.002

H = 120
W = 360
LW = 384
EH = 144

GRAD = DT_STEP * KAPPA_H
ADV = DT_STEP * 0.5
VERT = DT_STEP * KAPPA_V
ROOT = 1.0 / math.sqrt(KL)

LEV0 = 8
TR0 = 17
VE0 = 29
C_T0 = 48
C_T1 = 56
C_V1 = 64

R_LEV = 8
R_TR = 24
R_VE = 40

F32 = jnp.float32
VMEM_LIMIT = 40 * 1024 * 1024


def lanes(shape):
    return lax.broadcasted_iota(jnp.int32, shape, 1)


def rows(shape):
    return lax.broadcasted_iota(jnp.int32, shape, 0)


def widen(x, width):
    return jnp.concatenate([x, jnp.zeros((x.shape[0], width - x.shape[1]), x.dtype)], axis=1)


def roll(x, shift, axis):
    shift = shift % x.shape[axis]
    return x if shift == 0 else pltpu.roll(x, shift, axis)


def thickness(level):
    return 1.0 + (0.5 / KL) * level


def tracer_kernel(
    mask_ref, kmt_ref, forcing_ref, t_hbm, u_hbm, v_hbm,
    upd_hbm, rhs_ref, lev_ref, msg_e, msg_w, row_n, row_s,
    t_s, u_s, v_s, o_s, min_e, min_n, col, sem_in, sem_out,
):
    def load(i, k):
        src, dst = ((t_hbm, t_s), (u_hbm, u_s), (v_hbm, v_s))[i]
        return pltpu.make_async_copy(src.at[k], dst.at[k], sem_in.at[i, k])

    def store(k):
        return pltpu.make_async_copy(o_s.at[k], upd_hbm.at[k], sem_out.at[k])

    for k in range(KL):
        for i in range(3):
            load(i, k).start()

    lane = lanes((8, LW))
    row = rows((8, LW))
    for r in range(0, H, 8):
        keep = jnp.zeros((8, LW), jnp.int32)
        for b in range(W // BSX):
            inside = (lane >= b * BSX) & (lane < (b + 1) * BSX)
            upper = jnp.where(row + r < BSY, mask_ref[0, b], mask_ref[1, b])
            keep = jnp.where(inside, upper, keep)
        lev = widen(kmt_ref[r : r + 8, :], LW) * keep
        lev_ref[r : r + 8, :] = lev.astype(F32)
    for r in range(0, H, 8):
        lev = lev_ref[r : r + 8, :]
        if r + 8 < H:
            north = lev_ref[r + 1 : r + 9, :]
        else:
            north = jnp.where(row == 7, 0.0, roll(lev, -1, 0))
        min_e[r : r + 8, :] = jnp.minimum(lev, roll(lev, -1, 1))
        min_n[r : r + 8, :] = jnp.minimum(lev, north)
        col[r : r + 8, :] = jnp.zeros((8, LW), F32)
    row_n[...] = jnp.zeros((32, LW), F32)
    row_s[...] = jnp.zeros((16, LW), F32)

    load(0, 0).wait()
    row360 = rows((8, W))

    def level(k, carry):
        above = jnp.minimum(k + 1, KL - 1)
        below = jnp.maximum(k - 1, 0)

        @pl.when(k < KL - 1)
        def _():
            load(0, above).wait()

        load(1, k).wait()
        load(2, k).wait()
        kf = k.astype(F32)
        thick = thickness(kf)
        before = jnp.zeros((8, W), F32)
        for r in range(0, H, 8):
            here = slice(r, r + 8)
            t = t_s[k, here, :]
            t_e = roll(widen(t, LW), -1, 1)[:, :W]
            if r + 8 < H:
                t_n = t_s[k, r + 1 : r + 9, :]
            else:
                t_n = roll(t, -1, 0)
            u = u_s[k, here, :]
            v = v_s[k, here, :]
            lev = lev_ref[here, :W]
            f_e = jnp.where(min_e[here, :W] > kf, GRAD * (t_e - t) - (ADV * u) * (t + t_e), 0.0)
            f_n = jnp.where(min_n[here, :W] > kf, GRAD * (t_n - t) - (ADV * v) * (t + t_n), 0.0)
            f_w = roll(widen(f_e, LW), 1, 1)[:, :W]
            shifted = roll(f_n, 1, 0)
            f_s = jnp.where(row360 == 0, before, shifted)
            before = shifted
            wet = lev > kf
            up = jnp.where(lev > kf + 1.0, t_s[above, here, :] - t, 0.0)
            down = jnp.where(wet, t - t_s[below, here, :], 0.0)
            updated = t + ((f_e - f_w) + (f_n - f_s) + VERT * (up - down))
            o_s[k, here, :] = updated
            col[here, :W] += jnp.where(wet, thick * updated, 0.0)
        store(k).start()
        row_s[pl.ds(k, 1), :] = widen(t_s[k, 0:1, :], LW)
        row_n[pl.ds(k, 1), :] = widen(t_s[k, H - 1 : H, :], LW)
        row_n[pl.ds(16 + k, 1), :] = widen(v_s[k, H - 1 : H, :], LW)
        return carry

    lax.fori_loop(0, KL, level, 0)

    lane = lanes((8, 128))
    for r in range(0, H, 8):
        here = slice(r, r + 8)
        lev = lev_ref[here, :]
        rhs = jnp.where(
            lev > 0.0, ROOT * col[here, :] + widen(forcing_ref[here, :], LW), 0.0
        )
        rhs_ref[here, :] = rhs
        east = jnp.where(lane < LEV0, roll(rhs[:, 256:], 32, 1), roll(lev[:, 256:], LEV0 - 95, 1))
        west = jnp.where(lane < LEV0, rhs[:, :128], roll(lev[:, :128], LEV0, 1))
        east = jnp.where(lane < TR0, east, 0.0)
        west = jnp.where(lane < TR0, west, 0.0)
        for k in range(KL):
            t2 = roll(widen(t_s[k, here, 256:W], 128), TR0 + k - 103, 1)
            u2 = roll(widen(u_s[k, here, 256:W], 128), VE0 + k - 103, 1)
            t0 = roll(t_s[k, here, :128], TR0 + k, 1)
            east = jnp.where(lane == TR0 + k, t2, east)
            east = jnp.where(lane == VE0 + k, u2, east)
            west = jnp.where(lane == TR0 + k, t0, west)
        if r < 16:
            for at, src, base in ((C_T0, row_s, 0), (C_T1, row_n, 0), (C_V1, row_n, 16)):
                inside = (lane >= at) & (lane < at + 8)
                piece = src[base + r : base + r + 8, :]
                east = jnp.where(inside, roll(piece[:, 256:], at - 96, 1), east)
                west = jnp.where(inside, roll(piece[:, :128], at, 1), west)
        msg_e[here, :] = east
        msg_w[here, :] = west

    def drain(k, carry):
        store(k).wait()
        return carry

    lax.fori_loop(0, KL, drain, 0)


def tracer_part(mask, kmt, forcing, tracer, east, north):
    vmem = pl.BlockSpec(memory_space=pltpu.VMEM)
    hbm = pl.BlockSpec(memory_space=pl.ANY)
    shape = jax.ShapeDtypeStruct
    return pl.pallas_call(
        tracer_kernel,
        out_shape=[
            shape((KL, H, W), F32),
            shape((H, LW), F32),
            shape((H, LW), F32),
            shape((H, 128), F32),
            shape((H, 128), F32),
            shape((32, LW), F32),
            shape((16, LW), F32),
        ],
        in_specs=[pl.BlockSpec(memory_space=pltpu.SMEM), vmem, vmem, hbm, hbm, hbm],
        out_specs=[hbm] + [vmem] * 6,
        scratch_shapes=[pltpu.VMEM((KL, H, W), F32)] * 4
        + [pltpu.VMEM((H, LW), F32)] * 3
        + [pltpu.SemaphoreType.DMA((3, KL)), pltpu.SemaphoreType.DMA((KL,))],
        compiler_params=pltpu.CompilerParams(vmem_limit_bytes=VMEM_LIMIT),
        name="tracer",
    )(mask, kmt, forcing, tracer, east, north)


def sides_kernel(
    from_w, from_e, own_e, own_w, rhs_ref, lev_ref, row_n, row_s,
    rhs_x, lev_x, msg_n, msg_s, flux_e, flux_w,
):
    lane = lanes((8, 128))
    kf = (lane - TR0).astype(F32)
    inside = (lane >= TR0) & (lane < TR0 + KL)
    weight = ROOT * thickness(kf)
    for r in range(0, H, 8):
        here = slice(r, r + 8)
        mw, me = from_w[here, :], from_e[here, :]
        mine_e, mine_w = own_e[here, :], own_w[here, :]
        lev0 = jnp.minimum(mw[:, LEV0 + 8 : LEV0 + 9], mine_w[:, LEV0 : LEV0 + 1])
        lev1 = jnp.minimum(me[:, LEV0 : LEV0 + 1], mine_e[:, LEV0 + 8 : LEV0 + 9])
        f_w = GRAD * (mine_w - mw) - (ADV * roll(mw, TR0 - VE0, 1)) * (mine_w + mw)
        f_e = GRAD * (me - mine_e) - (ADV * roll(mine_e, TR0 - VE0, 1)) * (me + mine_e)
        f_w = jnp.where(inside & (lev0 > kf), f_w, 0.0)
        f_e = jnp.where(inside & (lev1 > kf), f_e, 0.0)
        flux_w[here, :] = f_w
        flux_e[here, :] = f_e
        c_w = jnp.sum(weight * f_w, axis=1, keepdims=True)
        c_e = jnp.sum(weight * f_e, axis=1, keepdims=True)
        rhs_x[here, :128] = rhs_ref[here, :128] - jnp.where(lane == 0, c_w, 0.0)
        rhs_x[here, 128:256] = rhs_ref[here, 128:256]
        last = rhs_ref[here, 256:]
        last = jnp.where((lane >= 104) & (lane < 112), roll(me, 104, 1), last)
        last = jnp.where(lane >= 120, roll(mw, 120, 1), last)
        last = last + jnp.where(lane == 103, c_e, 0.0) - jnp.where(lane == 104, c_e, 0.0)
        rhs_x[here, 256:] = last + jnp.where(lane == 127, c_w, 0.0)
        lev_x[here, :256] = lev_ref[here, :256]
        last = lev_ref[here, 256:]
        last = jnp.where((lane >= 104) & (lane < 113), roll(me, 104 - LEV0, 1), last)
        last = jnp.where(lane >= 119, roll(mw, 119 - LEV0, 1), last)
        lev_x[here, 256:] = last
    msg_n[0:8, :] = rhs_x[H - 8 : H, :]
    msg_s[0:8, :] = rhs_x[0:8, :]
    msg_n[R_LEV : R_LEV + 16, :] = lev_x[H - 16 : H, :]
    msg_s[R_LEV : R_LEV + 16, :] = lev_x[0:16, :]
    for dst, at, src, base, lane0 in (
        (msg_s, R_TR, row_s, 0, C_T0), (msg_n, R_TR, row_n, 0, C_T1), (msg_n, R_VE, row_n, 16, C_V1),
    ):
        for r in (0, 8):
            mw, me = from_w[r : r + 8, :], from_e[r : r + 8, :]
            piece = src[base + r : base + r + 8, :]
            last = piece[:, 256:]
            last = jnp.where((lane >= 104) & (lane < 112), roll(me, 104 - lane0, 1), last)
            last = jnp.where(lane >= 120, roll(mw, 120 - lane0, 1), last)
            dst[at + r : at + r + 8, :256] = piece[:, :256]
            dst[at + r : at + r + 8, 256:] = last


def sides_part(from_w, from_e, own_e, own_w, rhs, lev, row_n, row_s):
    vmem = pl.BlockSpec(memory_space=pltpu.VMEM)
    shape = jax.ShapeDtypeStruct
    return pl.pallas_call(
        sides_kernel,
        out_shape=[
            shape((H, LW), F32),
            shape((H, LW), F32),
            shape((56, LW), F32),
            shape((40, LW), F32),
            shape((H, 128), F32),
            shape((H, 128), F32),
        ],
        in_specs=[vmem] * 8,
        out_specs=[vmem] * 6,
        compiler_params=pltpu.CompilerParams(vmem_limit_bytes=VMEM_LIMIT),
        name="sides",
    )(from_w, from_e, own_e, own_w, rhs, lev, row_n, row_s)


def basis_kernel(
    from_s, from_n, own_n, own_s, rhs_ref, lev_ref,
    basis, diag, sums, flux_n, flux_s,
    depth, face_e, face_n, w_e, w_w, w_n, w_s, weight, parts,
):
    lev_row = rows((16, LW))
    kf = lev_row.astype(F32)
    factor = ROOT * thickness(kf)

    def face(t_from, t_to, vel, lev):
        flux = GRAD * (t_to - t_from) - (ADV * vel) * (t_from + t_to)
        return jnp.where((lev_row < KL) & (lev > kf), flux, 0.0)

    tr = slice(R_TR, R_TR + 16)
    ve = slice(R_VE, R_VE + 16)
    lev_n = jnp.minimum(lev_ref[H - 1 : H, :], from_n[R_LEV : R_LEV + 1, :])
    lev_s = jnp.minimum(lev_ref[0:1, :], from_s[R_LEV + 15 : R_LEV + 16, :])
    f_n = face(own_n[tr, :], from_n[tr, :], own_n[ve, :], lev_n)
    f_s = face(from_s[tr, :], own_s[tr, :], from_s[ve, :], lev_s)
    flux_n[...] = f_n
    flux_s[...] = f_s
    c_n = jnp.sum(factor * f_n, axis=0, keepdims=True)
    c_s = jnp.sum(factor * f_s, axis=0, keepdims=True)

    row = rows((8, LW))
    lane = lanes((8, LW))

    def level_rows(r):
        if r < H:
            return lev_ref[r : r + 8, :]
        if r == H:
            return from_n[R_LEV : R_LEV + 8, :]
        if r == H + 8:
            first = from_n[R_LEV + 8 : R_LEV + 9, :]
            last = from_s[R_LEV + 7 : R_LEV + 8, :]
            return jnp.where(row == 0, first, jnp.where(row == 7, last, 0.0))
        return from_s[R_LEV + 8 : R_LEV + 16, :]

    def rhs_rows(r):
        if r < H:
            value = rhs_ref[r : r + 8, :]
            if r == 0:
                value = value - jnp.where(row == 0, c_s, 0.0)
            if r == H - 8:
                value = value + jnp.where(row == 7, c_n, 0.0)
            return value
        if r == H:
            return from_n[0:8, :] - jnp.where(row == 0, c_n, 0.0)
        if r == H + 8:
            return jnp.zeros((8, LW), F32)
        return from_s[0:8, :] + jnp.where(row == 7, c_s, 0.0)

    def north(ref, r):
        if r + 8 < EH:
            return ref[r + 1 : r + 9, :]
        return jnp.where(row == 7, roll(ref[0:8, :], -1, 0), roll(ref[r : r + 8, :], -1, 0))

    def south(ref, r):
        if r > 0:
            return ref[r - 1 : r + 7, :]
        return jnp.where(row == 0, roll(ref[EH - 8 : EH, :], 1, 0), roll(ref[0:8, :], 1, 0))

    for r in range(0, EH, 8):
        lev = level_rows(r)
        depth[r : r + 8, :] = lev + lev * (lev - 1.0) * (0.25 / KL)
    for r in range(0, EH, 8):
        here = slice(r, r + 8)
        d = depth[here, :]
        d_e, d_n = roll(d, -1, 1), north(depth, r)
        face_e[here, :] = jnp.where((d > 0.0) & (d_e > 0.0), 0.5 * (d + d_e), 0.0)
        face_n[here, :] = jnp.where((d > 0.0) & (d_n > 0.0), 0.5 * (d + d_n), 0.0)
    lone = jnp.zeros((8, LW), F32)
    for r in range(0, EH, 8):
        here = slice(r, r + 8)
        d = depth[here, :]
        e, n = face_e[here, :], face_n[here, :]
        w = roll(e, 1, 1)
        s = south(face_n, r)
        faces = e + w + n + s
        dg = jnp.where(d > 0.0, SHIFT * d + faces, 1.0)
        inv = 1.0 / dg
        z = rhs_rows(r) * inv
        basis[0, here, :] = z
        w_e[here, :] = e * inv
        w_w[here, :] = w * inv
        w_n[here, :] = n * inv
        w_s[here, :] = s * inv
        if r < H:
            diag[here, :] = dg
            own = jnp.where(lane < W, dg, 0.0)
            joined = faces > 0.0
            weight[here, :] = jnp.where(joined, own, 0.0)
            lone = lone + jnp.where(joined, 0.0, own * z * z)

    def fold(x):
        return jnp.sum(x[:, :128] + x[:, 128:256] + x[:, 256:], axis=0, keepdims=True)

    parts[...] = jnp.zeros((24, 128), F32)
    parts[16:17, :] = fold(lone)

    def step(k, carry):
        first = k == 1
        twice = jnp.where(first, 1.0, 2.0)
        keep = jnp.where(first, 0.0, 1.0)
        older = jnp.maximum(k - 2, 0)
        now = basis.at[k - 1]
        even = jnp.zeros((8, LW), F32)
        odd = jnp.zeros((8, LW), F32)
        for r in range(0, EH, 8):
            here = slice(r, r + 8)
            c = now[here, :]
            image = w_e[here, :] * roll(c, -1, 1) + w_w[here, :] * roll(c, 1, 1)
            image = image + (w_n[here, :] * north(now, r) + w_s[here, :] * south(now, r))
            value = twice * image - keep * basis[older, here, :]
            basis[k, here, :] = value
            if r < H:
                scaled = weight[here, :] * c
                even = even + scaled * c
                odd = odd + scaled * value
        parts[pl.ds(2 * k - 2, 1), :] = fold(even)
        parts[pl.ds(2 * k - 1, 1), :] = fold(odd)
        return carry

    lax.fori_loop(1, ITERS + 1, step, 0)

    total = jnp.sum(parts[...], axis=1, keepdims=True)
    prow = rows((24, 128))
    plane = lanes((24, 128))
    place = (prow < 16) & ((plane == prow) | (plane == 128 - prow)) | (prow == 16) & (plane == 64)
    line = jnp.sum(jnp.where(place, total, 0.0), axis=0, keepdims=True)
    sums[...] = jnp.broadcast_to(line, sums.shape)


def basis_part(from_s, from_n, own_n, own_s, rhs, lev, count):
    vmem = pl.BlockSpec(memory_space=pltpu.VMEM)
    shape = jax.ShapeDtypeStruct
    return pl.pallas_call(
        basis_kernel,
        out_shape=[
            shape((ITERS + 1, EH, LW), F32),
            shape((H, LW), F32),
            shape((count, 128), F32),
            shape((16, LW), F32),
            shape((16, LW), F32),
        ],
        in_specs=[vmem] * 6,
        out_specs=[vmem] * 5,
        scratch_shapes=[pltpu.VMEM((EH, LW), F32)] * 8 + [pltpu.VMEM((24, 128), F32)],
        compiler_params=pltpu.CompilerParams(vmem_limit_bytes=VMEM_LIMIT),
        name="basis",
    )(from_s, from_n, own_n, own_s, rhs, lev)


def polynomials(gathered):
    sums = jnp.sum(gathered, axis=0, keepdims=True)
    lane = lanes((1, 128))
    alone = sums[:, 64:65]
    distance = jnp.minimum(lane, 128 - lane)
    odd = lax.rem(lane, 2) == 1
    base = jnp.where(odd, sums[:, 1:2], sums[:, 0:1])
    moments = jnp.where(distance < 2, sums, jnp.where(distance < 16, 2.0 * sums - base, 0.0))
    row = rows((8, 128))
    lane = lanes((8, 128))
    quarter = lax.rem(lane, 4)
    origin = jnp.where(quarter == 0, alone, jnp.where(quarter == 2, -alone, 0.0))
    now = jnp.where(row == 0, moments, 0.0)
    now = jnp.where((row == 1) & (lane == 0), 2.0, now)
    now = jnp.where(row == 3, 1.0, now)
    now = jnp.where(row == 4, origin, now)
    before = jnp.zeros((8, 128), F32)
    corner = (row == 2) & (lane == 0)
    last_inv = last_ratio = None
    for k in range(ITERS):
        both = now[0:1, :] + now[4:5, :]
        size = both[:, k : k + 1]
        inv = 1.0 / size
        ratio = both[:, k + 1 : k + 2] * inv * (1.0 if k == 0 else 0.5)
        image = 0.5 * (roll(now, 1, 1) + roll(now, -1, 1))
        image = image + jnp.where(corner, 2.0 * now[3:4, 0:1], 0.0)
        if k == 0:
            after = image - ratio * now
        else:
            shrink = size * last_inv * (1.0 if k == 1 else 0.5)
            after = image - (ratio - last_ratio) * now - shrink * before
        last_inv = inv
        last_ratio = ratio
        before, now = now, after
    scale = 1.0 / now[3:4, 0:1]
    half = jnp.where(lanes((1, 128)) == 0, 0.5, 1.0)
    return now[2:3, :] * half * scale, now[1:2, :] * half * scale


def finish_kernel(gathered, basis, diag, sea, residual):
    lift, rest = polynomials(gathered[...])
    lift = [lift[:, j : j + 1] for j in range(ITERS)]
    rest = [rest[:, j : j + 1] for j in range(ITERS + 1)]
    for r in range(0, H, 8):
        here = slice(r, r + 8)
        c = basis[0, here, :]
        a, b = lift[0] * c, rest[0] * c
        for j in range(1, ITERS + 1):
            c = basis[j, here, :]
            b = b + rest[j] * c
            if j < ITERS:
                a = a + lift[j] * c
        sea[here, :] = a[:, :W]
        residual[here, :] = (diag[here, :] * b)[:, :W]


def finish_part(gathered, basis, diag):
    vmem = pl.BlockSpec(memory_space=pltpu.VMEM)
    shape = jax.ShapeDtypeStruct
    return pl.pallas_call(
        finish_kernel,
        out_shape=[shape((H, W), F32), shape((H, W), F32)],
        in_specs=[vmem] * 3,
        out_specs=[vmem] * 2,
        compiler_params=pltpu.CompilerParams(vmem_limit_bytes=VMEM_LIMIT),
        name="finish",
    )(gathered, basis, diag)


def edges_kernel(partial, flux_e, flux_w, flux_n, flux_s, out):
    k = pl.program_id(0)
    lane = lanes((8, 128))
    wide = lanes((8, W))
    f_n = flux_n[pl.ds(k, 1), :][:, :W]
    f_s = flux_s[pl.ds(k, 1), :][:, :W]
    row = rows((8, W))
    for r in range(0, H, 8):
        here = slice(r, r + 8)
        pick = lane == TR0 + k
        f_e = jnp.sum(jnp.where(pick, flux_e[here, :], 0.0), axis=1, keepdims=True)
        f_w = jnp.sum(jnp.where(pick, flux_w[here, :], 0.0), axis=1, keepdims=True)
        value = partial[0, here, :]
        value = value + jnp.where(wide == W - 1, f_e, 0.0) - jnp.where(wide == 0, f_w, 0.0)
        if r == 0:
            value = value - jnp.where(row == 0, f_s, 0.0)
        if r == H - 8:
            value = value + jnp.where(row == 7, f_n, 0.0)
        out[0, here, :] = value


def edges_part(partial, flux_e, flux_w, flux_n, flux_s):
    level = pl.BlockSpec((1, H, W), lambda k: (k, 0, 0))

    def whole(x):
        return pl.BlockSpec(x.shape, lambda k: (0, 0))

    return pl.pallas_call(
        edges_kernel,
        grid=(KL,),
        out_shape=jax.ShapeDtypeStruct((KL, H, W), F32),
        in_specs=[level] + [whole(x) for x in (flux_e, flux_w, flux_n, flux_s)],
        out_specs=level,
        input_output_aliases={0: 0},
        compiler_params=pltpu.CompilerParams(vmem_limit_bytes=VMEM_LIMIT),
        name="edges",
    )(partial, flux_e, flux_w, flux_n, flux_s)


def shards(tracer, east_velocity, north_velocity, kmt, block_mask, surface_forcing):
    nx, ny = lax.axis_size("gx"), lax.axis_size("gy")
    partial, rhs, lev, msg_e, msg_w, row_n, row_s = tracer_part(
        block_mask, kmt, surface_forcing, tracer, east_velocity, north_velocity
    )
    from_w = lax.ppermute(msg_e, "gx", [(i, (i + 1) % nx) for i in range(nx)])
    from_e = lax.ppermute(msg_w, "gx", [((i + 1) % nx, i) for i in range(nx)])
    rhs_x, lev_x, msg_n, msg_s, flux_e, flux_w = sides_part(
        from_w, from_e, msg_e, msg_w, rhs, lev, row_n, row_s
    )
    from_s = lax.ppermute(msg_n, "gy", [(i, i + 1) for i in range(ny - 1)])
    from_n = lax.ppermute(msg_s, "gy", [(i + 1, i) for i in range(ny - 1)])
    basis, diag, sums, flux_n, flux_s = basis_part(
        from_s, from_n, msg_n, msg_s, rhs_x, lev_x, nx * ny
    )
    updated = edges_part(partial, flux_e, flux_w, flux_n, flux_s)
    gathered = lax.all_to_all(sums, ("gx", "gy"), 0, 0, tiled=True)
    sea_level, residual = finish_part(gathered, basis, diag)
    return (updated, sea_level, residual)


def solution(mesh):
    in_specs = (
        P(None, "gy", "gx"),
        P(None, "gy", "gx"),
        P(None, "gy", "gx"),
        P("gy", "gx"),
        P("gy", "gx"),
        P("gy", "gx"),
    )
    out_specs = (P(None, "gy", "gx"), P("gy", "gx"), P("gy", "gx"))
    return jax.shard_map(shards, mesh=mesh, in_specs=in_specs, out_specs=out_specs, check_vma=False)
```

```python
import math

import jax
import jax.numpy as jnp
from jax import lax
from jax.experimental import pallas as pl
from jax.experimental.pallas import tpu as pltpu
from jax.sharding import PartitionSpec as P

BSX = 90
BSY = 60
KL = 12
ITERS = 8

DT_STEP = 0.2
KAPPA_H = 0.2
KAPPA_V = 0.3
SHIFT = 0.002

H = 120
W = 360
LW = 384
EH = 144

EB = EH // 8

GRAD = DT_STEP * KAPPA_H
ADV = DT_STEP * 0.5
VERT = DT_STEP * KAPPA_V
ROOT = 1.0 / math.sqrt(KL)

LEV0 = 8
TR0 = 17
VE0 = 29
C_T0 = 48
C_T1 = 56
C_V1 = 64

R_LEV = 8
R_TR = 24
R_VE = 40

F32 = jnp.float32
VMEM_LIMIT = 40 * 1024 * 1024


def lanes(shape):
    return lax.broadcasted_iota(jnp.int32, shape, 1)


def rows(shape):
    return lax.broadcasted_iota(jnp.int32, shape, 0)


def widen(x, width):
    return jnp.concatenate([x, jnp.zeros((x.shape[0], width - x.shape[1]), x.dtype)], axis=1)


def roll(x, shift, axis):
    shift = shift % x.shape[axis]
    return x if shift == 0 else pltpu.roll(x, shift, axis)


def strided(ref, i, step):
    return jnp.concatenate([ref[j, pl.ds(i, 8, step), :] for j in range(3)], axis=1)


def put_strided(ref, i, step, value):
    for j in range(3):
        ref[j, pl.ds(i, 8, step), :] = value[:, 128 * j : 128 * j + 128]


def tiles(ref, here, value):
    for j in range(3):
        ref[j, here, :] = value[:, 128 * j : 128 * j + 128]


def thickness(level):
    return 1.0 + (0.5 / KL) * level


def tracer_kernel(
    mask_hbm, kmt_hbm, forcing_hbm, t_hbm, u_hbm, v_hbm,
    upd_hbm, rhs_ref, lev_ref, msg_e, msg_w, row_n, row_s,
    t_s, u_s, v_s, o_s, kmt, forcing, mask, min_e, min_n, col, sem_in, sem_out, sem_2d,
):
    def load(i, k):
        src, dst = ((t_hbm, t_s), (u_hbm, u_s), (v_hbm, v_s))[i]
        return pltpu.make_async_copy(src.at[k], dst.at[k], sem_in.at[i, k])

    def store(k):
        return pltpu.make_async_copy(o_s.at[k], upd_hbm.at[k], sem_out.at[k])

    load_mask = pltpu.make_async_copy(mask_hbm, mask, sem_2d.at[0])
    load_kmt = pltpu.make_async_copy(kmt_hbm, kmt, sem_2d.at[1])
    load_forcing = pltpu.make_async_copy(forcing_hbm, forcing, sem_2d.at[2])
    load_mask.start()
    load_kmt.start()
    for k in range(KL):
        for i in range(3):
            load(i, k).start()
    load_forcing.start()

    lane = lanes((8, LW))
    row = rows((8, LW))
    load_mask.wait()
    load_kmt.wait()
    for r in range(0, H, 8):
        keep = jnp.zeros((8, LW), jnp.int32)
        for b in range(W // BSX):
            inside = (lane >= b * BSX) & (lane < (b + 1) * BSX)
            upper = jnp.where(row + r < BSY, mask[0, b], mask[1, b])
            keep = jnp.where(inside, upper, keep)
        lev = widen(kmt[r : r + 8, :], LW) * keep
        lev_ref[r : r + 8, :] = lev.astype(F32)
    for r in range(0, H, 8):
        here = slice(r, r + 8)
        lev = lev_ref[here, :]
        if r + 8 < H:
            north = lev_ref[r + 1 : r + 9, :]
        else:
            north = jnp.where(row == 7, 0.0, roll(lev, -1, 0))
        min_e[here, :] = jnp.minimum(lev, roll(lev, -1, 1))
        min_n[here, :] = jnp.minimum(lev, north)
        col[here, :] = jnp.zeros((8, LW), F32)
    row_n[...] = jnp.zeros((32, LW), F32)
    row_s[...] = jnp.zeros((16, LW), F32)

    load(0, 0).wait()
    row360 = rows((8, W))

    def level(k, carry):
        above = jnp.minimum(k + 1, KL - 1)
        below = jnp.maximum(k - 1, 0)

        @pl.when(k < KL - 1)
        def _():
            load(0, above).wait()

        load(1, k).wait()
        load(2, k).wait()
        kf = k.astype(F32)
        thick = thickness(kf)
        f_low = jnp.zeros((8, W), F32)
        t = t_s[k, 0:8, :]
        t_turned = roll(t, -1, 0)
        for r in range(0, H, 8):
            here = slice(r, r + 8)
            if r + 8 < H:
                ahead = t_s[k, r + 8 : r + 16, :]
                ahead_turned = roll(ahead, -1, 0)
                t_n = jnp.where(row360 == 7, ahead_turned, t_turned)
            else:
                ahead = ahead_turned = None
                t_n = t_turned
            t_e = roll(widen(t, LW), -1, 1)[:, :W]
            lev = lev_ref[here, :W]
            f_e = GRAD * (t_e - t) - (ADV * u_s[k, here, :]) * (t + t_e)
            f_n = GRAD * (t_n - t) - (ADV * v_s[k, here, :]) * (t + t_n)
            f_e = jnp.where(min_e[here, :W] > kf, f_e, 0.0)
            f_n = jnp.where(min_n[here, :W] > kf, f_n, 0.0)
            f_w = roll(widen(f_e, LW), 1, 1)[:, :W]
            f_turned = roll(f_n, 1, 0)
            f_s = jnp.where(row360 == 0, f_low, f_turned)
            f_low = f_turned
            wet = lev > kf
            up = jnp.where(lev > kf + 1.0, t_s[above, here, :] - t, 0.0)
            down = jnp.where(wet, t - t_s[below, here, :], 0.0)
            updated = t + ((f_e - f_w) + (f_n - f_s) + VERT * (up - down))
            o_s[k, here, :] = updated
            col[here, :W] += jnp.where(wet, thick * updated, 0.0)
            t, t_turned = ahead, ahead_turned
        store(k).start()
        row_s[pl.ds(k, 1), :] = widen(t_s[k, 0:1, :], LW)
        row_n[pl.ds(k, 1), :] = widen(t_s[k, H - 1 : H, :], LW)
        row_n[pl.ds(16 + k, 1), :] = widen(v_s[k, H - 1 : H, :], LW)
        return carry

    lax.fori_loop(0, KL, level, 0)

    load_forcing.wait()
    lane = lanes((8, 128))
    for r in range(0, H, 8):
        here = slice(r, r + 8)
        lev = lev_ref[here, :]
        rhs = ROOT * col[here, :W] + forcing[here, :]
        rhs = widen(jnp.where(lev[:, :W] > 0.0, rhs, 0.0), LW)
        rhs_ref[here, :] = rhs
        east = jnp.where(lane < LEV0, roll(rhs[:, 256:], 32, 1), roll(lev[:, 256:], LEV0 - 95, 1))
        west = jnp.where(lane < LEV0, rhs[:, :128], roll(lev[:, :128], LEV0, 1))
        east = jnp.where(lane < TR0, east, 0.0)
        west = jnp.where(lane < TR0, west, 0.0)
        for k in range(KL):
            t2 = roll(widen(t_s[k, here, 256:W], 128), TR0 + k - 103, 1)
            u2 = roll(widen(u_s[k, here, 256:W], 128), VE0 + k - 103, 1)
            t0 = roll(t_s[k, here, :128], TR0 + k, 1)
            east = jnp.where(lane == TR0 + k, t2, east)
            east = jnp.where(lane == VE0 + k, u2, east)
            west = jnp.where(lane == TR0 + k, t0, west)
        if r < 16:
            for at, src, base in ((C_T0, row_s, 0), (C_T1, row_n, 0), (C_V1, row_n, 16)):
                inside = (lane >= at) & (lane < at + 8)
                piece = src[base + r : base + r + 8, :]
                east = jnp.where(inside, roll(piece[:, 256:], at - 96, 1), east)
                west = jnp.where(inside, roll(piece[:, :128], at, 1), west)
        msg_e[here, :] = east
        msg_w[here, :] = west

    def drain(k, carry):
        store(k).wait()
        return carry

    lax.fori_loop(0, KL, drain, 0)


def tracer_part(mask, kmt, forcing, tracer, east, north):
    vmem = pl.BlockSpec(memory_space=pltpu.VMEM)
    hbm = pl.BlockSpec(memory_space=pltpu.HBM)
    shape = jax.ShapeDtypeStruct
    return pl.pallas_call(
        tracer_kernel,
        out_shape=[
            shape((KL, H, W), F32),
            shape((H, LW), F32),
            shape((H, LW), F32),
            shape((H, 128), F32),
            shape((H, 128), F32),
            shape((32, LW), F32),
            shape((16, LW), F32),
        ],
        in_specs=[hbm] * 6,
        out_specs=[hbm] + [vmem] * 6,
        scratch_shapes=[pltpu.VMEM((KL, H, W), F32)] * 4
        + [pltpu.VMEM((H, W), jnp.int32), pltpu.VMEM((H, W), F32), pltpu.SMEM(mask.shape, jnp.int32)]
        + [pltpu.VMEM((H, LW), F32)] * 3
        + [
            pltpu.SemaphoreType.DMA((3, KL)),
            pltpu.SemaphoreType.DMA((KL,)),
            pltpu.SemaphoreType.DMA((3,)),
        ],
        compiler_params=pltpu.CompilerParams(vmem_limit_bytes=VMEM_LIMIT),
        name="tracer",
    )(*(pltpu.with_memory_space_constraint(x, pltpu.HBM) for x in (mask, kmt, forcing, tracer, east, north)))


def sides_kernel(
    from_w, from_e, own_e, own_w, rhs_ref, lev_ref, row_n, row_s,
    rhs_x, lev_x, msg_n, msg_s, flux_e, flux_w,
):
    lane = lanes((8, 128))
    kf = (lane - TR0).astype(F32)
    inside = (lane >= TR0) & (lane < TR0 + KL)
    weight = ROOT * thickness(kf)
    for r in range(0, H, 8):
        here = slice(r, r + 8)
        mw, me = from_w[here, :], from_e[here, :]
        mine_e, mine_w = own_e[here, :], own_w[here, :]
        lev0 = jnp.minimum(mw[:, LEV0 + 8 : LEV0 + 9], mine_w[:, LEV0 : LEV0 + 1])
        lev1 = jnp.minimum(me[:, LEV0 : LEV0 + 1], mine_e[:, LEV0 + 8 : LEV0 + 9])
        f_w = GRAD * (mine_w - mw) - (ADV * roll(mw, TR0 - VE0, 1)) * (mine_w + mw)
        f_e = GRAD * (me - mine_e) - (ADV * roll(mine_e, TR0 - VE0, 1)) * (me + mine_e)
        f_w = jnp.where(inside & (lev0 > kf), f_w, 0.0)
        f_e = jnp.where(inside & (lev1 > kf), f_e, 0.0)
        flux_w[here, :] = f_w
        flux_e[here, :] = f_e
        c_w = jnp.sum(weight * f_w, axis=1, keepdims=True)
        c_e = jnp.sum(weight * f_e, axis=1, keepdims=True)
        rhs_x[here, :128] = rhs_ref[here, :128] - jnp.where(lane == 0, c_w, 0.0)
        rhs_x[here, 128:256] = rhs_ref[here, 128:256]
        last = rhs_ref[here, 256:]
        last = jnp.where((lane >= 104) & (lane < 112), roll(me, 104, 1), last)
        last = jnp.where(lane >= 120, roll(mw, 120, 1), last)
        last = last + jnp.where(lane == 103, c_e, 0.0) - jnp.where(lane == 104, c_e, 0.0)
        rhs_x[here, 256:] = last + jnp.where(lane == 127, c_w, 0.0)
        lev_x[here, :256] = lev_ref[here, :256]
        last = lev_ref[here, 256:]
        last = jnp.where((lane >= 104) & (lane < 113), roll(me, 104 - LEV0, 1), last)
        last = jnp.where(lane >= 119, roll(mw, 119 - LEV0, 1), last)
        lev_x[here, 256:] = last
    msg_n[0:8, :] = rhs_x[H - 8 : H, :]
    msg_s[0:8, :] = rhs_x[0:8, :]
    msg_n[R_LEV : R_LEV + 16, :] = lev_x[H - 16 : H, :]
    msg_s[R_LEV : R_LEV + 16, :] = lev_x[0:16, :]
    for dst, at, src, base, lane0 in (
        (msg_s, R_TR, row_s, 0, C_T0), (msg_n, R_TR, row_n, 0, C_T1), (msg_n, R_VE, row_n, 16, C_V1),
    ):
        for r in (0, 8):
            mw, me = from_w[r : r + 8, :], from_e[r : r + 8, :]
            piece = src[base + r : base + r + 8, :]
            last = piece[:, 256:]
            last = jnp.where((lane >= 104) & (lane < 112), roll(me, 104 - lane0, 1), last)
            last = jnp.where(lane >= 120, roll(mw, 120 - lane0, 1), last)
            dst[at + r : at + r + 8, :256] = piece[:, :256]
            dst[at + r : at + r + 8, 256:] = last


def sides_part(from_w, from_e, own_e, own_w, rhs, lev, row_n, row_s):
    vmem = pl.BlockSpec(memory_space=pltpu.VMEM)
    shape = jax.ShapeDtypeStruct
    return pl.pallas_call(
        sides_kernel,
        out_shape=[
            shape((H, LW), F32),
            shape((H, LW), F32),
            shape((56, LW), F32),
            shape((40, LW), F32),
            shape((H, 128), F32),
            shape((H, 128), F32),
        ],
        in_specs=[vmem] * 8,
        out_specs=[vmem] * 6,
        compiler_params=pltpu.CompilerParams(vmem_limit_bytes=VMEM_LIMIT),
        name="sides",
    )(from_w, from_e, own_e, own_w, rhs, lev, row_n, row_s)


def basis_kernel(
    from_s, from_n, own_n, own_s, rhs_ref, lev_ref, partial,
    basis, diag, sums, updated,
    lev_x, rhs_x, w_e, w_w, w_n, w_s, weight, parts, slab_n, slab_s, sem,
):
    high, low = pl.ds(H - 8, 8), pl.ds(0, 8)
    loads = (
        pltpu.make_async_copy(partial.at[:, high, :], slab_n, sem.at[0]),
        pltpu.make_async_copy(partial.at[:, low, :], slab_s, sem.at[1]),
    )
    stores = (
        pltpu.make_async_copy(slab_n, updated.at[:, high, :], sem.at[2]),
        pltpu.make_async_copy(slab_s, updated.at[:, low, :], sem.at[3]),
    )
    for load in loads:
        load.start()
    lev_row = rows((16, LW))
    kf = lev_row.astype(F32)
    factor = ROOT * thickness(kf)

    def flux(t_from, t_to, vel, lev):
        value = GRAD * (t_to - t_from) - (ADV * vel) * (t_from + t_to)
        return jnp.where((lev_row < KL) & (lev > kf), value, 0.0)

    tr = slice(R_TR, R_TR + 16)
    ve = slice(R_VE, R_VE + 16)
    lev_n = jnp.minimum(lev_ref[H - 1 : H, :], from_n[R_LEV : R_LEV + 1, :])
    lev_s = jnp.minimum(lev_ref[0:1, :], from_s[R_LEV + 15 : R_LEV + 16, :])
    f_n = flux(own_n[tr, :], from_n[tr, :], own_n[ve, :], lev_n)
    f_s = flux(from_s[tr, :], own_s[tr, :], from_s[ve, :], lev_s)
    c_n = jnp.sum(factor * f_n, axis=0, keepdims=True)
    c_s = jnp.sum(factor * f_s, axis=0, keepdims=True)

    row = rows((8, LW))
    ninth = jnp.where(row == 7, from_s[R_LEV : R_LEV + 8, :], 0.0)
    ninth = jnp.where(row == 0, from_n[R_LEV + 8 : R_LEV + 16, :], ninth)
    tiles(lev_x, slice(0, H), lev_ref[...])
    tiles(lev_x, slice(H, H + 8), from_n[R_LEV : R_LEV + 8, :])
    tiles(lev_x, slice(H + 8, H + 16), ninth)
    tiles(lev_x, slice(H + 16, EH), from_s[R_LEV + 8 : R_LEV + 16, :])
    tiles(rhs_x, slice(0, 8), rhs_ref[0:8, :] - jnp.where(row == 0, c_s, 0.0))
    tiles(rhs_x, slice(8, H - 8), rhs_ref[8 : H - 8, :])
    tiles(rhs_x, slice(H - 8, H), rhs_ref[H - 8 : H, :] + jnp.where(row == 7, c_n, 0.0))
    tiles(rhs_x, slice(H, H + 8), from_n[0:8, :] - jnp.where(row == 0, c_n, 0.0))
    tiles(rhs_x, slice(H + 8, H + 16), jnp.zeros((8, LW), F32))
    tiles(rhs_x, slice(H + 16, EH), from_s[0:8, :] + jnp.where(row == 7, c_s, 0.0))

    def depth_of(i):
        lev = strided(lev_x, i, EB)
        return lev + lev * (lev - 1.0) * (0.25 / KL)

    def face(d, other):
        return jnp.where((d > 0.0) & (other > 0.0), 0.5 * (d + other), 0.0)

    lane = lanes((8, LW))
    first = depth_of(0)
    last = depth_of(EB - 1)
    beyond = roll(first, -1, 0)
    n_last = face(last, beyond)
    s = roll(n_last, 1, 0)
    lone = jnp.zeros((8, LW), F32)
    d = first
    for i in range(EB):
        if i < EB - 1:
            d_n = last if i == EB - 2 else depth_of(i + 1)
            n = face(d, d_n)
        else:
            d_n, n = beyond, n_last
        e = face(d, roll(d, -1, 1))
        w = roll(e, 1, 1)
        faces = (e + w) + (n + s)
        dg = jnp.where(d > 0.0, SHIFT * d + faces, 1.0)
        inv = 1.0 / dg
        z = strided(rhs_x, i, EB) * inv
        basis[0, i] = z
        inv = 2.0 * inv
        w_e[i] = e * inv
        w_w[i] = w * inv
        w_n[i] = n * inv
        w_s[i] = s * inv
        diag[i] = dg
        own = (lane < W) & (row * EB + i < H)
        own = jnp.where(own, dg, 0.0)
        joined = faces > 0.0
        weight[i] = jnp.where(joined, own, 0.0)
        lone = lone + jnp.where(joined, 0.0, own * z * z)
        d, s = d_n, n

    def fold(x):
        return jnp.sum(x[:, :128] + x[:, 128:256] + x[:, 256:], axis=0, keepdims=True)

    parts[...] = jnp.zeros((24, 128), F32)
    parts[16:17, :] = fold(lone)

    def step(k, older):
        now = basis.at[k - 1]
        even = jnp.zeros((8, LW), F32)
        odd = jnp.zeros((8, LW), F32)
        first = now[0]
        last = now[EB - 1]
        beyond = roll(first, -1, 0)
        c_s = roll(last, 1, 0)
        c = first
        for i in range(EB):
            if i < EB - 1:
                c_n = last if i == EB - 2 else now[i + 1]
            else:
                c_n = beyond
            image = w_e[i] * roll(c, -1, 1) + w_w[i] * roll(c, 1, 1)
            image = image + (w_n[i] * c_n + w_s[i] * c_s)
            value = 0.5 * image if older is None else image - basis[older, i]
            basis[k, i] = value
            scaled = weight[i] * c
            even = even + scaled * c
            odd = odd + scaled * value
            c_s, c = c, c_n
        parts[pl.ds(2 * k - 2, 1), :] = fold(even)
        parts[pl.ds(2 * k - 1, 1), :] = fold(odd)

    def later_step(k, carry):
        step(k, k - 2)
        return carry

    step(1, None)
    row360 = rows((8, W))
    for load in loads:
        load.wait()
    for k in range(KL):
        at_n = jnp.where(row360 == 7, f_n[k : k + 1, :W], 0.0)
        at_s = jnp.where(row360 == 0, f_s[k : k + 1, :W], 0.0)
        slab_n[k] = slab_n[k] + at_n
        slab_s[k] = slab_s[k] - at_s
    for store in stores:
        store.start()
    lax.fori_loop(2, ITERS + 1, later_step, 0)

    total = jnp.sum(parts[...], axis=1, keepdims=True)
    prow = rows((24, 128))
    plane = lanes((24, 128))
    place = (prow < 16) & ((plane == prow) | (plane == 128 - prow)) | (prow == 16) & (plane == 64)
    line = jnp.sum(jnp.where(place, total, 0.0), axis=0, keepdims=True)
    sums[...] = jnp.broadcast_to(line, sums.shape)
    for store in stores:
        store.wait()


def basis_part(from_s, from_n, own_n, own_s, rhs, lev, partial, count):
    vmem = pl.BlockSpec(memory_space=pltpu.VMEM)
    hbm = pl.BlockSpec(memory_space=pltpu.HBM)
    shape = jax.ShapeDtypeStruct
    return pl.pallas_call(
        basis_kernel,
        out_shape=[
            shape((ITERS + 1, EB, 8, LW), F32),
            shape((EB, 8, LW), F32),
            shape((count, 128), F32),
            shape((KL, H, W), F32),
        ],
        in_specs=[vmem] * 6 + [hbm],
        out_specs=[vmem] * 3 + [hbm],
        input_output_aliases={6: 3},
        scratch_shapes=[pltpu.VMEM((3, EH, 128), F32)] * 2
        + [pltpu.VMEM((EB, 8, LW), F32)] * 5
        + [pltpu.VMEM((24, 128), F32)]
        + [pltpu.VMEM((KL, 8, W), F32)] * 2
        + [pltpu.SemaphoreType.DMA((4,))],
        compiler_params=pltpu.CompilerParams(vmem_limit_bytes=VMEM_LIMIT),
        name="basis",
    )(from_s, from_n, own_n, own_s, rhs, lev, partial)


def polynomials(gathered):
    sums = jnp.sum(gathered, axis=0, keepdims=True)
    lane = lanes((1, 128))
    alone = sums[:, 64:65]
    distance = jnp.minimum(lane, 128 - lane)
    odd = lax.rem(lane, 2) == 1
    base = jnp.where(odd, sums[:, 1:2], sums[:, 0:1])
    moments = jnp.where(distance < 2, sums, jnp.where(distance < 16, 2.0 * sums - base, 0.0))
    row = rows((8, 128))
    lane = lanes((8, 128))
    quarter = lax.rem(lane, 4)
    origin = jnp.where(quarter == 0, alone, jnp.where(quarter == 2, -alone, 0.0))
    now = jnp.where(row == 0, moments, 0.0)
    now = jnp.where((row == 1) & (lane == 0), 2.0, now)
    now = jnp.where(row == 3, 1.0, now)
    now = jnp.where(row == 4, origin, now)
    before = jnp.zeros((8, 128), F32)
    corner = (row == 2) & (lane == 0)
    last_inv = last_ratio = None
    for k in range(ITERS):
        both = now[0:1, :] + now[4:5, :]
        size = both[:, k : k + 1]
        inv = 1.0 / size
        ratio = both[:, k + 1 : k + 2] * inv * (1.0 if k == 0 else 0.5)
        image = 0.5 * (roll(now, 1, 1) + roll(now, -1, 1))
        image = image + jnp.where(corner, 2.0 * now[3:4, 0:1], 0.0)
        if k == 0:
            after = image - ratio * now
        else:
            shrink = size * last_inv * (1.0 if k == 1 else 0.5)
            after = image - (ratio - last_ratio) * now - shrink * before
        last_inv = inv
        last_ratio = ratio
        before, now = now, after
    scale = 1.0 / now[3:4, 0:1]
    half = jnp.where(lanes((1, 128)) == 0, 0.5, 1.0)
    return now[2:3, :] * half * scale, now[1:2, :] * half * scale


def finish_kernel(gathered, basis, diag, sea, residual, sea_t, residual_t):
    lift, rest = polynomials(gathered[...])
    lift = [lift[:, j : j + 1] for j in range(ITERS)]
    rest = [rest[:, j : j + 1] for j in range(ITERS + 1)]
    for i in range(EB):
        c = basis[0, i]
        a, b = lift[0] * c, rest[0] * c
        for j in range(1, ITERS + 1):
            c = basis[j, i]
            b = b + rest[j] * c
            if j < ITERS:
                a = a + lift[j] * c
        b = diag[i] * b
        put_strided(sea_t, i, EB, a)
        put_strided(residual_t, i, EB, b)
    for out, by_tile in ((sea, sea_t), (residual, residual_t)):
        out[:, 0:128] = by_tile[0, :H, :]
        out[:, 128:256] = by_tile[1, :H, :]
        out[:, 256:W] = by_tile[2, :H, : W - 256]


def finish_part(gathered, basis, diag):
    vmem = pl.BlockSpec(memory_space=pltpu.VMEM)
    shape = jax.ShapeDtypeStruct
    return pl.pallas_call(
        finish_kernel,
        out_shape=[shape((H, W), F32), shape((H, W), F32)],
        in_specs=[vmem] * 3,
        out_specs=[vmem] * 2,
        scratch_shapes=[pltpu.VMEM((3, EH, 128), F32)] * 2,
        compiler_params=pltpu.CompilerParams(vmem_limit_bytes=VMEM_LIMIT),
        name="finish",
    )(gathered, basis, diag)


def edges_kernel(flux_e, flux_w, src, dst, level, sem_in, sem_out):
    def load(k):
        return pltpu.make_async_copy(src.at[k], level.at[k], sem_in.at[k])

    def store(k):
        return pltpu.make_async_copy(level.at[k], dst.at[k], sem_out.at[k])

    for k in range(KL):
        load(k).start()
    lane = lanes((8, 128))
    lane_e = lanes((8, W - 256))
    for k in range(KL):
        load(k).wait()
        for r in range(0, H, 8):
            here = slice(r, r + 8)
            at_w = jnp.where(lane == 0, roll(flux_w[here, :], -TR0 - k, 1), 0.0)
            at_e = roll(flux_e[here, :], W - 257 - TR0 - k, 1)[:, : W - 256]
            at_e = jnp.where(lane_e == W - 257, at_e, 0.0)
            level[k, here, :128] = level[k, here, :128] - at_w
            level[k, here, 256:W] = level[k, here, 256:W] + at_e
        store(k).start()
    for k in range(KL):
        store(k).wait()


def edges_part(partial, flux_e, flux_w):
    vmem = pl.BlockSpec(memory_space=pltpu.VMEM)
    hbm = pl.BlockSpec(memory_space=pltpu.HBM)
    return pl.pallas_call(
        edges_kernel,
        out_shape=jax.ShapeDtypeStruct((KL, H, W), F32),
        in_specs=[vmem, vmem, hbm],
        out_specs=hbm,
        input_output_aliases={2: 0},
        scratch_shapes=[
            pltpu.VMEM((KL, H, W), F32),
            pltpu.SemaphoreType.DMA((KL,)),
            pltpu.SemaphoreType.DMA((KL,)),
        ],
        compiler_params=pltpu.CompilerParams(vmem_limit_bytes=VMEM_LIMIT),
        name="edges",
    )(flux_e, flux_w, partial)


def shards(tracer, east_velocity, north_velocity, kmt, block_mask, surface_forcing):
    nx, ny = lax.axis_size("gx"), lax.axis_size("gy")
    partial, rhs, lev, msg_e, msg_w, row_n, row_s = tracer_part(
        block_mask, kmt, surface_forcing, tracer, east_velocity, north_velocity
    )
    from_w = lax.ppermute(msg_e, "gx", [(i, (i + 1) % nx) for i in range(nx)])
    from_e = lax.ppermute(msg_w, "gx", [((i + 1) % nx, i) for i in range(nx)])
    rhs_x, lev_x, msg_n, msg_s, flux_e, flux_w = sides_part(
        from_w, from_e, msg_e, msg_w, rhs, lev, row_n, row_s
    )
    from_s = lax.ppermute(msg_n, "gy", [(i, i + 1) for i in range(ny - 1)])
    from_n = lax.ppermute(msg_s, "gy", [(i + 1, i) for i in range(ny - 1)])
    partial = edges_part(partial, flux_e, flux_w)
    basis, diag, sums, updated = basis_part(
        from_s, from_n, msg_n, msg_s, rhs_x, lev_x, partial, nx * ny
    )
    gathered = lax.all_to_all(sums, ("gx", "gy"), 0, 0, tiled=True)
    sea_level, residual = finish_part(gathered, basis, diag)
    return (updated, sea_level, residual)


def solution(mesh):
    in_specs = (
        P(None, "gy", "gx"),
        P(None, "gy", "gx"),
        P(None, "gy", "gx"),
        P("gy", "gx"),
        P("gy", "gx"),
        P("gy", "gx"),
    )
    out_specs = (P(None, "gy", "gx"), P("gy", "gx"), P("gy", "gx"))
    return jax.shard_map(shards, mesh=mesh, in_specs=in_specs, out_specs=out_specs, check_vma=False)
```

```python
import math

import jax
import jax.numpy as jnp
from jax import lax
from jax.experimental import pallas as pl
from jax.experimental.pallas import tpu as pltpu
from jax.sharding import PartitionSpec as P

BSX = 90
BSY = 60
KL = 12
ITERS = 8

DT_STEP = 0.2
KAPPA_H = 0.2
KAPPA_V = 0.3
SHIFT = 0.002

H = 120
W = 360
LW = 384
EH = 144

EB = EH // 8

GRAD = DT_STEP * KAPPA_H
ADV = DT_STEP * 0.5
VERT = DT_STEP * KAPPA_V
ROOT = 1.0 / math.sqrt(KL)

LEV0 = 8
TR0 = 17
VE0 = 29
C_T0 = 48
C_T1 = 56
C_V1 = 64

R_LEV = 8
R_TR = 24
R_VE = 40

F32 = jnp.float32
VMEM_LIMIT = 40 * 1024 * 1024


def lanes(shape):
    return lax.broadcasted_iota(jnp.int32, shape, 1)


def rows(shape):
    return lax.broadcasted_iota(jnp.int32, shape, 0)


def widen(x, width):
    return jnp.concatenate([x, jnp.zeros((x.shape[0], width - x.shape[1]), x.dtype)], axis=1)


def roll(x, shift, axis):
    shift = shift % x.shape[axis]
    return x if shift == 0 else pltpu.roll(x, shift, axis)


def strided(ref, i, step):
    return jnp.concatenate([ref[j, pl.ds(i, 8, step), :] for j in range(3)], axis=1)


def put_strided(ref, i, step, value):
    for j in range(3):
        ref[j, pl.ds(i, 8, step), :] = value[:, 128 * j : 128 * j + 128]


def tiles(ref, here, value):
    for j in range(3):
        ref[j, here, :] = value[:, 128 * j : 128 * j + 128]


def thickness(level):
    return 1.0 + (0.5 / KL) * level


def tracer_kernel(
    mask_hbm, kmt_hbm, forcing_hbm, t_hbm, u_hbm, v_hbm,
    o_s, rhs_ref, lev_ref, msg_e, msg_w, row_n, row_s,
    t_s, u_s, v_s, kmt, forcing, mask, min_e, min_n, col, drop, sem_in, sem_2d,
):
    def load(i, k):
        src, dst = ((t_hbm, t_s), (u_hbm, u_s), (v_hbm, v_s))[i]
        return pltpu.make_async_copy(src.at[k], dst.at[k], sem_in.at[i, k])

    load_mask = pltpu.make_async_copy(mask_hbm, mask, sem_2d.at[0])
    load_kmt = pltpu.make_async_copy(kmt_hbm, kmt, sem_2d.at[1])
    load_forcing = pltpu.make_async_copy(forcing_hbm, forcing, sem_2d.at[2])
    load_mask.start()
    load_kmt.start()
    for k in range(KL):
        for i in range(3):
            load(i, k).start(priority=0 if k < 4 else 1)
    load_forcing.start(priority=1)

    lane = lanes((8, LW))
    row = rows((8, LW))
    load_mask.wait()
    load_kmt.wait()
    for r in range(0, H, 8):
        keep = jnp.zeros((8, LW), jnp.int32)
        for b in range(W // BSX):
            inside = (lane >= b * BSX) & (lane < (b + 1) * BSX)
            upper = jnp.where(row + r < BSY, mask[0, b], mask[1, b])
            keep = jnp.where(inside, upper, keep)
        lev = widen(kmt[r : r + 8, :], LW) * keep
        lev_ref[r : r + 8, :] = lev.astype(F32)
    for r in range(0, H, 8):
        here = slice(r, r + 8)
        lev = lev_ref[here, :]
        if r + 8 < H:
            north = lev_ref[r + 1 : r + 9, :]
        else:
            north = jnp.where(row == 7, 0.0, roll(lev, -1, 0))
        min_e[here, :] = jnp.minimum(lev, roll(lev, -1, 1))
        min_n[here, :] = jnp.minimum(lev, north)
    row_n[...] = jnp.zeros((32, LW), F32)
    row_s[...] = jnp.zeros((16, LW), F32)

    load(0, 0).wait()
    row360 = rows((8, W))

    for k in range(KL):
        if k + 1 < KL:
            load(0, k + 1).wait()
        load(1, k).wait()
        load(2, k).wait()
        kf = float(k)
        f_low = jnp.zeros((8, W), F32)
        t = t_s[k, 0:8, :]
        t_turned = roll(t, -1, 0)
        for r in range(0, H, 8):
            here = slice(r, r + 8)
            if r + 8 < H:
                ahead = t_s[k, r + 8 : r + 16, :]
                ahead_turned = roll(ahead, -1, 0)
                t_n = jnp.where(row360 == 7, ahead_turned, t_turned)
            else:
                ahead = ahead_turned = None
                t_n = t_turned
            t_e = roll(widen(t, LW), -1, 1)[:, :W]
            f_e = (t_e - t) - (ADV / GRAD * u_s[k, here, :]) * (t + t_e)
            f_n = (t_n - t) - (ADV / GRAD * v_s[k, here, :]) * (t + t_n)
            f_e = jnp.where(min_e[here, :W] > kf, f_e, 0.0)
            f_n = jnp.where(min_n[here, :W] > kf, f_n, 0.0)
            f_w = roll(widen(f_e, LW), 1, 1)[:, :W]
            f_turned = roll(f_n, 1, 0)
            f_s = jnp.where(row360 == 0, f_low, f_turned)
            f_low = f_turned
            lev = lev_ref[here, :W]
            gain = (f_e - f_w) + (f_n - f_s)
            if k + 1 < KL:
                step = VERT / GRAD * (t_s[k + 1, here, :] - t)
                step = jnp.where(lev > kf + 1.0, step, 0.0)
                gain = gain + step
            if k > 0:
                gain = gain - drop[here, :W]
            if k + 1 < KL:
                drop[here, :W] = step
            updated = t + GRAD * gain
            o_s[k, here, :] = updated
            share = jnp.where(lev > kf, thickness(kf) * updated, 0.0)
            col[here, :W] = share if k == 0 else col[here, :W] + share
            t, t_turned = ahead, ahead_turned
        row_s[k : k + 1, :] = widen(t_s[k, 0:1, :], LW)
        row_n[k : k + 1, :] = widen(t_s[k, H - 1 : H, :], LW)
        row_n[16 + k : 17 + k, :] = widen(v_s[k, H - 1 : H, :], LW)

    load_forcing.wait()
    lane = lanes((8, 128))
    for r in range(0, H, 8):
        here = slice(r, r + 8)
        lev = lev_ref[here, :]
        rhs = ROOT * col[here, :W] + forcing[here, :]
        rhs = widen(jnp.where(lev[:, :W] > 0.0, rhs, 0.0), LW)
        rhs_ref[here, :] = rhs
        east = jnp.where(lane < LEV0, roll(rhs[:, 256:], 32, 1), roll(lev[:, 256:], LEV0 - 95, 1))
        west = jnp.where(lane < LEV0, rhs[:, :128], roll(lev[:, :128], LEV0, 1))
        east = jnp.where(lane < TR0, east, 0.0)
        west = jnp.where(lane < TR0, west, 0.0)
        for k in range(KL):
            t2 = roll(widen(t_s[k, here, 256:W], 128), TR0 + k - 103, 1)
            u2 = roll(widen(u_s[k, here, 256:W], 128), VE0 + k - 103, 1)
            t0 = roll(t_s[k, here, :128], TR0 + k, 1)
            east = jnp.where(lane == TR0 + k, t2, east)
            east = jnp.where(lane == VE0 + k, u2, east)
            west = jnp.where(lane == TR0 + k, t0, west)
        if r < 16:
            for at, src, base in ((C_T0, row_s, 0), (C_T1, row_n, 0), (C_V1, row_n, 16)):
                inside = (lane >= at) & (lane < at + 8)
                piece = src[base + r : base + r + 8, :]
                east = jnp.where(inside, roll(piece[:, 256:], at - 96, 1), east)
                west = jnp.where(inside, roll(piece[:, :128], at, 1), west)
        msg_e[here, :] = east
        msg_w[here, :] = west


def tracer_part(mask, kmt, forcing, tracer, east, north):
    vmem = pl.BlockSpec(memory_space=pltpu.VMEM)
    hbm = pl.BlockSpec(memory_space=pltpu.HBM)
    shape = jax.ShapeDtypeStruct
    return pl.pallas_call(
        tracer_kernel,
        out_shape=[
            shape((KL, H, W), F32),
            shape((H, LW), F32),
            shape((H, LW), F32),
            shape((H, 128), F32),
            shape((H, 128), F32),
            shape((32, LW), F32),
            shape((16, LW), F32),
        ],
        in_specs=[hbm] * 6,
        out_specs=[vmem] * 7,
        scratch_shapes=[pltpu.VMEM((KL, H, W), F32)] * 3
        + [pltpu.VMEM((H, W), jnp.int32), pltpu.VMEM((H, W), F32), pltpu.SMEM(mask.shape, jnp.int32)]
        + [pltpu.VMEM((H, LW), F32)] * 4
        + [
            pltpu.SemaphoreType.DMA((3, KL)),
            pltpu.SemaphoreType.DMA((3,)),
        ],
        compiler_params=pltpu.CompilerParams(vmem_limit_bytes=VMEM_LIMIT),
        name="tracer",
    )(*(pltpu.with_memory_space_constraint(x, pltpu.HBM) for x in (mask, kmt, forcing, tracer, east, north)))


def sides_kernel(
    from_w, from_e, own_e, own_w, rhs_ref, lev_ref, row_n, row_s,
    rhs_x, lev_x, msg_n, msg_s, flux_e, flux_w,
    sum_e, sum_w,
):
    from_lane = rows((128, 128))

    def spread(x, first, count, precision):
        chosen = (from_lane >= first) & (from_lane < first + count)
        return jnp.dot(
            x, jnp.where(chosen, 1.0, 0.0), precision=precision, preferred_element_type=F32
        )

    def level_at(ref, at):
        return spread(ref[...], at, 1, lax.Precision.DEFAULT)

    lane = lanes((H, 128))
    kf = (lane - TR0).astype(F32)
    inside = (lane >= TR0) & (lane < TR0 + KL)
    weight = ROOT * thickness(kf)
    lev_w = jnp.minimum(level_at(from_w, LEV0 + 8), level_at(own_w, LEV0))
    lev_e = jnp.minimum(level_at(from_e, LEV0), level_at(own_e, LEV0 + 8))
    mw, me, mine_w, mine_e = from_w[...], from_e[...], own_w[...], own_e[...]
    f_w = GRAD * (mine_w - mw) - (ADV * roll(mw, TR0 - VE0, 1)) * (mine_w + mw)
    f_e = GRAD * (me - mine_e) - (ADV * roll(mine_e, TR0 - VE0, 1)) * (me + mine_e)
    f_w = jnp.where(inside & (lev_w > kf), f_w, 0.0)
    f_e = jnp.where(inside & (lev_e > kf), f_e, 0.0)
    flux_w[...] = f_w
    flux_e[...] = f_e
    sum_w[...] = spread(weight * f_w, TR0, KL, lax.Precision.HIGHEST)
    sum_e[...] = spread(weight * f_e, TR0, KL, lax.Precision.HIGHEST)
    lane = lanes((8, 128))
    for r in range(0, H, 8):
        here = slice(r, r + 8)
        mw, me = from_w[here, :], from_e[here, :]
        c_w, c_e = sum_w[here, :], sum_e[here, :]
        rhs_x[here, :128] = rhs_ref[here, :128] - jnp.where(lane == 0, c_w, 0.0)
        rhs_x[here, 128:256] = rhs_ref[here, 128:256]
        last = rhs_ref[here, 256:]
        last = jnp.where((lane >= 104) & (lane < 112), roll(me, 104, 1), last)
        last = jnp.where(lane >= 120, roll(mw, 120, 1), last)
        last = last + jnp.where(lane == 103, c_e, 0.0) - jnp.where(lane == 104, c_e, 0.0)
        rhs_x[here, 256:] = last + jnp.where(lane == 127, c_w, 0.0)
        lev_x[here, :256] = lev_ref[here, :256]
        last = lev_ref[here, 256:]
        last = jnp.where((lane >= 104) & (lane < 113), roll(me, 104 - LEV0, 1), last)
        last = jnp.where(lane >= 119, roll(mw, 119 - LEV0, 1), last)
        lev_x[here, 256:] = last
    msg_n[0:8, :] = rhs_x[H - 8 : H, :]
    msg_s[0:8, :] = rhs_x[0:8, :]
    msg_n[R_LEV : R_LEV + 16, :] = lev_x[H - 16 : H, :]
    msg_s[R_LEV : R_LEV + 16, :] = lev_x[0:16, :]
    for dst, at, src, base, lane0 in (
        (msg_s, R_TR, row_s, 0, C_T0), (msg_n, R_TR, row_n, 0, C_T1), (msg_n, R_VE, row_n, 16, C_V1),
    ):
        for r in (0, 8):
            mw, me = from_w[r : r + 8, :], from_e[r : r + 8, :]
            piece = src[base + r : base + r + 8, :]
            last = piece[:, 256:]
            last = jnp.where((lane >= 104) & (lane < 112), roll(me, 104 - lane0, 1), last)
            last = jnp.where(lane >= 120, roll(mw, 120 - lane0, 1), last)
            dst[at + r : at + r + 8, :256] = piece[:, :256]
            dst[at + r : at + r + 8, 256:] = last


def sides_part(from_w, from_e, own_e, own_w, rhs, lev, row_n, row_s):
    vmem = pl.BlockSpec(memory_space=pltpu.VMEM)
    shape = jax.ShapeDtypeStruct
    return pl.pallas_call(
        sides_kernel,
        out_shape=[
            shape((H, LW), F32),
            shape((H, LW), F32),
            shape((56, LW), F32),
            shape((40, LW), F32),
            shape((H, 128), F32),
            shape((H, 128), F32),
        ],
        in_specs=[vmem] * 8,
        out_specs=[vmem] * 6,
        scratch_shapes=[pltpu.VMEM((H, 128), F32)] * 2,
        compiler_params=pltpu.CompilerParams(vmem_limit_bytes=VMEM_LIMIT),
        name="sides",
    )(from_w, from_e, own_e, own_w, rhs, lev, row_n, row_s)


def basis_kernel(
    from_s, from_n, own_n, own_s, rhs_ref, lev_ref, partial,
    basis, diag, sums, updated,
    lev_x, rhs_x, w_e, w_w, w_n, w_s, weight, parts, slab_n, slab_s, sem,
):
    high, low = pl.ds(H - 8, 8), pl.ds(0, 8)
    loads = (
        pltpu.make_async_copy(partial.at[:, high, :], slab_n, sem.at[0]),
        pltpu.make_async_copy(partial.at[:, low, :], slab_s, sem.at[1]),
    )
    stores = (
        pltpu.make_async_copy(slab_n, updated.at[:, high, :], sem.at[2]),
        pltpu.make_async_copy(slab_s, updated.at[:, low, :], sem.at[3]),
    )
    for load in loads:
        load.start()
    lev_row = rows((16, LW))
    kf = lev_row.astype(F32)
    factor = ROOT * thickness(kf)

    def flux(t_from, t_to, vel, lev):
        value = GRAD * (t_to - t_from) - (ADV * vel) * (t_from + t_to)
        return jnp.where((lev_row < KL) & (lev > kf), value, 0.0)

    tr = slice(R_TR, R_TR + 16)
    ve = slice(R_VE, R_VE + 16)
    lev_n = jnp.minimum(lev_ref[H - 1 : H, :], from_n[R_LEV : R_LEV + 1, :])
    lev_s = jnp.minimum(lev_ref[0:1, :], from_s[R_LEV + 15 : R_LEV + 16, :])
    f_n = flux(own_n[tr, :], from_n[tr, :], own_n[ve, :], lev_n)
    f_s = flux(from_s[tr, :], own_s[tr, :], from_s[ve, :], lev_s)
    c_n = jnp.sum(factor * f_n, axis=0, keepdims=True)
    c_s = jnp.sum(factor * f_s, axis=0, keepdims=True)

    row = rows((8, LW))
    ninth = jnp.where(row == 7, from_s[R_LEV : R_LEV + 8, :], 0.0)
    ninth = jnp.where(row == 0, from_n[R_LEV + 8 : R_LEV + 16, :], ninth)
    tiles(lev_x, slice(0, H), lev_ref[...])
    tiles(lev_x, slice(H, H + 8), from_n[R_LEV : R_LEV + 8, :])
    tiles(lev_x, slice(H + 8, H + 16), ninth)
    tiles(lev_x, slice(H + 16, EH), from_s[R_LEV + 8 : R_LEV + 16, :])
    tiles(rhs_x, slice(0, 8), rhs_ref[0:8, :] - jnp.where(row == 0, c_s, 0.0))
    tiles(rhs_x, slice(8, H - 8), rhs_ref[8 : H - 8, :])
    tiles(rhs_x, slice(H - 8, H), rhs_ref[H - 8 : H, :] + jnp.where(row == 7, c_n, 0.0))
    tiles(rhs_x, slice(H, H + 8), from_n[0:8, :] - jnp.where(row == 0, c_n, 0.0))
    tiles(rhs_x, slice(H + 8, H + 16), jnp.zeros((8, LW), F32))
    tiles(rhs_x, slice(H + 16, EH), from_s[0:8, :] + jnp.where(row == 7, c_s, 0.0))

    def depth_of(i):
        lev = strided(lev_x, i, EB)
        return lev + lev * (lev - 1.0) * (0.25 / KL)

    def face(d, other):
        return jnp.where((d > 0.0) & (other > 0.0), 0.5 * (d + other), 0.0)

    lane = lanes((8, LW))
    first = depth_of(0)
    last = depth_of(EB - 1)
    beyond = roll(first, -1, 0)
    n_last = face(last, beyond)
    s = roll(n_last, 1, 0)
    lone = jnp.zeros((8, LW), F32)
    d = first
    for i in range(EB):
        if i < EB - 1:
            d_n = last if i == EB - 2 else depth_of(i + 1)
            n = face(d, d_n)
        else:
            d_n, n = beyond, n_last
        e = face(d, roll(d, -1, 1))
        w = roll(e, 1, 1)
        faces = (e + w) + (n + s)
        dg = jnp.where(d > 0.0, SHIFT * d + faces, 1.0)
        inv = 1.0 / dg
        z = strided(rhs_x, i, EB) * inv
        basis[0, i] = z
        inv = 2.0 * inv
        w_e[i] = e * inv
        w_w[i] = w * inv
        w_n[i] = n * inv
        w_s[i] = s * inv
        diag[i] = dg
        own = (lane < W) & (row * EB + i < H)
        own = jnp.where(own, dg, 0.0)
        joined = faces > 0.0
        weight[i] = jnp.where(joined, own, 0.0)
        lone = lone + jnp.where(joined, 0.0, own * z * z)
        d, s = d_n, n

    def fold(x):
        return jnp.sum(x[:, :128] + x[:, 128:256] + x[:, 256:], axis=0, keepdims=True)

    parts[...] = jnp.zeros((24, 128), F32)
    parts[16:17, :] = fold(lone)

    def step(k, older):
        now = basis.at[k - 1]
        even = jnp.zeros((8, LW), F32)
        odd = jnp.zeros((8, LW), F32)
        first = now[0]
        last = now[EB - 1]
        beyond = roll(first, -1, 0)
        c_s = roll(last, 1, 0)
        c = first
        for i in range(EB):
            if i < EB - 1:
                c_n = last if i == EB - 2 else now[i + 1]
            else:
                c_n = beyond
            image = w_e[i] * roll(c, -1, 1) + w_w[i] * roll(c, 1, 1)
            image = image + (w_n[i] * c_n + w_s[i] * c_s)
            value = 0.5 * image if older is None else image - basis[older, i]
            basis[k, i] = value
            scaled = weight[i] * c
            even = even + scaled * c
            odd = odd + scaled * value
            c_s, c = c, c_n
        parts[2 * k - 2 : 2 * k - 1, :] = fold(even)
        parts[2 * k - 1 : 2 * k, :] = fold(odd)

    step(1, None)
    row360 = rows((8, W))
    for load in loads:
        load.wait()
    for k in range(KL):
        at_n = jnp.where(row360 == 7, f_n[k : k + 1, :W], 0.0)
        at_s = jnp.where(row360 == 0, f_s[k : k + 1, :W], 0.0)
        slab_n[k] = slab_n[k] + at_n
        slab_s[k] = slab_s[k] - at_s
    for store in stores:
        store.start()
    for k in range(2, ITERS + 1):
        step(k, k - 2)

    total = jnp.sum(parts[...], axis=1, keepdims=True)
    prow = rows((24, 128))
    plane = lanes((24, 128))
    place = (prow < 16) & ((plane == prow) | (plane == 128 - prow)) | (prow == 16) & (plane == 64)
    line = jnp.sum(jnp.where(place, total, 0.0), axis=0, keepdims=True)
    sums[...] = jnp.broadcast_to(line, sums.shape)
    for store in stores:
        store.wait()


def basis_part(from_s, from_n, own_n, own_s, rhs, lev, partial, count):
    vmem = pl.BlockSpec(memory_space=pltpu.VMEM)
    hbm = pl.BlockSpec(memory_space=pltpu.HBM)
    shape = jax.ShapeDtypeStruct
    return pl.pallas_call(
        basis_kernel,
        out_shape=[
            shape((ITERS + 1, EB, 8, LW), F32),
            shape((EB, 8, LW), F32),
            shape((count, 128), F32),
            shape((KL, H, W), F32),
        ],
        in_specs=[vmem] * 6 + [hbm],
        out_specs=[vmem] * 3 + [hbm],
        input_output_aliases={6: 3},
        scratch_shapes=[pltpu.VMEM((3, EH, 128), F32)] * 2
        + [pltpu.VMEM((EB, 8, LW), F32)] * 5
        + [pltpu.VMEM((24, 128), F32)]
        + [pltpu.VMEM((KL, 8, W), F32)] * 2
        + [pltpu.SemaphoreType.DMA((4,))],
        compiler_params=pltpu.CompilerParams(vmem_limit_bytes=VMEM_LIMIT),
        name="basis",
    )(from_s, from_n, own_n, own_s, rhs, lev, partial)


def polynomials(gathered):
    sums = jnp.broadcast_to(jnp.sum(gathered, axis=0, keepdims=True), (8, 128))

    def pick(lane):
        return jnp.broadcast_to(sums[:, lane : lane + 1], (8, 128))

    moments = [pick(j) for j in range(2 * ITERS)]
    alone = pick(64)
    now = [x if j < 2 else 2.0 * x - moments[j % 2] for j, x in enumerate(moments)]
    before = [0.0] * len(now)
    one = jnp.ones((8, 128), F32)
    rest, rest_before = [one], []
    lift, lift_before = [], []
    at0, at0_before = alone, 0.0
    at1, at1_before = one, 0.0

    def coefficient(p, j):
        return p[j] if 0 <= j < len(p) else None

    def total(terms):
        terms = [x for x in terms if x is not None]
        return sum(terms[1:], terms[0]) if terms else jnp.zeros((8, 128), F32)

    def advance(p, p_before, a, b, count, constant=None):
        out = []
        for j in range(count):
            terms = [constant if j == 0 else None]
            below, above = coefficient(p, j - 1), coefficient(p, j + 1)
            if below is not None:
                terms.append(below if j == 1 else 0.5 * below)
            if above is not None:
                terms.append(0.5 * above)
            if coefficient(p, j) is not None:
                terms.append(-(a * p[j]))
            if coefficient(p_before, j) is not None:
                terms.append(-(b * p_before[j]))
            out.append(total(terms))
        return out

    def lone_part(j):
        return (at0, None, -at0, None)[j % 4]

    last_inv = last_ratio = None
    for k in range(ITERS):
        size = total([now[k], lone_part(k)])
        cross = total([now[k + 1], lone_part(k + 1)])
        inv = 1.0 / size
        ratio = cross * inv * (1.0 if k == 0 else 0.5)
        if k == 0:
            a, b = ratio, jnp.zeros((8, 128), F32)
        else:
            a, b = ratio - last_ratio, size * last_inv * (1.0 if k == 1 else 0.5)
        last_inv, last_ratio = inv, ratio
        after = [None] * len(now)
        for j in range(k + 1, 2 * ITERS - 1 - k):
            after[j] = 0.5 * (now[j - 1] + now[j + 1]) - a * now[j] - b * before[j]
        before, now = now, after
        lift, lift_before = advance(lift, lift_before, a, b, k + 1, at1), lift
        rest, rest_before = advance(rest, rest_before, a, b, k + 2), rest
        at0, at0_before = -(a * at0) - b * at0_before, at0
        at1, at1_before = (1.0 - a) * at1 - b * at1_before, at1
    scale = 1.0 / at1
    return [x * scale for x in lift], [x * scale for x in rest]


def finish_kernel(gathered, basis, diag, sea, residual, sea_t, residual_t):
    lift, rest = polynomials(gathered[...])
    for i in range(EB):
        for j in range(3):
            here = slice(128 * j, 128 * j + 128)
            c = basis[0, i, :, here]
            a, b = lift[0] * c, rest[0] * c
            for k in range(1, ITERS + 1):
                c = basis[k, i, :, here]
                b = b + rest[k] * c
                if k < ITERS:
                    a = a + lift[k] * c
            sea_t[j, pl.ds(i, 8, EB), :] = a
            residual_t[j, pl.ds(i, 8, EB), :] = diag[i, :, here] * b
    for out, by_tile in ((sea, sea_t), (residual, residual_t)):
        out[:, 0:128] = by_tile[0, :H, :]
        out[:, 128:256] = by_tile[1, :H, :]
        out[:, 256:W] = by_tile[2, :H, : W - 256]


def finish_part(gathered, basis, diag):
    vmem = pl.BlockSpec(memory_space=pltpu.VMEM)
    shape = jax.ShapeDtypeStruct
    return pl.pallas_call(
        finish_kernel,
        out_shape=[shape((H, W), F32), shape((H, W), F32)],
        in_specs=[vmem] * 3,
        out_specs=[vmem] * 2,
        scratch_shapes=[pltpu.VMEM((3, EH, 128), F32)] * 2,
        compiler_params=pltpu.CompilerParams(vmem_limit_bytes=VMEM_LIMIT),
        name="finish",
    )(gathered, basis, diag)


def edges_kernel(partial, flux_e, flux_w, dst, level, sem):
    def store(k):
        return pltpu.make_async_copy(level.at[k], dst.at[k], sem.at[k])

    lane = lanes((8, 128))
    lane_e = lanes((8, W - 256))
    for k in range(KL):
        for r in range(0, H, 8):
            here = slice(r, r + 8)
            at_w = jnp.where(lane == 0, roll(flux_w[here, :], -TR0 - k, 1), 0.0)
            at_e = roll(flux_e[here, :], W - 257 - TR0 - k, 1)[:, : W - 256]
            at_e = jnp.where(lane_e == W - 257, at_e, 0.0)
            level[k, here, :128] = partial[k, here, :128] - at_w
            level[k, here, 128:256] = partial[k, here, 128:256]
            level[k, here, 256:W] = partial[k, here, 256:W] + at_e
        store(k).start()
    for k in range(KL):
        store(k).wait()


def edges_part(partial, flux_e, flux_w):
    vmem = pl.BlockSpec(memory_space=pltpu.VMEM)
    hbm = pl.BlockSpec(memory_space=pltpu.HBM)
    return pl.pallas_call(
        edges_kernel,
        out_shape=jax.ShapeDtypeStruct((KL, H, W), F32),
        in_specs=[vmem] * 3,
        out_specs=hbm,
        scratch_shapes=[pltpu.VMEM((KL, H, W), F32), pltpu.SemaphoreType.DMA((KL,))],
        compiler_params=pltpu.CompilerParams(vmem_limit_bytes=VMEM_LIMIT),
        name="edges",
    )(partial, flux_e, flux_w)


def shards(tracer, east_velocity, north_velocity, kmt, block_mask, surface_forcing):
    nx, ny = lax.axis_size("gx"), lax.axis_size("gy")
    partial, rhs, lev, msg_e, msg_w, row_n, row_s = tracer_part(
        block_mask, kmt, surface_forcing, tracer, east_velocity, north_velocity
    )
    from_w = lax.ppermute(msg_e, "gx", [(i, (i + 1) % nx) for i in range(nx)])
    from_e = lax.ppermute(msg_w, "gx", [((i + 1) % nx, i) for i in range(nx)])
    rhs_x, lev_x, msg_n, msg_s, flux_e, flux_w = sides_part(
        from_w, from_e, msg_e, msg_w, rhs, lev, row_n, row_s
    )
    from_s = lax.ppermute(msg_n, "gy", [(i, i + 1) for i in range(ny - 1)])
    from_n = lax.ppermute(msg_s, "gy", [(i + 1, i) for i in range(ny - 1)])
    partial = edges_part(partial, flux_e, flux_w)
    basis, diag, sums, updated = basis_part(
        from_s, from_n, msg_n, msg_s, rhs_x, lev_x, partial, nx * ny
    )
    gathered = lax.all_to_all(sums, ("gx", "gy"), 0, 0, tiled=True)
    sea_level, residual = finish_part(gathered, basis, diag)
    return (updated, sea_level, residual)


def solution(mesh):
    in_specs = (
        P(None, "gy", "gx"),
        P(None, "gy", "gx"),
        P(None, "gy", "gx"),
        P("gy", "gx"),
        P("gy", "gx"),
        P("gy", "gx"),
    )
    out_specs = (P(None, "gy", "gx"), P("gy", "gx"), P("gy", "gx"))
    return jax.shard_map(shards, mesh=mesh, in_specs=in_specs, out_specs=out_specs, check_vma=False)
```

```python
import math

import jax
import jax.numpy as jnp
from jax import lax
from jax.experimental import pallas as pl
from jax.experimental.pallas import tpu as pltpu
from jax.sharding import PartitionSpec as P

BSX = 90
BSY = 60
KL = 12
ITERS = 8

DT_STEP = 0.2
KAPPA_H = 0.2
KAPPA_V = 0.3
SHIFT = 0.002

H = 120
W = 360
LW = 384
EH = 144

EB = EH // 8

GRAD = DT_STEP * KAPPA_H
ADV = DT_STEP * 0.5
VERT = DT_STEP * KAPPA_V
ROOT = 1.0 / math.sqrt(KL)

LEV0 = 8
TR0 = 17
VE0 = 29
C_T0 = 48
C_T1 = 56
C_V1 = 64

R_LEV = 8
R_TR = 24
R_VE = 40

F32 = jnp.float32
VMEM_LIMIT = 40 * 1024 * 1024


def lanes(shape):
    return lax.broadcasted_iota(jnp.int32, shape, 1)


def rows(shape):
    return lax.broadcasted_iota(jnp.int32, shape, 0)


def widen(x, width):
    return jnp.concatenate([x, jnp.zeros((x.shape[0], width - x.shape[1]), x.dtype)], axis=1)


def roll(x, shift, axis):
    shift = shift % x.shape[axis]
    return x if shift == 0 else pltpu.roll(x, shift, axis)


def strided(ref, i, step):
    return jnp.concatenate([ref[j, pl.ds(i, 8, step), :] for j in range(3)], axis=1)


def put_strided(ref, i, step, value):
    for j in range(3):
        ref[j, pl.ds(i, 8, step), :] = value[:, 128 * j : 128 * j + 128]


def tiles(ref, here, value):
    for j in range(3):
        ref[j, here, :] = value[:, 128 * j : 128 * j + 128]


def thickness(level):
    return 1.0 + (0.5 / KL) * level


def tile(ref, j, *at):
    if ref.shape[-1] == LW or j < 2:
        return ref[(*at, slice(128 * j, 128 * j + 128))]
    return widen(ref[(*at, slice(256, W))], 128)


def sweep_level(k, j, t_s, u_s, v_s, lev_ref, min_e, min_n, drop, col, put):
    static = isinstance(k, int)
    kf = float(k) if static else k.astype(F32)
    first, last = static and k == 0, static and k == KL - 1
    above = min(k + 1, KL - 1) if static else jnp.minimum(k + 1, KL - 1)
    lane = lanes((8, 128))
    row = rows((8, 128))
    f_low = jnp.zeros((8, 128), F32)
    t = tile(t_s, j, k, slice(0, 8))
    t_turned = roll(t, -1, 0)
    for r in range(0, H, 8):
        here = slice(r, r + 8)
        if r + 8 < H:
            ahead = tile(t_s, j, k, slice(r + 8, r + 16))
            ahead_turned = roll(ahead, -1, 0)
            t_n = jnp.where(row == 7, ahead_turned, t_turned)
        else:
            ahead = ahead_turned = None
            t_n = t_turned
        t_e = roll(t, -1, 1)
        f_e = (t_e - t) - (ADV / GRAD * tile(u_s, j, k, here)) * (t + t_e)
        f_n = (t_n - t) - (ADV / GRAD * tile(v_s, j, k, here)) * (t + t_n)
        f_e = jnp.where(tile(min_e, j, here) > kf, f_e, 0.0)
        f_n = jnp.where(tile(min_n, j, here) > kf, f_n, 0.0)
        f_w = roll(f_e, 1, 1)
        f_turned = roll(f_n, 1, 0)
        f_s = jnp.where(row == 0, f_low, f_turned)
        f_low = f_turned
        lev = tile(lev_ref, j, here)
        gain = (f_e - f_w) + (f_n - f_s)
        if not last:
            step = VERT / GRAD * (tile(t_s, j, above, here) - t)
            step = jnp.where(lev > kf + 1.0, step, 0.0)
            gain = gain + step
        if not first:
            gain = gain - tile(drop, j, here)
        if not last:
            drop[here, 128 * j : 128 * j + 128] = step
        updated = t + GRAD * gain
        put(here, updated)
        share = jnp.where(lev > kf, thickness(kf) * updated, 0.0)
        col[here, 128 * j : 128 * j + 128] = share if first else tile(col, j, here) + share
        t, t_turned = ahead, ahead_turned


def outer_kernel(
    mask_hbm, kmt_hbm, forcing_hbm, t_hbm, u_hbm, v_hbm,
    t_s, u_s, v_s, forcing, outer, rhs_ref, lev_ref, min_e, min_in, min_n, msg_e, msg_w, row_n, row_s,
    kmt, mask, col, drop, sem_in, sem_2d,
):
    def load(i, k):
        src, dst = ((t_hbm, t_s), (u_hbm, u_s), (v_hbm, v_s))[i]
        return pltpu.make_async_copy(src.at[k], dst.at[k], sem_in.at[i, k])

    load_mask = pltpu.make_async_copy(mask_hbm, mask, sem_2d.at[0])
    load_kmt = pltpu.make_async_copy(kmt_hbm, kmt, sem_2d.at[1])
    load_forcing = pltpu.make_async_copy(forcing_hbm, forcing, sem_2d.at[2])
    load_mask.start()
    load_kmt.start()
    for k in range(KL):
        for i in range(3):
            load(i, k).start(priority=0 if k < 4 else 1)
    load_forcing.start(priority=1)

    lane = lanes((8, LW))
    row = rows((8, LW))
    load_mask.wait()
    load_kmt.wait()
    for r in range(0, H, 8):
        keep = jnp.zeros((8, LW), jnp.int32)
        for b in range(W // BSX):
            inside = (lane >= b * BSX) & (lane < (b + 1) * BSX)
            upper = jnp.where(row + r < BSY, mask[0, b], mask[1, b])
            keep = jnp.where(inside, upper, keep)
        lev = widen(kmt[r : r + 8, :], LW) * keep
        lev_ref[r : r + 8, :] = lev.astype(F32)
    inner = (lane != 127) & (lane != 255)
    for r in range(0, H, 8):
        here = slice(r, r + 8)
        lev = lev_ref[here, :]
        if r + 8 < H:
            north = lev_ref[r + 1 : r + 9, :]
        else:
            north = jnp.where(row == 7, 0.0, roll(lev, -1, 0))
        east = jnp.minimum(lev, roll(lev, -1, 1))
        min_e[here, :] = east
        min_in[here, :] = jnp.where(inner, east, 0.0)
        min_n[here, :] = jnp.minimum(lev, north)
    row_n[...] = jnp.zeros((32, LW), F32)
    row_s[...] = jnp.zeros((16, LW), F32)

    load(0, 0).wait()
    for k in range(KL):
        if k + 1 < KL:
            load(0, k + 1).wait()
        load(1, k).wait()
        load(2, k).wait()
        for j in (0, 2):

            def put(here, updated, k=k, j=j):
                outer[k, here, 64 * j : 64 * j + 128] = updated

            sweep_level(k, j, t_s, u_s, v_s, lev_ref, min_in, min_n, drop, col, put)
        row_s[k : k + 1, :] = widen(t_s[k, 0:1, :], LW)
        row_n[k : k + 1, :] = widen(t_s[k, H - 1 : H, :], LW)
        row_n[16 + k : 17 + k, :] = widen(v_s[k, H - 1 : H, :], LW)

    load_forcing.wait()
    lane = lanes((8, 128))
    for r in range(0, H, 8):
        here = slice(r, r + 8)
        lev0, lev2 = tile(lev_ref, 0, here), tile(lev_ref, 2, here)
        rhs0 = jnp.where(lev0 > 0.0, ROOT * tile(col, 0, here) + tile(forcing, 0, here), 0.0)
        rhs2 = jnp.where(lev2 > 0.0, ROOT * tile(col, 2, here) + tile(forcing, 2, here), 0.0)
        rhs_ref[here, :128] = rhs0
        rhs_ref[here, 128:] = rhs2
        east = jnp.where(lane < LEV0, roll(rhs2, 32, 1), roll(lev2, LEV0 - 95, 1))
        west = jnp.where(lane < LEV0, rhs0, roll(lev0, LEV0, 1))
        east = jnp.where(lane < TR0, east, 0.0)
        west = jnp.where(lane < TR0, west, 0.0)
        for k in range(KL):
            t2 = roll(tile(t_s, 2, k, here), TR0 + k - 103, 1)
            u2 = roll(tile(u_s, 2, k, here), VE0 + k - 103, 1)
            t0 = roll(tile(t_s, 0, k, here), TR0 + k, 1)
            east = jnp.where(lane == TR0 + k, t2, east)
            east = jnp.where(lane == VE0 + k, u2, east)
            west = jnp.where(lane == TR0 + k, t0, west)
        if r < 16:
            for at, src, base in ((C_T0, row_s, 0), (C_T1, row_n, 0), (C_V1, row_n, 16)):
                inside = (lane >= at) & (lane < at + 8)
                piece = src[base + r : base + r + 8, :]
                east = jnp.where(inside, roll(piece[:, 256:], at - 96, 1), east)
                west = jnp.where(inside, roll(piece[:, :128], at, 1), west)
        msg_e[here, :] = east
        msg_w[here, :] = west


def outer_part(mask, kmt, forcing, tracer, east, north):
    vmem = pl.BlockSpec(memory_space=pltpu.VMEM)
    hbm = pl.BlockSpec(memory_space=pltpu.HBM)
    shape = jax.ShapeDtypeStruct
    return pl.pallas_call(
        outer_kernel,
        out_shape=[shape((KL, H, W), F32)] * 3
        + [
            shape((H, W), F32),
            shape((KL, H, 256), F32),
            shape((H, 256), F32),
            shape((H, LW), F32),
            shape((H, LW), F32),
            shape((H, LW), F32),
            shape((H, LW), F32),
            shape((H, 128), F32),
            shape((H, 128), F32),
            shape((32, LW), F32),
            shape((16, LW), F32),
        ],
        in_specs=[hbm] * 6,
        out_specs=[vmem] * 14,
        scratch_shapes=[pltpu.VMEM((H, W), jnp.int32), pltpu.SMEM(mask.shape, jnp.int32)]
        + [pltpu.VMEM((H, LW), F32)] * 2
        + [pltpu.SemaphoreType.DMA((3, KL)), pltpu.SemaphoreType.DMA((3,))],
        compiler_params=pltpu.CompilerParams(vmem_limit_bytes=VMEM_LIMIT),
        name="outer",
    )(*(pltpu.with_memory_space_constraint(x, pltpu.HBM) for x in (mask, kmt, forcing, tracer, east, north)))


def middle_kernel(
    t_s, u_s, v_s, forcing, outer, rhs_outer, lev_ref, min_e, min_in, min_n,
    partial, rhs_ref, min_w, col, col_w, col_e, drop,
):
    lane = lanes((8, 128))
    for r in range(0, H, 8):
        here = slice(r, r + 8)
        min_w[here, :] = roll(tile(min_e, 0, here), 1, 1)
        for total in (col_w, col_e):
            total[here, :] = jnp.zeros((8, 128), F32)
        for total in (col, drop):
            total[here, 128:256] = jnp.zeros((8, 128), F32)

    def level(k, carry):
        kf = k.astype(F32)

        def put(here, updated):
            t = t_s[k, here, 128:256]
            t_w = roll(t_s[k, here, :128], 1, 1)
            u_w = roll(u_s[k, here, :128], 1, 1)
            t_e = roll(tile(t_s, 2, k, here), -1, 1)
            f_w = (t - t_w) - (ADV / GRAD * u_w) * (t_w + t)
            f_e = (t_e - t) - (ADV / GRAD * u_s[k, here, 128:256]) * (t + t_e)
            f_w = jnp.where((lane == 0) & (min_w[here, :] > kf), GRAD * f_w, 0.0)
            f_e = jnp.where((lane == 127) & (tile(min_e, 1, here) > kf), GRAD * f_e, 0.0)
            col_w[here, :] = col_w[here, :] + thickness(kf) * f_w
            col_e[here, :] = col_e[here, :] + thickness(kf) * f_e
            partial[k, here, :128] = outer[k, here, :128] + roll(f_w, -1, 1)
            partial[k, here, 128:256] = updated + (f_e - f_w)
            partial[k, here, 256:W] = (outer[k, here, 128:] - roll(f_e, 1, 1))[:, : W - 256]

        sweep_level(k, 1, t_s, u_s, v_s, lev_ref, min_in, min_n, drop, col, put)
        return carry

    lax.fori_loop(0, KL, level, 0)
    for r in range(0, H, 8):
        here = slice(r, r + 8)
        c_w, c_e = ROOT * col_w[here, :], ROOT * col_e[here, :]
        rhs = ROOT * tile(col, 1, here) + tile(forcing, 1, here) + (c_e - c_w)
        rhs_ref[here, :128] = rhs_outer[here, :128] + roll(c_w, -1, 1)
        rhs_ref[here, 128:256] = jnp.where(tile(lev_ref, 1, here) > 0.0, rhs, 0.0)
        rhs_ref[here, 256:] = rhs_outer[here, 128:] - roll(c_e, 1, 1)


def middle_part(t_s, u_s, v_s, forcing, outer, rhs_outer, lev, min_e, min_in, min_n):
    vmem = pl.BlockSpec(memory_space=pltpu.VMEM)
    shape = jax.ShapeDtypeStruct
    return pl.pallas_call(
        middle_kernel,
        out_shape=[shape((KL, H, W), F32), shape((H, LW), F32)],
        in_specs=[vmem] * 10,
        out_specs=[vmem] * 2,
        scratch_shapes=[pltpu.VMEM((H, 128), F32)]
        + [pltpu.VMEM((H, LW), F32)]
        + [pltpu.VMEM((H, 128), F32)] * 2
        + [pltpu.VMEM((H, LW), F32)],
        compiler_params=pltpu.CompilerParams(vmem_limit_bytes=VMEM_LIMIT),
        name="middle",
    )(t_s, u_s, v_s, forcing, outer, rhs_outer, lev, min_e, min_in, min_n)


def sides_kernel(
    from_w, from_e, own_e, own_w, rhs_ref, lev_ref, row_n, row_s,
    rhs_x, lev_x, msg_n, msg_s, flux_e, flux_w,
    sum_e, sum_w,
):
    from_lane = rows((128, 128))

    def spread(x, first, count, precision):
        chosen = (from_lane >= first) & (from_lane < first + count)
        return jnp.dot(
            x, jnp.where(chosen, 1.0, 0.0), precision=precision, preferred_element_type=F32
        )

    def level_at(ref, at):
        return spread(ref[...], at, 1, lax.Precision.DEFAULT)

    lane = lanes((H, 128))
    kf = (lane - TR0).astype(F32)
    inside = (lane >= TR0) & (lane < TR0 + KL)
    weight = ROOT * thickness(kf)
    lev_w = jnp.minimum(level_at(from_w, LEV0 + 8), level_at(own_w, LEV0))
    lev_e = jnp.minimum(level_at(from_e, LEV0), level_at(own_e, LEV0 + 8))
    mw, me, mine_w, mine_e = from_w[...], from_e[...], own_w[...], own_e[...]
    f_w = GRAD * (mine_w - mw) - (ADV * roll(mw, TR0 - VE0, 1)) * (mine_w + mw)
    f_e = GRAD * (me - mine_e) - (ADV * roll(mine_e, TR0 - VE0, 1)) * (me + mine_e)
    f_w = jnp.where(inside & (lev_w > kf), f_w, 0.0)
    f_e = jnp.where(inside & (lev_e > kf), f_e, 0.0)
    flux_w[...] = f_w
    flux_e[...] = f_e
    sum_w[...] = spread(weight * f_w, TR0, KL, lax.Precision.HIGHEST)
    sum_e[...] = spread(weight * f_e, TR0, KL, lax.Precision.HIGHEST)
    lane = lanes((8, 128))
    for r in range(0, H, 8):
        here = slice(r, r + 8)
        mw, me = from_w[here, :], from_e[here, :]
        c_w, c_e = sum_w[here, :], sum_e[here, :]
        rhs_x[here, :128] = rhs_ref[here, :128] - jnp.where(lane == 0, c_w, 0.0)
        rhs_x[here, 128:256] = rhs_ref[here, 128:256]
        last = rhs_ref[here, 256:]
        last = jnp.where((lane >= 104) & (lane < 112), roll(me, 104, 1), last)
        last = jnp.where(lane >= 120, roll(mw, 120, 1), last)
        last = last + jnp.where(lane == 103, c_e, 0.0) - jnp.where(lane == 104, c_e, 0.0)
        rhs_x[here, 256:] = last + jnp.where(lane == 127, c_w, 0.0)
        lev_x[here, :256] = lev_ref[here, :256]
        last = lev_ref[here, 256:]
        last = jnp.where((lane >= 104) & (lane < 113), roll(me, 104 - LEV0, 1), last)
        last = jnp.where(lane >= 119, roll(mw, 119 - LEV0, 1), last)
        lev_x[here, 256:] = last
    msg_n[0:8, :] = rhs_x[H - 8 : H, :]
    msg_s[0:8, :] = rhs_x[0:8, :]
    msg_n[R_LEV : R_LEV + 16, :] = lev_x[H - 16 : H, :]
    msg_s[R_LEV : R_LEV + 16, :] = lev_x[0:16, :]
    for dst, at, src, base, lane0 in (
        (msg_s, R_TR, row_s, 0, C_T0), (msg_n, R_TR, row_n, 0, C_T1), (msg_n, R_VE, row_n, 16, C_V1),
    ):
        for r in (0, 8):
            mw, me = from_w[r : r + 8, :], from_e[r : r + 8, :]
            piece = src[base + r : base + r + 8, :]
            last = piece[:, 256:]
            last = jnp.where((lane >= 104) & (lane < 112), roll(me, 104 - lane0, 1), last)
            last = jnp.where(lane >= 120, roll(mw, 120 - lane0, 1), last)
            dst[at + r : at + r + 8, :256] = piece[:, :256]
            dst[at + r : at + r + 8, 256:] = last


def sides_part(from_w, from_e, own_e, own_w, rhs, lev, row_n, row_s):
    vmem = pl.BlockSpec(memory_space=pltpu.VMEM)
    shape = jax.ShapeDtypeStruct
    return pl.pallas_call(
        sides_kernel,
        out_shape=[
            shape((H, LW), F32),
            shape((H, LW), F32),
            shape((56, LW), F32),
            shape((40, LW), F32),
            shape((H, 128), F32),
            shape((H, 128), F32),
        ],
        in_specs=[vmem] * 8,
        out_specs=[vmem] * 6,
        scratch_shapes=[pltpu.VMEM((H, 128), F32)] * 2,
        compiler_params=pltpu.CompilerParams(vmem_limit_bytes=VMEM_LIMIT),
        name="sides",
    )(from_w, from_e, own_e, own_w, rhs, lev, row_n, row_s)


def basis_kernel(
    from_s, from_n, own_n, own_s, rhs_ref, lev_ref, partial,
    basis, diag, sums, updated,
    lev_x, rhs_x, w_e, w_w, w_n, w_s, weight, parts, slab_n, slab_s, sem,
):
    high, low = pl.ds(H - 8, 8), pl.ds(0, 8)
    loads = (
        pltpu.make_async_copy(partial.at[:, high, :], slab_n, sem.at[0]),
        pltpu.make_async_copy(partial.at[:, low, :], slab_s, sem.at[1]),
    )
    stores = (
        pltpu.make_async_copy(slab_n, updated.at[:, high, :], sem.at[2]),
        pltpu.make_async_copy(slab_s, updated.at[:, low, :], sem.at[3]),
    )
    for load in loads:
        load.start()
    lev_row = rows((16, LW))
    kf = lev_row.astype(F32)
    factor = ROOT * thickness(kf)

    def flux(t_from, t_to, vel, lev):
        value = GRAD * (t_to - t_from) - (ADV * vel) * (t_from + t_to)
        return jnp.where((lev_row < KL) & (lev > kf), value, 0.0)

    tr = slice(R_TR, R_TR + 16)
    ve = slice(R_VE, R_VE + 16)
    lev_n = jnp.minimum(lev_ref[H - 1 : H, :], from_n[R_LEV : R_LEV + 1, :])
    lev_s = jnp.minimum(lev_ref[0:1, :], from_s[R_LEV + 15 : R_LEV + 16, :])
    f_n = flux(own_n[tr, :], from_n[tr, :], own_n[ve, :], lev_n)
    f_s = flux(from_s[tr, :], own_s[tr, :], from_s[ve, :], lev_s)
    c_n = jnp.sum(factor * f_n, axis=0, keepdims=True)
    c_s = jnp.sum(factor * f_s, axis=0, keepdims=True)

    row = rows((8, LW))
    ninth = jnp.where(row == 7, from_s[R_LEV : R_LEV + 8, :], 0.0)
    ninth = jnp.where(row == 0, from_n[R_LEV + 8 : R_LEV + 16, :], ninth)
    tiles(lev_x, slice(0, H), lev_ref[...])
    tiles(lev_x, slice(H, H + 8), from_n[R_LEV : R_LEV + 8, :])
    tiles(lev_x, slice(H + 8, H + 16), ninth)
    tiles(lev_x, slice(H + 16, EH), from_s[R_LEV + 8 : R_LEV + 16, :])
    tiles(rhs_x, slice(0, 8), rhs_ref[0:8, :] - jnp.where(row == 0, c_s, 0.0))
    tiles(rhs_x, slice(8, H - 8), rhs_ref[8 : H - 8, :])
    tiles(rhs_x, slice(H - 8, H), rhs_ref[H - 8 : H, :] + jnp.where(row == 7, c_n, 0.0))
    tiles(rhs_x, slice(H, H + 8), from_n[0:8, :] - jnp.where(row == 0, c_n, 0.0))
    tiles(rhs_x, slice(H + 8, H + 16), jnp.zeros((8, LW), F32))
    tiles(rhs_x, slice(H + 16, EH), from_s[0:8, :] + jnp.where(row == 7, c_s, 0.0))

    def depth_of(i):
        lev = strided(lev_x, i, EB)
        return lev + lev * (lev - 1.0) * (0.25 / KL)

    def face(d, other):
        return jnp.where((d > 0.0) & (other > 0.0), 0.5 * (d + other), 0.0)

    lane = lanes((8, LW))
    first = depth_of(0)
    last = depth_of(EB - 1)
    beyond = roll(first, -1, 0)
    n_last = face(last, beyond)
    s = roll(n_last, 1, 0)
    lone = jnp.zeros((8, LW), F32)
    d = first
    for i in range(EB):
        if i < EB - 1:
            d_n = last if i == EB - 2 else depth_of(i + 1)
            n = face(d, d_n)
        else:
            d_n, n = beyond, n_last
        e = face(d, roll(d, -1, 1))
        w = roll(e, 1, 1)
        faces = (e + w) + (n + s)
        dg = jnp.where(d > 0.0, SHIFT * d + faces, 1.0)
        inv = 1.0 / dg
        z = strided(rhs_x, i, EB) * inv
        basis[0, i] = z
        inv = 2.0 * inv
        w_e[i] = e * inv
        w_w[i] = w * inv
        w_n[i] = n * inv
        w_s[i] = s * inv
        diag[i] = dg
        own = (lane < W) & (row * EB + i < H)
        own = jnp.where(own, dg, 0.0)
        joined = faces > 0.0
        weight[i] = jnp.where(joined, own, 0.0)
        lone = lone + jnp.where(joined, 0.0, own * z * z)
        d, s = d_n, n

    def fold(x):
        return jnp.sum(x[:, :128] + x[:, 128:256] + x[:, 256:], axis=0, keepdims=True)

    parts[...] = jnp.zeros((24, 128), F32)
    parts[16:17, :] = fold(lone)

    def step(k, older):
        now = basis.at[k - 1]
        even = jnp.zeros((8, LW), F32)
        odd = jnp.zeros((8, LW), F32)
        first = now[0]
        last = now[EB - 1]
        beyond = roll(first, -1, 0)
        c_s = roll(last, 1, 0)
        c = first
        for i in range(EB):
            if i < EB - 1:
                c_n = last if i == EB - 2 else now[i + 1]
            else:
                c_n = beyond
            image = w_e[i] * roll(c, -1, 1) + w_w[i] * roll(c, 1, 1)
            image = image + (w_n[i] * c_n + w_s[i] * c_s)
            value = 0.5 * image if older is None else image - basis[older, i]
            basis[k, i] = value
            scaled = weight[i] * c
            even = even + scaled * c
            odd = odd + scaled * value
            c_s, c = c, c_n
        parts[2 * k - 2 : 2 * k - 1, :] = fold(even)
        parts[2 * k - 1 : 2 * k, :] = fold(odd)

    step(1, None)
    row360 = rows((8, W))
    for load in loads:
        load.wait()
    for k in range(KL):
        at_n = jnp.where(row360 == 7, f_n[k : k + 1, :W], 0.0)
        at_s = jnp.where(row360 == 0, f_s[k : k + 1, :W], 0.0)
        slab_n[k] = slab_n[k] + at_n
        slab_s[k] = slab_s[k] - at_s
    for store in stores:
        store.start()
    for k in range(2, ITERS + 1):
        step(k, k - 2)

    total = jnp.sum(parts[...], axis=1, keepdims=True)
    prow = rows((24, 128))
    plane = lanes((24, 128))
    place = (prow < 16) & ((plane == prow) | (plane == 128 - prow)) | (prow == 16) & (plane == 64)
    line = jnp.sum(jnp.where(place, total, 0.0), axis=0, keepdims=True)
    sums[...] = jnp.broadcast_to(line, sums.shape)
    for store in stores:
        store.wait()


def basis_part(from_s, from_n, own_n, own_s, rhs, lev, partial, count):
    vmem = pl.BlockSpec(memory_space=pltpu.VMEM)
    hbm = pl.BlockSpec(memory_space=pltpu.HBM)
    shape = jax.ShapeDtypeStruct
    return pl.pallas_call(
        basis_kernel,
        out_shape=[
            shape((ITERS + 1, EB, 8, LW), F32),
            shape((EB, 8, LW), F32),
            shape((count, 128), F32),
            shape((KL, H, W), F32),
        ],
        in_specs=[vmem] * 6 + [hbm],
        out_specs=[vmem] * 3 + [hbm],
        input_output_aliases={6: 3},
        scratch_shapes=[pltpu.VMEM((3, EH, 128), F32)] * 2
        + [pltpu.VMEM((EB, 8, LW), F32)] * 5
        + [pltpu.VMEM((24, 128), F32)]
        + [pltpu.VMEM((KL, 8, W), F32)] * 2
        + [pltpu.SemaphoreType.DMA((4,))],
        compiler_params=pltpu.CompilerParams(vmem_limit_bytes=VMEM_LIMIT),
        name="basis",
    )(from_s, from_n, own_n, own_s, rhs, lev, partial)


def polynomials(gathered):
    sums = jnp.broadcast_to(jnp.sum(gathered, axis=0, keepdims=True), (8, 128))

    def pick(lane):
        return jnp.broadcast_to(sums[:, lane : lane + 1], (8, 128))

    moments = [pick(j) for j in range(2 * ITERS)]
    alone = pick(64)
    now = [x if j < 2 else 2.0 * x - moments[j % 2] for j, x in enumerate(moments)]
    before = [0.0] * len(now)
    one = jnp.ones((8, 128), F32)
    rest, rest_before = [one], []
    lift, lift_before = [], []
    at0, at0_before = alone, 0.0
    at1, at1_before = one, 0.0

    def coefficient(p, j):
        return p[j] if 0 <= j < len(p) else None

    def total(terms):
        terms = [x for x in terms if x is not None]
        return sum(terms[1:], terms[0]) if terms else jnp.zeros((8, 128), F32)

    def advance(p, p_before, a, b, count, constant=None):
        out = []
        for j in range(count):
            terms = [constant if j == 0 else None]
            below, above = coefficient(p, j - 1), coefficient(p, j + 1)
            if below is not None:
                terms.append(below if j == 1 else 0.5 * below)
            if above is not None:
                terms.append(0.5 * above)
            if coefficient(p, j) is not None:
                terms.append(-(a * p[j]))
            if coefficient(p_before, j) is not None:
                terms.append(-(b * p_before[j]))
            out.append(total(terms))
        return out

    def lone_part(j):
        return (at0, None, -at0, None)[j % 4]

    last_inv = last_ratio = None
    for k in range(ITERS):
        size = total([now[k], lone_part(k)])
        cross = total([now[k + 1], lone_part(k + 1)])
        inv = 1.0 / size
        ratio = cross * inv * (1.0 if k == 0 else 0.5)
        if k == 0:
            a, b = ratio, jnp.zeros((8, 128), F32)
        else:
            a, b = ratio - last_ratio, size * last_inv * (1.0 if k == 1 else 0.5)
        last_inv, last_ratio = inv, ratio
        after = [None] * len(now)
        for j in range(k + 1, 2 * ITERS - 1 - k):
            after[j] = 0.5 * (now[j - 1] + now[j + 1]) - a * now[j] - b * before[j]
        before, now = now, after
        lift, lift_before = advance(lift, lift_before, a, b, k + 1, at1), lift
        rest, rest_before = advance(rest, rest_before, a, b, k + 2), rest
        at0, at0_before = -(a * at0) - b * at0_before, at0
        at1, at1_before = (1.0 - a) * at1 - b * at1_before, at1
    scale = 1.0 / at1
    return [x * scale for x in lift], [x * scale for x in rest]


def finish_kernel(gathered, basis, diag, sea, residual, sea_t, residual_t):
    lift, rest = polynomials(gathered[...])
    for i in range(EB):
        for j in range(3):
            here = slice(128 * j, 128 * j + 128)
            c = basis[0, i, :, here]
            a, b = lift[0] * c, rest[0] * c
            for k in range(1, ITERS + 1):
                c = basis[k, i, :, here]
                b = b + rest[k] * c
                if k < ITERS:
                    a = a + lift[k] * c
            sea_t[j, pl.ds(i, 8, EB), :] = a
            residual_t[j, pl.ds(i, 8, EB), :] = diag[i, :, here] * b
    for out, by_tile in ((sea, sea_t), (residual, residual_t)):
        out[:, 0:128] = by_tile[0, :H, :]
        out[:, 128:256] = by_tile[1, :H, :]
        out[:, 256:W] = by_tile[2, :H, : W - 256]


def finish_part(gathered, basis, diag):
    vmem = pl.BlockSpec(memory_space=pltpu.VMEM)
    shape = jax.ShapeDtypeStruct
    return pl.pallas_call(
        finish_kernel,
        out_shape=[shape((H, W), F32), shape((H, W), F32)],
        in_specs=[vmem] * 3,
        out_specs=[vmem] * 2,
        scratch_shapes=[pltpu.VMEM((3, EH, 128), F32)] * 2,
        compiler_params=pltpu.CompilerParams(vmem_limit_bytes=VMEM_LIMIT),
        name="finish",
    )(gathered, basis, diag)


def edges_kernel(partial, flux_e, flux_w, dst, level, sem):
    def store(k):
        return pltpu.make_async_copy(level.at[k], dst.at[k], sem.at[k])

    lane = lanes((8, 128))
    lane_e = lanes((8, W - 256))
    for k in range(KL):
        for r in range(0, H, 8):
            here = slice(r, r + 8)
            at_w = jnp.where(lane == 0, roll(flux_w[here, :], -TR0 - k, 1), 0.0)
            at_e = roll(flux_e[here, :], W - 257 - TR0 - k, 1)[:, : W - 256]
            at_e = jnp.where(lane_e == W - 257, at_e, 0.0)
            level[k, here, :128] = partial[k, here, :128] - at_w
            level[k, here, 128:256] = partial[k, here, 128:256]
            level[k, here, 256:W] = partial[k, here, 256:W] + at_e
        store(k).start()
    for k in range(KL):
        store(k).wait()


def edges_part(partial, flux_e, flux_w):
    vmem = pl.BlockSpec(memory_space=pltpu.VMEM)
    hbm = pl.BlockSpec(memory_space=pltpu.HBM)
    return pl.pallas_call(
        edges_kernel,
        out_shape=jax.ShapeDtypeStruct((KL, H, W), F32),
        in_specs=[vmem] * 3,
        out_specs=hbm,
        scratch_shapes=[pltpu.VMEM((KL, H, W), F32), pltpu.SemaphoreType.DMA((KL,))],
        compiler_params=pltpu.CompilerParams(vmem_limit_bytes=VMEM_LIMIT),
        name="edges",
    )(partial, flux_e, flux_w)


def shards(tracer, east_velocity, north_velocity, kmt, block_mask, surface_forcing):
    nx, ny = lax.axis_size("gx"), lax.axis_size("gy")
    *fields, lev, min_e, min_in, min_n, msg_e, msg_w, row_n, row_s = outer_part(
        block_mask, kmt, surface_forcing, tracer, east_velocity, north_velocity
    )
    from_w = lax.ppermute(msg_e, "gx", [(i, (i + 1) % nx) for i in range(nx)])
    from_e = lax.ppermute(msg_w, "gx", [((i + 1) % nx, i) for i in range(nx)])
    partial, rhs = middle_part(*fields, lev, min_e, min_in, min_n)
    rhs_x, lev_x, msg_n, msg_s, flux_e, flux_w = sides_part(
        from_w, from_e, msg_e, msg_w, rhs, lev, row_n, row_s
    )
    from_s = lax.ppermute(msg_n, "gy", [(i, (i + 1) % ny) for i in range(ny)])
    from_n = lax.ppermute(msg_s, "gy", [((i + 1) % ny, i) for i in range(ny)])
    partial = edges_part(partial, flux_e, flux_w)
    basis, diag, sums, updated = basis_part(
        from_s, from_n, msg_n, msg_s, rhs_x, lev_x, partial, nx * ny
    )
    gathered = lax.all_to_all(sums, ("gx", "gy"), 0, 0, tiled=True)
    sea_level, residual = finish_part(gathered, basis, diag)
    return (updated, sea_level, residual)


def solution(mesh):
    in_specs = (
        P(None, "gy", "gx"),
        P(None, "gy", "gx"),
        P(None, "gy", "gx"),
        P("gy", "gx"),
        P("gy", "gx"),
        P("gy", "gx"),
    )
    out_specs = (P(None, "gy", "gx"), P("gy", "gx"), P("gy", "gx"))
    return jax.shard_map(shards, mesh=mesh, in_specs=in_specs, out_specs=out_specs, check_vma=False)
```

```python
import math

import jax
import jax.numpy as jnp
from jax import lax
from jax.experimental import pallas as pl
from jax.experimental.pallas import tpu as pltpu
from jax.sharding import PartitionSpec as P

BSX = 90
BSY = 60
KL = 12
ITERS = 8

DT_STEP = 0.2
KAPPA_H = 0.2
KAPPA_V = 0.3
SHIFT = 0.002

H = 120
W = 360
LW = 384
EH = 144

EB = EH // 8

GRAD = DT_STEP * KAPPA_H
ADV = DT_STEP * 0.5
VERT = DT_STEP * KAPPA_V
ROOT = 1.0 / math.sqrt(KL)

LEV0 = 8
TR0 = 17
VE0 = 29
C_T0 = 48
C_T1 = 56
C_V1 = 64

THIRD = H // 3
WIDTH = 42

CHUNKS = (0, 1, 3, 6, 9, 12)
EARLY = 8

R_LEV = 8
R_TR = 24
R_VE = 40

F32 = jnp.float32
VMEM_LIMIT = 40 * 1024 * 1024


def lanes(shape):
    return lax.broadcasted_iota(jnp.int32, shape, 1)


def rows(shape):
    return lax.broadcasted_iota(jnp.int32, shape, 0)


def widen(x, width):
    return jnp.concatenate([x, jnp.zeros((x.shape[0], width - x.shape[1]), x.dtype)], axis=1)


def roll(x, shift, axis):
    shift = shift % x.shape[axis]
    return x if shift == 0 else pltpu.roll(x, shift, axis)


def strided(ref, i, step):
    return jnp.concatenate([ref[j, pl.ds(i, 8, step), :] for j in range(3)], axis=1)


def put_strided(ref, i, step, value):
    for j in range(3):
        ref[j, pl.ds(i, 8, step), :] = value[:, 128 * j : 128 * j + 128]


def tiles(ref, here, value):
    for j in range(3):
        ref[j, here, :] = value[:, 128 * j : 128 * j + 128]


def thickness(level):
    return 1.0 + (0.5 / KL) * level


def tile(ref, j, *at):
    if ref.shape[-1] == LW or j < 2:
        return ref[(*at, slice(128 * j, 128 * j + 128))]
    return widen(ref[(*at, slice(256, W))], 128)


def sweep_level(k, j, t_s, u_s, v_s, lev_ref, min_e, min_n, drop, col, put):
    static = isinstance(k, int)
    kf = float(k) if static else k.astype(F32)
    first, last = static and k == 0, static and k == KL - 1
    above = min(k + 1, KL - 1) if static else jnp.minimum(k + 1, KL - 1)
    lane = lanes((8, 128))
    row = rows((8, 128))
    f_low = jnp.zeros((8, 128), F32)
    t = tile(t_s, j, k, slice(0, 8))
    t_turned = roll(t, -1, 0)
    for r in range(0, H, 8):
        here = slice(r, r + 8)
        if r + 8 < H:
            ahead = tile(t_s, j, k, slice(r + 8, r + 16))
            ahead_turned = roll(ahead, -1, 0)
            t_n = jnp.where(row == 7, ahead_turned, t_turned)
        else:
            ahead = ahead_turned = None
            t_n = t_turned
        t_e = roll(t, -1, 1)
        f_e = (t_e - t) - (ADV / GRAD * tile(u_s, j, k, here)) * (t + t_e)
        f_n = (t_n - t) - (ADV / GRAD * tile(v_s, j, k, here)) * (t + t_n)
        f_e = jnp.where(tile(min_e, j, here) > kf, f_e, 0.0)
        f_n = jnp.where(tile(min_n, j, here) > kf, f_n, 0.0)
        f_w = roll(f_e, 1, 1)
        f_turned = roll(f_n, 1, 0)
        f_s = jnp.where(row == 0, f_low, f_turned)
        f_low = f_turned
        lev = tile(lev_ref, j, here)
        gain = (f_e - f_w) + (f_n - f_s)
        if not last:
            step = VERT / GRAD * (tile(t_s, j, above, here) - t)
            step = jnp.where(lev > kf + 1.0, step, 0.0)
            gain = gain + step
        if not first:
            gain = gain - tile(drop, j, here)
        if not last:
            drop[here, 128 * j : 128 * j + 128] = step
        updated = t + GRAD * gain
        put(here, updated)
        share = jnp.where(lev > kf, thickness(kf) * updated, 0.0)
        col[here, 128 * j : 128 * j + 128] = share if first else tile(col, j, here) + share
        t, t_turned = ahead, ahead_turned


def outer_kernel(
    mask_hbm, kmt_hbm, forcing_hbm, t_hbm, u_hbm, v_hbm,
    t_s, u_s, v_s, forcing, outer, rhs_ref, lev_ref, min_e, min_in, min_n, msg_e, msg_w, out_e, out_w, row_n, row_s,
    kmt, mask, col, drop, sem_in, sem_2d,
):
    def load(i, k):
        src, dst = ((t_hbm, t_s), (u_hbm, u_s), (v_hbm, v_s))[i]
        here = slice(CHUNKS[k], CHUNKS[k + 1])
        return pltpu.make_async_copy(src.at[here], dst.at[here], sem_in.at[i, k])

    load_mask = pltpu.make_async_copy(mask_hbm, mask, sem_2d.at[0])
    load_kmt = pltpu.make_async_copy(kmt_hbm, kmt, sem_2d.at[1])
    load_forcing = pltpu.make_async_copy(forcing_hbm, forcing, sem_2d.at[2])
    load_mask.start()
    load_kmt.start()
    for k in range(len(CHUNKS) - 1):
        for i in range(3):
            load(i, k).start(priority=0 if k == 0 else 1)
    load_forcing.start(priority=1)

    lane = lanes((8, LW))
    row = rows((8, LW))
    load_mask.wait()
    load_kmt.wait()
    for r in range(0, H, 8):
        keep = jnp.zeros((8, LW), jnp.int32)
        for b in range(W // BSX):
            inside = (lane >= b * BSX) & (lane < (b + 1) * BSX)
            upper = jnp.where(row + r < BSY, mask[0, b], mask[1, b])
            keep = jnp.where(inside, upper, keep)
        lev = widen(kmt[r : r + 8, :], LW) * keep
        lev_ref[r : r + 8, :] = lev.astype(F32)
    inner = (lane != 127) & (lane != 255)
    for r in range(0, H, 8):
        here = slice(r, r + 8)
        lev = lev_ref[here, :]
        if r + 8 < H:
            north = lev_ref[r + 1 : r + 9, :]
        else:
            north = jnp.where(row == 7, 0.0, roll(lev, -1, 0))
        east = jnp.minimum(lev, roll(lev, -1, 1))
        min_e[here, :] = east
        min_in[here, :] = jnp.where(inner, east, 0.0)
        min_n[here, :] = jnp.minimum(lev, north)
    row_n[...] = jnp.zeros((32, LW), F32)
    row_s[...] = jnp.zeros((16, LW), F32)

    lane128 = lanes((8, 128))

    def pack(levels, r, east, west):
        here = slice(r, r + 8)
        for k in levels:
            t2 = roll(tile(t_s, 2, k, here), TR0 + k - 103, 1)
            u2 = roll(tile(u_s, 2, k, here), VE0 + k - 103, 1)
            t0 = roll(tile(t_s, 0, k, here), TR0 + k, 1)
            east = jnp.where(lane128 == TR0 + k, t2, east)
            east = jnp.where(lane128 == VE0 + k, u2, east)
            west = jnp.where(lane128 == TR0 + k, t0, west)
        return east, west

    load(0, 0).wait()
    for k in range(KL):
        if k + 1 in CHUNKS[:-1]:
            load(0, CHUNKS.index(k + 1)).wait()
        if k in CHUNKS:
            load(1, CHUNKS.index(k)).wait()
            load(2, CHUNKS.index(k)).wait()
        if k == EARLY:
            for r in range(0, H, 8):
                zero = jnp.zeros((8, 128), F32)
                msg_e[r : r + 8, :], msg_w[r : r + 8, :] = pack(range(EARLY), r, zero, zero)
        for j in (0, 2):

            def put(here, updated, k=k, j=j):
                outer[k, here, 64 * j : 64 * j + 128] = updated

            sweep_level(k, j, t_s, u_s, v_s, lev_ref, min_in, min_n, drop, col, put)
        row_s[k : k + 1, :] = widen(t_s[k, 0:1, :], LW)
        row_n[k : k + 1, :] = widen(t_s[k, H - 1 : H, :], LW)
        row_n[16 + k : 17 + k, :] = widen(v_s[k, H - 1 : H, :], LW)

    load_forcing.wait()
    lane = lane128
    for r in range(0, H, 8):
        here = slice(r, r + 8)
        lev0, lev2 = tile(lev_ref, 0, here), tile(lev_ref, 2, here)
        rhs0 = jnp.where(lev0 > 0.0, ROOT * tile(col, 0, here) + tile(forcing, 0, here), 0.0)
        rhs2 = jnp.where(lev2 > 0.0, ROOT * tile(col, 2, here) + tile(forcing, 2, here), 0.0)
        rhs_ref[here, :128] = rhs0
        rhs_ref[here, 128:] = rhs2
        east, west = pack(range(EARLY, KL), r, msg_e[here, :], msg_w[here, :])
        head_e = jnp.where(lane < LEV0, roll(rhs2, 32, 1), roll(lev2, LEV0 - 95, 1))
        head_w = jnp.where(lane < LEV0, rhs0, roll(lev0, LEV0, 1))
        east = jnp.where(lane < TR0, head_e, east)
        west = jnp.where(lane < TR0, head_w, west)
        if r < 16:
            for at, src, base in ((C_T0, row_s, 0), (C_T1, row_n, 0), (C_V1, row_n, 16)):
                inside = (lane >= at) & (lane < at + 8)
                piece = src[base + r : base + r + 8, :]
                east = jnp.where(inside, roll(piece[:, 256:], at - 96, 1), east)
                west = jnp.where(inside, roll(piece[:, :128], at, 1), west)
        msg_e[here, :] = east
        msg_w[here, :] = west
    for dst, src in ((out_e, msg_e), (out_w, msg_w)):
        for r in range(0, THIRD, 8):
            value = src[r : r + 8, :]
            for i in (1, 2):
                part = roll(src[r + THIRD * i : r + THIRD * i + 8, :], WIDTH * i, 1)
                value = jnp.where(lane < WIDTH * i, value, part)
            dst[r : r + 8, :] = value
        dst[THIRD : THIRD + 16, :] = src[0:16, :]


def outer_part(mask, kmt, forcing, tracer, east, north):
    vmem = pl.BlockSpec(memory_space=pltpu.VMEM)
    hbm = pl.BlockSpec(memory_space=pltpu.HBM)
    shape = jax.ShapeDtypeStruct
    return pl.pallas_call(
        outer_kernel,
        out_shape=[shape((KL, H, W), F32)] * 3
        + [
            shape((H, W), F32),
            shape((KL, H, 256), F32),
            shape((H, 256), F32),
            shape((H, LW), F32),
            shape((H, LW), F32),
            shape((H, LW), F32),
            shape((H, LW), F32),
            shape((H, 128), F32),
            shape((H, 128), F32),
            shape((THIRD + 16, 128), F32),
            shape((THIRD + 16, 128), F32),
            shape((32, LW), F32),
            shape((16, LW), F32),
        ],
        in_specs=[hbm] * 6,
        out_specs=[vmem] * 16,
        scratch_shapes=[pltpu.VMEM((H, W), jnp.int32), pltpu.SMEM(mask.shape, jnp.int32)]
        + [pltpu.VMEM((H, LW), F32)] * 2
        + [pltpu.SemaphoreType.DMA((3, len(CHUNKS) - 1)), pltpu.SemaphoreType.DMA((3,))],
        compiler_params=pltpu.CompilerParams(vmem_limit_bytes=VMEM_LIMIT),
        name="outer",
    )(*(pltpu.with_memory_space_constraint(x, pltpu.HBM) for x in (mask, kmt, forcing, tracer, east, north)))


def middle_kernel(
    t_s, u_s, v_s, forcing, outer, rhs_outer, lev_ref, min_e, min_in, min_n,
    partial, rhs_ref, min_w, col, col_w, col_e, drop,
):
    lane = lanes((8, 128))
    for r in range(0, H, 8):
        here = slice(r, r + 8)
        min_w[here, :] = roll(tile(min_e, 0, here), 1, 1)
        for total in (col_w, col_e):
            total[here, :] = jnp.zeros((8, 128), F32)
        for total in (col, drop):
            total[here, 128:256] = jnp.zeros((8, 128), F32)

    def level(k, carry):
        kf = k.astype(F32)

        def put(here, updated):
            t = t_s[k, here, 128:256]
            t_w = roll(t_s[k, here, :128], 1, 1)
            u_w = roll(u_s[k, here, :128], 1, 1)
            t_e = roll(tile(t_s, 2, k, here), -1, 1)
            f_w = (t - t_w) - (ADV / GRAD * u_w) * (t_w + t)
            f_e = (t_e - t) - (ADV / GRAD * u_s[k, here, 128:256]) * (t + t_e)
            f_w = jnp.where((lane == 0) & (min_w[here, :] > kf), GRAD * f_w, 0.0)
            f_e = jnp.where((lane == 127) & (tile(min_e, 1, here) > kf), GRAD * f_e, 0.0)
            col_w[here, :] = col_w[here, :] + thickness(kf) * f_w
            col_e[here, :] = col_e[here, :] + thickness(kf) * f_e
            partial[k, here, :128] = outer[k, here, :128] + roll(f_w, -1, 1)
            partial[k, here, 128:256] = updated + (f_e - f_w)
            partial[k, here, 256:W] = (outer[k, here, 128:] - roll(f_e, 1, 1))[:, : W - 256]

        sweep_level(k, 1, t_s, u_s, v_s, lev_ref, min_in, min_n, drop, col, put)
        return carry

    lax.fori_loop(0, KL, level, 0)
    for r in range(0, H, 8):
        here = slice(r, r + 8)
        c_w, c_e = ROOT * col_w[here, :], ROOT * col_e[here, :]
        rhs = ROOT * tile(col, 1, here) + tile(forcing, 1, here) + (c_e - c_w)
        rhs_ref[here, :128] = rhs_outer[here, :128] + roll(c_w, -1, 1)
        rhs_ref[here, 128:256] = jnp.where(tile(lev_ref, 1, here) > 0.0, rhs, 0.0)
        rhs_ref[here, 256:] = rhs_outer[here, 128:] - roll(c_e, 1, 1)


def middle_part(t_s, u_s, v_s, forcing, outer, rhs_outer, lev, min_e, min_in, min_n):
    vmem = pl.BlockSpec(memory_space=pltpu.VMEM)
    shape = jax.ShapeDtypeStruct
    return pl.pallas_call(
        middle_kernel,
        out_shape=[shape((KL, H, W), F32), shape((H, LW), F32)],
        in_specs=[vmem] * 10,
        out_specs=[vmem] * 2,
        scratch_shapes=[pltpu.VMEM((H, 128), F32)]
        + [pltpu.VMEM((H, LW), F32)]
        + [pltpu.VMEM((H, 128), F32)] * 2
        + [pltpu.VMEM((H, LW), F32)],
        compiler_params=pltpu.CompilerParams(vmem_limit_bytes=VMEM_LIMIT),
        name="middle",
    )(t_s, u_s, v_s, forcing, outer, rhs_outer, lev, min_e, min_in, min_n)


def sides_kernel(
    sent_w, sent_e, own_e, own_w, rhs_ref, lev_ref, row_n, row_s,
    rhs_x, lev_x, msg_n, msg_s, flux_e, flux_w,
    from_w, from_e, sum_e, sum_w,
):
    for dst, src in ((from_w, sent_w), (from_e, sent_e)):
        for i in range(3):
            dst[THIRD * i : THIRD * i + THIRD, :] = roll(src[0:THIRD, :], -WIDTH * i, 1)
    from_lane = rows((128, 128))

    def spread(x, first, count, precision):
        chosen = (from_lane >= first) & (from_lane < first + count)
        return jnp.dot(
            x, jnp.where(chosen, 1.0, 0.0), precision=precision, preferred_element_type=F32
        )

    def level_at(ref, at):
        return spread(ref[...], at, 1, lax.Precision.DEFAULT)

    lane = lanes((H, 128))
    kf = (lane - TR0).astype(F32)
    inside = (lane >= TR0) & (lane < TR0 + KL)
    weight = ROOT * thickness(kf)
    lev_w = jnp.minimum(level_at(from_w, LEV0 + 8), level_at(own_w, LEV0))
    lev_e = jnp.minimum(level_at(from_e, LEV0), level_at(own_e, LEV0 + 8))
    mw, me, mine_w, mine_e = from_w[...], from_e[...], own_w[...], own_e[...]
    f_w = GRAD * (mine_w - mw) - (ADV * roll(mw, TR0 - VE0, 1)) * (mine_w + mw)
    f_e = GRAD * (me - mine_e) - (ADV * roll(mine_e, TR0 - VE0, 1)) * (me + mine_e)
    f_w = jnp.where(inside & (lev_w > kf), f_w, 0.0)
    f_e = jnp.where(inside & (lev_e > kf), f_e, 0.0)
    flux_w[...] = f_w
    flux_e[...] = f_e
    sum_w[...] = spread(weight * f_w, TR0, KL, lax.Precision.HIGHEST)
    sum_e[...] = spread(weight * f_e, TR0, KL, lax.Precision.HIGHEST)
    lane = lanes((8, 128))
    for r in range(0, H, 8):
        here = slice(r, r + 8)
        mw, me = from_w[here, :], from_e[here, :]
        c_w, c_e = sum_w[here, :], sum_e[here, :]
        rhs_x[here, :128] = rhs_ref[here, :128] - jnp.where(lane == 0, c_w, 0.0)
        rhs_x[here, 128:256] = rhs_ref[here, 128:256]
        last = rhs_ref[here, 256:]
        last = jnp.where((lane >= 104) & (lane < 112), roll(me, 104, 1), last)
        last = jnp.where(lane >= 120, roll(mw, 120, 1), last)
        last = last + jnp.where(lane == 103, c_e, 0.0) - jnp.where(lane == 104, c_e, 0.0)
        rhs_x[here, 256:] = last + jnp.where(lane == 127, c_w, 0.0)
        lev_x[here, :256] = lev_ref[here, :256]
        last = lev_ref[here, 256:]
        last = jnp.where((lane >= 104) & (lane < 113), roll(me, 104 - LEV0, 1), last)
        last = jnp.where(lane >= 119, roll(mw, 119 - LEV0, 1), last)
        lev_x[here, 256:] = last
    msg_n[0:8, :] = rhs_x[H - 8 : H, :]
    msg_s[0:8, :] = rhs_x[0:8, :]
    msg_n[R_LEV : R_LEV + 16, :] = lev_x[H - 16 : H, :]
    msg_s[R_LEV : R_LEV + 16, :] = lev_x[0:16, :]
    for dst, at, src, base, lane0 in (
        (msg_s, R_TR, row_s, 0, C_T0), (msg_n, R_TR, row_n, 0, C_T1), (msg_n, R_VE, row_n, 16, C_V1),
    ):
        for r in (0, 8):
            corner = slice(THIRD + r, THIRD + r + 8)
            mw, me = sent_w[corner, :], sent_e[corner, :]
            piece = src[base + r : base + r + 8, :]
            last = piece[:, 256:]
            last = jnp.where((lane >= 104) & (lane < 112), roll(me, 104 - lane0, 1), last)
            last = jnp.where(lane >= 120, roll(mw, 120 - lane0, 1), last)
            dst[at + r : at + r + 8, :256] = piece[:, :256]
            dst[at + r : at + r + 8, 256:] = last


def sides_part(from_w, from_e, own_e, own_w, rhs, lev, row_n, row_s):
    vmem = pl.BlockSpec(memory_space=pltpu.VMEM)
    shape = jax.ShapeDtypeStruct
    return pl.pallas_call(
        sides_kernel,
        out_shape=[
            shape((H, LW), F32),
            shape((H, LW), F32),
            shape((56, LW), F32),
            shape((40, LW), F32),
            shape((H, 128), F32),
            shape((H, 128), F32),
        ],
        in_specs=[vmem] * 8,
        out_specs=[vmem] * 6,
        scratch_shapes=[pltpu.VMEM((H, 128), F32)] * 4,
        compiler_params=pltpu.CompilerParams(vmem_limit_bytes=VMEM_LIMIT),
        name="sides",
    )(from_w, from_e, own_e, own_w, rhs, lev, row_n, row_s)


def basis_kernel(
    from_s, from_n, own_n, own_s, rhs_ref, lev_ref, partial,
    basis, diag, sums, updated,
    lev_x, rhs_x, w_e, w_w, w_n, w_s, weight, parts, slab_n, slab_s, sem,
):
    high, low = pl.ds(H - 8, 8), pl.ds(0, 8)
    loads = (
        pltpu.make_async_copy(partial.at[:, high, :], slab_n, sem.at[0]),
        pltpu.make_async_copy(partial.at[:, low, :], slab_s, sem.at[1]),
    )
    stores = (
        pltpu.make_async_copy(slab_n, updated.at[:, high, :], sem.at[2]),
        pltpu.make_async_copy(slab_s, updated.at[:, low, :], sem.at[3]),
    )
    for load in loads:
        load.start()
    lev_row = rows((16, LW))
    kf = lev_row.astype(F32)
    factor = ROOT * thickness(kf)

    def flux(t_from, t_to, vel, lev):
        value = GRAD * (t_to - t_from) - (ADV * vel) * (t_from + t_to)
        return jnp.where((lev_row < KL) & (lev > kf), value, 0.0)

    tr = slice(R_TR, R_TR + 16)
    ve = slice(R_VE, R_VE + 16)
    lev_n = jnp.minimum(lev_ref[H - 1 : H, :], from_n[R_LEV : R_LEV + 1, :])
    lev_s = jnp.minimum(lev_ref[0:1, :], from_s[R_LEV + 15 : R_LEV + 16, :])
    f_n = flux(own_n[tr, :], from_n[tr, :], own_n[ve, :], lev_n)
    f_s = flux(from_s[tr, :], own_s[tr, :], from_s[ve, :], lev_s)
    c_n = jnp.sum(factor * f_n, axis=0, keepdims=True)
    c_s = jnp.sum(factor * f_s, axis=0, keepdims=True)

    row = rows((8, LW))
    ninth = jnp.where(row == 7, from_s[R_LEV : R_LEV + 8, :], 0.0)
    ninth = jnp.where(row == 0, from_n[R_LEV + 8 : R_LEV + 16, :], ninth)
    tiles(lev_x, slice(0, H), lev_ref[...])
    tiles(lev_x, slice(H, H + 8), from_n[R_LEV : R_LEV + 8, :])
    tiles(lev_x, slice(H + 8, H + 16), ninth)
    tiles(lev_x, slice(H + 16, EH), from_s[R_LEV + 8 : R_LEV + 16, :])
    tiles(rhs_x, slice(0, 8), rhs_ref[0:8, :] - jnp.where(row == 0, c_s, 0.0))
    tiles(rhs_x, slice(8, H - 8), rhs_ref[8 : H - 8, :])
    tiles(rhs_x, slice(H - 8, H), rhs_ref[H - 8 : H, :] + jnp.where(row == 7, c_n, 0.0))
    tiles(rhs_x, slice(H, H + 8), from_n[0:8, :] - jnp.where(row == 0, c_n, 0.0))
    tiles(rhs_x, slice(H + 8, H + 16), jnp.zeros((8, LW), F32))
    tiles(rhs_x, slice(H + 16, EH), from_s[0:8, :] + jnp.where(row == 7, c_s, 0.0))

    def depth_of(i):
        lev = strided(lev_x, i, EB)
        return lev + lev * (lev - 1.0) * (0.25 / KL)

    def face(d, other):
        return jnp.where((d > 0.0) & (other > 0.0), 0.5 * (d + other), 0.0)

    lane = lanes((8, LW))
    first = depth_of(0)
    last = depth_of(EB - 1)
    beyond = roll(first, -1, 0)
    n_last = face(last, beyond)
    s = roll(n_last, 1, 0)
    lone = jnp.zeros((8, LW), F32)
    d = first
    for i in range(EB):
        if i < EB - 1:
            d_n = last if i == EB - 2 else depth_of(i + 1)
            n = face(d, d_n)
        else:
            d_n, n = beyond, n_last
        e = face(d, roll(d, -1, 1))
        w = roll(e, 1, 1)
        faces = (e + w) + (n + s)
        dg = jnp.where(d > 0.0, SHIFT * d + faces, 1.0)
        inv = 1.0 / dg
        z = strided(rhs_x, i, EB) * inv
        basis[0, i] = z
        inv = 2.0 * inv
        w_e[i] = e * inv
        w_w[i] = w * inv
        w_n[i] = n * inv
        w_s[i] = s * inv
        diag[i] = dg
        own = (lane < W) & (row * EB + i < H)
        own = jnp.where(own, dg, 0.0)
        joined = faces > 0.0
        weight[i] = jnp.where(joined, own, 0.0)
        lone = lone + jnp.where(joined, 0.0, own * z * z)
        d, s = d_n, n

    def fold(x):
        return jnp.sum(x[:, :128] + x[:, 128:256] + x[:, 256:], axis=0, keepdims=True)

    parts[...] = jnp.zeros((24, 128), F32)
    parts[16:17, :] = fold(lone)

    def step(k, older):
        now = basis.at[k - 1]
        even = jnp.zeros((8, LW), F32)
        odd = jnp.zeros((8, LW), F32)
        first = now[0]
        last = now[EB - 1]
        beyond = roll(first, -1, 0)
        c_s = roll(last, 1, 0)
        c = first
        for i in range(EB):
            if i < EB - 1:
                c_n = last if i == EB - 2 else now[i + 1]
            else:
                c_n = beyond
            image = w_e[i] * roll(c, -1, 1) + w_w[i] * roll(c, 1, 1)
            image = image + (w_n[i] * c_n + w_s[i] * c_s)
            value = 0.5 * image if older is None else image - basis[older, i]
            basis[k, i] = value
            scaled = weight[i] * c
            even = even + scaled * c
            odd = odd + scaled * value
            c_s, c = c, c_n
        parts[2 * k - 2 : 2 * k - 1, :] = fold(even)
        parts[2 * k - 1 : 2 * k, :] = fold(odd)

    step(1, None)
    row360 = rows((8, W))
    for load in loads:
        load.wait()
    for k in range(KL):
        at_n = jnp.where(row360 == 7, f_n[k : k + 1, :W], 0.0)
        at_s = jnp.where(row360 == 0, f_s[k : k + 1, :W], 0.0)
        slab_n[k] = slab_n[k] + at_n
        slab_s[k] = slab_s[k] - at_s
    for store in stores:
        store.start()
    for k in range(2, ITERS + 1):
        step(k, k - 2)

    total = jnp.sum(parts[...], axis=1, keepdims=True)
    prow = rows((24, 128))
    plane = lanes((24, 128))
    place = (prow < 16) & ((plane == prow) | (plane == 128 - prow)) | (prow == 16) & (plane == 64)
    line = jnp.sum(jnp.where(place, total, 0.0), axis=0, keepdims=True)
    sums[...] = jnp.broadcast_to(line, sums.shape)
    for store in stores:
        store.wait()


def basis_part(from_s, from_n, own_n, own_s, rhs, lev, partial, count):
    vmem = pl.BlockSpec(memory_space=pltpu.VMEM)
    hbm = pl.BlockSpec(memory_space=pltpu.HBM)
    shape = jax.ShapeDtypeStruct
    return pl.pallas_call(
        basis_kernel,
        out_shape=[
            shape((ITERS + 1, EB, 8, LW), F32),
            shape((EB, 8, LW), F32),
            shape((count, 128), F32),
            shape((KL, H, W), F32),
        ],
        in_specs=[vmem] * 6 + [hbm],
        out_specs=[vmem] * 3 + [hbm],
        input_output_aliases={6: 3},
        scratch_shapes=[pltpu.VMEM((3, EH, 128), F32)] * 2
        + [pltpu.VMEM((EB, 8, LW), F32)] * 5
        + [pltpu.VMEM((24, 128), F32)]
        + [pltpu.VMEM((KL, 8, W), F32)] * 2
        + [pltpu.SemaphoreType.DMA((4,))],
        compiler_params=pltpu.CompilerParams(vmem_limit_bytes=VMEM_LIMIT),
        name="basis",
    )(from_s, from_n, own_n, own_s, rhs, lev, partial)


def polynomials(gathered):
    sums = jnp.broadcast_to(jnp.sum(gathered, axis=0, keepdims=True), (8, 128))

    def pick(lane):
        return jnp.broadcast_to(sums[:, lane : lane + 1], (8, 128))

    moments = [pick(j) for j in range(2 * ITERS)]
    alone = pick(64)
    now = [x if j < 2 else 2.0 * x - moments[j % 2] for j, x in enumerate(moments)]
    before = [0.0] * len(now)
    one = jnp.ones((8, 128), F32)
    rest, rest_before = [one], []
    lift, lift_before = [], []
    at0, at0_before = alone, 0.0
    at1, at1_before = one, 0.0

    def coefficient(p, j):
        return p[j] if 0 <= j < len(p) else None

    def total(terms):
        terms = [x for x in terms if x is not None]
        return sum(terms[1:], terms[0]) if terms else jnp.zeros((8, 128), F32)

    def advance(p, p_before, a, b, count, constant=None):
        out = []
        for j in range(count):
            terms = [constant if j == 0 else None]
            below, above = coefficient(p, j - 1), coefficient(p, j + 1)
            if below is not None:
                terms.append(below if j == 1 else 0.5 * below)
            if above is not None:
                terms.append(0.5 * above)
            if coefficient(p, j) is not None:
                terms.append(-(a * p[j]))
            if coefficient(p_before, j) is not None:
                terms.append(-(b * p_before[j]))
            out.append(total(terms))
        return out

    def lone_part(j):
        return (at0, None, -at0, None)[j % 4]

    last_inv = last_ratio = None
    for k in range(ITERS):
        size = total([now[k], lone_part(k)])
        cross = total([now[k + 1], lone_part(k + 1)])
        inv = 1.0 / size
        ratio = cross * inv * (1.0 if k == 0 else 0.5)
        if k == 0:
            a, b = ratio, jnp.zeros((8, 128), F32)
        else:
            a, b = ratio - last_ratio, size * last_inv * (1.0 if k == 1 else 0.5)
        last_inv, last_ratio = inv, ratio
        after = [None] * len(now)
        for j in range(k + 1, 2 * ITERS - 1 - k):
            after[j] = 0.5 * (now[j - 1] + now[j + 1]) - a * now[j] - b * before[j]
        before, now = now, after
        lift, lift_before = advance(lift, lift_before, a, b, k + 1, at1), lift
        rest, rest_before = advance(rest, rest_before, a, b, k + 2), rest
        at0, at0_before = -(a * at0) - b * at0_before, at0
        at1, at1_before = (1.0 - a) * at1 - b * at1_before, at1
    scale = 1.0 / at1
    return [x * scale for x in lift], [x * scale for x in rest]


def finish_kernel(gathered, basis, diag, sea, residual, sea_t, residual_t):
    lift, rest = polynomials(gathered[...])
    for i in range(EB):
        for j in range(3):
            here = slice(128 * j, 128 * j + 128)
            c = basis[0, i, :, here]
            a, b = lift[0] * c, rest[0] * c
            for k in range(1, ITERS + 1):
                c = basis[k, i, :, here]
                b = b + rest[k] * c
                if k < ITERS:
                    a = a + lift[k] * c
            sea_t[j, pl.ds(i, 8, EB), :] = a
            residual_t[j, pl.ds(i, 8, EB), :] = diag[i, :, here] * b
    for out, by_tile in ((sea, sea_t), (residual, residual_t)):
        out[:, 0:128] = by_tile[0, :H, :]
        out[:, 128:256] = by_tile[1, :H, :]
        out[:, 256:W] = by_tile[2, :H, : W - 256]


def finish_part(gathered, basis, diag):
    vmem = pl.BlockSpec(memory_space=pltpu.VMEM)
    shape = jax.ShapeDtypeStruct
    return pl.pallas_call(
        finish_kernel,
        out_shape=[shape((H, W), F32), shape((H, W), F32)],
        in_specs=[vmem] * 3,
        out_specs=[vmem] * 2,
        scratch_shapes=[pltpu.VMEM((3, EH, 128), F32)] * 2,
        compiler_params=pltpu.CompilerParams(vmem_limit_bytes=VMEM_LIMIT),
        name="finish",
    )(gathered, basis, diag)


def edges_kernel(partial, flux_e, flux_w, dst, level, sem):
    def store(k):
        return pltpu.make_async_copy(level.at[k], dst.at[k], sem.at[k])

    lane = lanes((8, 128))
    lane_e = lanes((8, W - 256))
    for k in range(KL):
        for r in range(0, H, 8):
            here = slice(r, r + 8)
            at_w = jnp.where(lane == 0, roll(flux_w[here, :], -TR0 - k, 1), 0.0)
            at_e = roll(flux_e[here, :], W - 257 - TR0 - k, 1)[:, : W - 256]
            at_e = jnp.where(lane_e == W - 257, at_e, 0.0)
            level[k, here, :128] = partial[k, here, :128] - at_w
            level[k, here, 128:256] = partial[k, here, 128:256]
            level[k, here, 256:W] = partial[k, here, 256:W] + at_e
        store(k).start()
    for k in range(KL):
        store(k).wait()


def edges_part(partial, flux_e, flux_w):
    vmem = pl.BlockSpec(memory_space=pltpu.VMEM)
    hbm = pl.BlockSpec(memory_space=pltpu.HBM)
    return pl.pallas_call(
        edges_kernel,
        out_shape=jax.ShapeDtypeStruct((KL, H, W), F32),
        in_specs=[vmem] * 3,
        out_specs=hbm,
        scratch_shapes=[pltpu.VMEM((KL, H, W), F32), pltpu.SemaphoreType.DMA((KL,))],
        compiler_params=pltpu.CompilerParams(vmem_limit_bytes=VMEM_LIMIT),
        name="edges",
    )(partial, flux_e, flux_w)


def shards(tracer, east_velocity, north_velocity, kmt, block_mask, surface_forcing):
    nx, ny = lax.axis_size("gx"), lax.axis_size("gy")
    *fields, lev, min_e, min_in, min_n, msg_e, msg_w, out_e, out_w, row_n, row_s = outer_part(
        block_mask, kmt, surface_forcing, tracer, east_velocity, north_velocity
    )
    from_w = lax.ppermute(out_e, "gx", [(i, (i + 1) % nx) for i in range(nx)])
    from_e = lax.ppermute(out_w, "gx", [((i + 1) % nx, i) for i in range(nx)])
    partial, rhs = middle_part(*fields, lev, min_e, min_in, min_n)
    rhs_x, lev_x, msg_n, msg_s, flux_e, flux_w = sides_part(
        from_w, from_e, msg_e, msg_w, rhs, lev, row_n, row_s
    )
    from_s = lax.ppermute(msg_n, "gy", [(i, (i + 1) % ny) for i in range(ny)])
    from_n = lax.ppermute(msg_s, "gy", [((i + 1) % ny, i) for i in range(ny)])
    partial = edges_part(partial, flux_e, flux_w)
    basis, diag, sums, updated = basis_part(
        from_s, from_n, msg_n, msg_s, rhs_x, lev_x, partial, nx * ny
    )
    gathered = lax.all_to_all(sums, ("gx", "gy"), 0, 0, tiled=True)
    sea_level, residual = finish_part(gathered, basis, diag)
    return (updated, sea_level, residual)


def solution(mesh):
    in_specs = (
        P(None, "gy", "gx"),
        P(None, "gy", "gx"),
        P(None, "gy", "gx"),
        P("gy", "gx"),
        P("gy", "gx"),
        P("gy", "gx"),
    )
    out_specs = (P(None, "gy", "gx"), P("gy", "gx"), P("gy", "gx"))
    return jax.shard_map(shards, mesh=mesh, in_specs=in_specs, out_specs=out_specs, check_vma=False)
```

```python
import math

import jax
import jax.numpy as jnp
from jax import lax
from jax.experimental import pallas as pl
from jax.experimental.pallas import tpu as pltpu
from jax.sharding import PartitionSpec as P

BSX = 90
BSY = 60
KL = 12
ITERS = 8

DT_STEP = 0.2
KAPPA_H = 0.2
KAPPA_V = 0.3
SHIFT = 0.002

H = 120
W = 360
LW = 384
EH = 144

EB = EH // 8

GRAD = DT_STEP * KAPPA_H
ADV = DT_STEP * 0.5
VERT = DT_STEP * KAPPA_V
ROOT = 1.0 / math.sqrt(KL)

LEV0 = 8
TR0 = 17
VE0 = 29
C_T0 = 48
C_T1 = 56
C_V1 = 64

THIRD = H // 3
WIDTH = 42

CHUNKS = (0, 1, 3, 6, 9, 12)
EARLY = 8

R_LEV = 8
R_TR = 24
R_VE = 40

F32 = jnp.float32
VMEM_LIMIT = 40 * 1024 * 1024


def lanes(shape):
    return lax.broadcasted_iota(jnp.int32, shape, 1)


def rows(shape):
    return lax.broadcasted_iota(jnp.int32, shape, 0)


def widen(x, width):
    return jnp.concatenate([x, jnp.zeros((x.shape[0], width - x.shape[1]), x.dtype)], axis=1)


def roll(x, shift, axis):
    shift = shift % x.shape[axis]
    return x if shift == 0 else pltpu.roll(x, shift, axis)


def strided(ref, i, step):
    return jnp.concatenate([ref[j, pl.ds(i, 8, step), :] for j in range(3)], axis=1)


def put_strided(ref, i, step, value):
    for j in range(3):
        ref[j, pl.ds(i, 8, step), :] = value[:, 128 * j : 128 * j + 128]


def tiles(ref, here, value):
    for j in range(3):
        ref[j, here, :] = value[:, 128 * j : 128 * j + 128]


def thickness(level):
    return 1.0 + (0.5 / KL) * level


def strip(ref, *at):
    last = ref[(*at, slice(256, ref.shape[-1]))]
    if ref.shape[-1] < LW:
        last = widen(last, 128)
    return jnp.where(lanes((8, 128)) < 64, ref[(*at, slice(0, 128))], last)


def outer_kernel(
    mask_hbm, kmt_hbm, forcing_hbm, t_hbm, u_hbm, v_hbm,
    t_s, u_s, v_s, forcing, lev_ref, min_e, min_n, msg_e, msg_w, out_e, out_w, row_n, row_s,
    kmt, mask, t_x, u_x, lev_x, min_ex, min_nx, col, drop, sem_in, sem_2d,
):
    def load(i, k):
        src, dst = ((t_hbm, t_s), (u_hbm, u_s), (v_hbm, v_s))[i]
        here = slice(CHUNKS[k], CHUNKS[k + 1])
        return pltpu.make_async_copy(src.at[here], dst.at[here], sem_in.at[i, k])

    load_mask = pltpu.make_async_copy(mask_hbm, mask, sem_2d.at[0])
    load_kmt = pltpu.make_async_copy(kmt_hbm, kmt, sem_2d.at[1])
    load_forcing = pltpu.make_async_copy(forcing_hbm, forcing, sem_2d.at[2])
    load_mask.start()
    load_kmt.start()
    for k in range(len(CHUNKS) - 1):
        for i in range(3):
            load(i, k).start(priority=0 if k == 0 else 1)
    load_forcing.start(priority=1)

    lane = lanes((8, LW))
    row = rows((8, LW))
    load_mask.wait()
    load_kmt.wait()
    for r in range(0, H, 8):
        keep = jnp.zeros((8, LW), jnp.int32)
        for b in range(W // BSX):
            inside = (lane >= b * BSX) & (lane < (b + 1) * BSX)
            upper = jnp.where(row + r < BSY, mask[0, b], mask[1, b])
            keep = jnp.where(inside, upper, keep)
        lev = widen(kmt[r : r + 8, :], LW) * keep
        lev_ref[r : r + 8, :] = lev.astype(F32)
    for r in range(0, H, 8):
        here = slice(r, r + 8)
        lev = lev_ref[here, :]
        if r + 8 < H:
            north = lev_ref[r + 1 : r + 9, :]
        else:
            north = jnp.where(row == 7, 0.0, roll(lev, -1, 0))
        min_e[here, :] = jnp.minimum(lev, roll(lev, -1, 1))
        min_n[here, :] = jnp.minimum(lev, north)
        lev_x[here, :] = strip(lev_ref, here)
        min_ex[here, :] = strip(min_e, here)
        min_nx[here, :] = strip(min_n, here)
    row_n[...] = jnp.zeros((32, LW), F32)
    row_s[...] = jnp.zeros((16, LW), F32)

    lane = lanes((8, 128))
    row = rows((8, 128))

    def pack(levels, r, east, west):
        here = slice(r, r + 8)
        for k in levels:
            t = t_x[k, here, :]
            east = jnp.where(lane == TR0 + k, roll(t, TR0 + k - 103, 1), east)
            east = jnp.where(lane == VE0 + k, roll(u_x[k, here, :], VE0 + k - 103, 1), east)
            west = jnp.where(lane == TR0 + k, roll(t, TR0 + k, 1), west)
        return east, west

    load(0, 0).wait()
    for r in range(0, H, 8):
        t_x[0, r : r + 8, :] = strip(t_s, 0, slice(r, r + 8))
    for k in range(KL):
        if k + 1 in CHUNKS[:-1]:
            load(0, CHUNKS.index(k + 1)).wait()
        if k in CHUNKS:
            load(1, CHUNKS.index(k)).wait()
            load(2, CHUNKS.index(k)).wait()
        if k == EARLY:
            for r in range(0, H, 8):
                zero = jnp.zeros((8, 128), F32)
                msg_e[r : r + 8, :], msg_w[r : r + 8, :] = pack(range(EARLY), r, zero, zero)
        kf = float(k)
        f_low = jnp.zeros((8, 128), F32)
        t = t_x[k, 0:8, :]
        t_turned = roll(t, -1, 0)
        for r in range(0, H, 8):
            here = slice(r, r + 8)
            if r + 8 < H:
                ahead = t_x[k, r + 8 : r + 16, :]
                ahead_turned = roll(ahead, -1, 0)
                t_n = jnp.where(row == 7, ahead_turned, t_turned)
            else:
                ahead = ahead_turned = None
                t_n = t_turned
            t_e = roll(t, -1, 1)
            u = strip(u_s, k, here)
            u_x[k, here, :] = u
            f_e = (t_e - t) - (ADV / GRAD * u) * (t + t_e)
            f_n = (t_n - t) - (ADV / GRAD * strip(v_s, k, here)) * (t + t_n)
            f_e = jnp.where(min_ex[here, :] > kf, f_e, 0.0)
            f_n = jnp.where(min_nx[here, :] > kf, f_n, 0.0)
            f_w = roll(f_e, 1, 1)
            f_turned = roll(f_n, 1, 0)
            f_s = jnp.where(row == 0, f_low, f_turned)
            f_low = f_turned
            lev = lev_x[here, :]
            gain = (f_e - f_w) + (f_n - f_s)
            if k + 1 < KL:
                above = strip(t_s, k + 1, here)
                t_x[k + 1, here, :] = above
                step = jnp.where(lev > kf + 1.0, VERT / GRAD * (above - t), 0.0)
                gain = gain + step
            if k > 0:
                gain = gain - drop[here, :]
            if k + 1 < KL:
                drop[here, :] = step
            share = jnp.where(lev > kf, thickness(kf) * (t + GRAD * gain), 0.0)
            col[here, :] = share if k == 0 else col[here, :] + share
            t, t_turned = ahead, ahead_turned
        row_s[k : k + 1, :] = widen(t_s[k, 0:1, :], LW)
        row_n[k : k + 1, :] = widen(t_s[k, H - 1 : H, :], LW)
        row_n[16 + k : 17 + k, :] = widen(v_s[k, H - 1 : H, :], LW)

    load_forcing.wait()
    for r in range(0, H, 8):
        here = slice(r, r + 8)
        lev = lev_x[here, :]
        rhs = jnp.where(lev > 0.0, ROOT * col[here, :] + strip(forcing, here), 0.0)
        east, west = pack(range(EARLY, KL), r, msg_e[here, :], msg_w[here, :])
        head_e = jnp.where(lane < LEV0, roll(rhs, 32, 1), roll(lev, LEV0 - 95, 1))
        head_w = jnp.where(lane < LEV0, rhs, roll(lev, LEV0, 1))
        east = jnp.where(lane < TR0, head_e, east)
        west = jnp.where(lane < TR0, head_w, west)
        if r < 16:
            for at, src, base in ((C_T0, row_s, 0), (C_T1, row_n, 0), (C_V1, row_n, 16)):
                inside = (lane >= at) & (lane < at + 8)
                piece = src[base + r : base + r + 8, :]
                east = jnp.where(inside, roll(piece[:, 256:], at - 96, 1), east)
                west = jnp.where(inside, roll(piece[:, :128], at, 1), west)
        msg_e[here, :] = east
        msg_w[here, :] = west
    for dst, src in ((out_e, msg_e), (out_w, msg_w)):
        for r in range(0, THIRD, 8):
            value = src[r : r + 8, :]
            for i in (1, 2):
                part = roll(src[r + THIRD * i : r + THIRD * i + 8, :], WIDTH * i, 1)
                value = jnp.where(lane < WIDTH * i, value, part)
            dst[r : r + 8, :] = value
        dst[THIRD : THIRD + 16, :] = src[0:16, :]


def outer_part(mask, kmt, forcing, tracer, east, north):
    vmem = pl.BlockSpec(memory_space=pltpu.VMEM)
    hbm = pl.BlockSpec(memory_space=pltpu.HBM)
    shape = jax.ShapeDtypeStruct
    return pl.pallas_call(
        outer_kernel,
        out_shape=[shape((KL, H, W), F32)] * 3
        + [shape((H, W), F32)]
        + [shape((H, LW), F32)] * 3
        + [shape((H, 128), F32)] * 2
        + [shape((THIRD + 16, 128), F32)] * 2
        + [shape((32, LW), F32), shape((16, LW), F32)],
        in_specs=[hbm] * 6,
        out_specs=[vmem] * 13,
        scratch_shapes=[pltpu.VMEM((H, W), jnp.int32), pltpu.SMEM(mask.shape, jnp.int32)]
        + [pltpu.VMEM((KL, H, 128), F32)] * 2
        + [pltpu.VMEM((H, 128), F32)] * 5
        + [pltpu.SemaphoreType.DMA((3, len(CHUNKS) - 1)), pltpu.SemaphoreType.DMA((3,))],
        compiler_params=pltpu.CompilerParams(vmem_limit_bytes=VMEM_LIMIT),
        name="outer",
    )(*(pltpu.with_memory_space_constraint(x, pltpu.HBM) for x in (mask, kmt, forcing, tracer, east, north)))


def tracer_kernel(t_s, u_s, v_s, forcing, lev_ref, min_e, min_n, partial, rhs_ref, col, drop):
    row = rows((8, W))
    for r in range(0, H, 8):
        col[r : r + 8, :] = jnp.zeros((8, W), F32)
        drop[r : r + 8, :] = jnp.zeros((8, W), F32)

    def level(k, carry):
        kf = k.astype(F32)
        thick = thickness(kf)
        above = jnp.minimum(k + 1, KL - 1)
        f_low = jnp.zeros((8, W), F32)
        t = t_s[k, 0:8, :]
        t_turned = roll(t, -1, 0)
        for r in range(0, H, 8):
            here = slice(r, r + 8)
            if r + 8 < H:
                ahead = t_s[k, r + 8 : r + 16, :]
                ahead_turned = roll(ahead, -1, 0)
                t_n = jnp.where(row == 7, ahead_turned, t_turned)
            else:
                ahead = ahead_turned = None
                t_n = t_turned
            t_e = roll(widen(t, LW), -1, 1)[:, :W]
            f_e = (t_e - t) - (ADV / GRAD * u_s[k, here, :]) * (t + t_e)
            f_n = (t_n - t) - (ADV / GRAD * v_s[k, here, :]) * (t + t_n)
            f_e = jnp.where(min_e[here, :W] > kf, f_e, 0.0)
            f_n = jnp.where(min_n[here, :W] > kf, f_n, 0.0)
            f_w = roll(widen(f_e, LW), 1, 1)[:, :W]
            f_turned = roll(f_n, 1, 0)
            f_s = jnp.where(row == 0, f_low, f_turned)
            f_low = f_turned
            lev = lev_ref[here, :W]
            step = VERT / GRAD * (t_s[above, here, :] - t)
            step = jnp.where(lev > kf + 1.0, step, 0.0)
            gain = (f_e - f_w) + (f_n - f_s) + (step - drop[here, :])
            drop[here, :] = step
            updated = t + GRAD * gain
            partial[k, here, :] = updated
            col[here, :] += jnp.where(lev > kf, thick * updated, 0.0)
            t, t_turned = ahead, ahead_turned
        return carry

    lax.fori_loop(0, KL, level, 0)
    for r in range(0, H, 8):
        here = slice(r, r + 8)
        rhs = ROOT * col[here, :] + forcing[here, :]
        rhs_ref[here, :] = widen(jnp.where(lev_ref[here, :W] > 0.0, rhs, 0.0), LW)


def tracer_part(t_s, u_s, v_s, forcing, lev, min_e, min_n):
    vmem = pl.BlockSpec(memory_space=pltpu.VMEM)
    shape = jax.ShapeDtypeStruct
    return pl.pallas_call(
        tracer_kernel,
        out_shape=[shape((KL, H, W), F32), shape((H, LW), F32)],
        in_specs=[vmem] * 7,
        out_specs=[vmem] * 2,
        scratch_shapes=[pltpu.VMEM((H, W), F32)] * 2,
        compiler_params=pltpu.CompilerParams(vmem_limit_bytes=VMEM_LIMIT),
        name="tracer",
    )(t_s, u_s, v_s, forcing, lev, min_e, min_n)


def sides_kernel(
    sent_w, sent_e, own_e, own_w, rhs_ref, lev_ref, row_n, row_s,
    rhs_x, lev_x, msg_n, msg_s, flux_e, flux_w,
    from_w, from_e, sum_e, sum_w,
):
    for dst, src in ((from_w, sent_w), (from_e, sent_e)):
        for i in range(3):
            dst[THIRD * i : THIRD * i + THIRD, :] = roll(src[0:THIRD, :], -WIDTH * i, 1)
    from_lane = rows((128, 128))

    def spread(x, first, count, precision):
        chosen = (from_lane >= first) & (from_lane < first + count)
        return jnp.dot(
            x, jnp.where(chosen, 1.0, 0.0), precision=precision, preferred_element_type=F32
        )

    def level_at(ref, at):
        return spread(ref[...], at, 1, lax.Precision.DEFAULT)

    lane = lanes((H, 128))
    kf = (lane - TR0).astype(F32)
    inside = (lane >= TR0) & (lane < TR0 + KL)
    weight = ROOT * thickness(kf)
    lev_w = jnp.minimum(level_at(from_w, LEV0 + 8), level_at(own_w, LEV0))
    lev_e = jnp.minimum(level_at(from_e, LEV0), level_at(own_e, LEV0 + 8))
    mw, me, mine_w, mine_e = from_w[...], from_e[...], own_w[...], own_e[...]
    f_w = GRAD * (mine_w - mw) - (ADV * roll(mw, TR0 - VE0, 1)) * (mine_w + mw)
    f_e = GRAD * (me - mine_e) - (ADV * roll(mine_e, TR0 - VE0, 1)) * (me + mine_e)
    f_w = jnp.where(inside & (lev_w > kf), f_w, 0.0)
    f_e = jnp.where(inside & (lev_e > kf), f_e, 0.0)
    flux_w[...] = f_w
    flux_e[...] = f_e
    sum_w[...] = spread(weight * f_w, TR0, KL, lax.Precision.HIGHEST)
    sum_e[...] = spread(weight * f_e, TR0, KL, lax.Precision.HIGHEST)
    lane = lanes((8, 128))
    for r in range(0, H, 8):
        here = slice(r, r + 8)
        mw, me = from_w[here, :], from_e[here, :]
        c_w, c_e = sum_w[here, :], sum_e[here, :]
        rhs_x[here, :128] = rhs_ref[here, :128] - jnp.where(lane == 0, c_w, 0.0)
        rhs_x[here, 128:256] = rhs_ref[here, 128:256]
        last = rhs_ref[here, 256:]
        last = jnp.where((lane >= 104) & (lane < 112), roll(me, 104, 1), last)
        last = jnp.where(lane >= 120, roll(mw, 120, 1), last)
        last = last + jnp.where(lane == 103, c_e, 0.0) - jnp.where(lane == 104, c_e, 0.0)
        rhs_x[here, 256:] = last + jnp.where(lane == 127, c_w, 0.0)
        lev_x[here, :256] = lev_ref[here, :256]
        last = lev_ref[here, 256:]
        last = jnp.where((lane >= 104) & (lane < 113), roll(me, 104 - LEV0, 1), last)
        last = jnp.where(lane >= 119, roll(mw, 119 - LEV0, 1), last)
        lev_x[here, 256:] = last
    msg_n[0:8, :] = rhs_x[H - 8 : H, :]
    msg_s[0:8, :] = rhs_x[0:8, :]
    msg_n[R_LEV : R_LEV + 16, :] = lev_x[H - 16 : H, :]
    msg_s[R_LEV : R_LEV + 16, :] = lev_x[0:16, :]
    for dst, at, src, base, lane0 in (
        (msg_s, R_TR, row_s, 0, C_T0), (msg_n, R_TR, row_n, 0, C_T1), (msg_n, R_VE, row_n, 16, C_V1),
    ):
        for r in (0, 8):
            corner = slice(THIRD + r, THIRD + r + 8)
            mw, me = sent_w[corner, :], sent_e[corner, :]
            piece = src[base + r : base + r + 8, :]
            last = piece[:, 256:]
            last = jnp.where((lane >= 104) & (lane < 112), roll(me, 104 - lane0, 1), last)
            last = jnp.where(lane >= 120, roll(mw, 120 - lane0, 1), last)
            dst[at + r : at + r + 8, :256] = piece[:, :256]
            dst[at + r : at + r + 8, 256:] = last


def sides_part(from_w, from_e, own_e, own_w, rhs, lev, row_n, row_s):
    vmem = pl.BlockSpec(memory_space=pltpu.VMEM)
    shape = jax.ShapeDtypeStruct
    return pl.pallas_call(
        sides_kernel,
        out_shape=[
            shape((H, LW), F32),
            shape((H, LW), F32),
            shape((56, LW), F32),
            shape((40, LW), F32),
            shape((H, 128), F32),
            shape((H, 128), F32),
        ],
        in_specs=[vmem] * 8,
        out_specs=[vmem] * 6,
        scratch_shapes=[pltpu.VMEM((H, 128), F32)] * 4,
        compiler_params=pltpu.CompilerParams(vmem_limit_bytes=VMEM_LIMIT),
        name="sides",
    )(from_w, from_e, own_e, own_w, rhs, lev, row_n, row_s)


def basis_kernel(
    from_s, from_n, own_n, own_s, rhs_ref, lev_ref, partial,
    basis, diag, sums, updated,
    lev_x, rhs_x, w_e, w_w, w_n, w_s, weight, parts, slab_n, slab_s, sem,
):
    high, low = pl.ds(H - 8, 8), pl.ds(0, 8)
    loads = (
        pltpu.make_async_copy(partial.at[:, high, :], slab_n, sem.at[0]),
        pltpu.make_async_copy(partial.at[:, low, :], slab_s, sem.at[1]),
    )
    stores = (
        pltpu.make_async_copy(slab_n, updated.at[:, high, :], sem.at[2]),
        pltpu.make_async_copy(slab_s, updated.at[:, low, :], sem.at[3]),
    )
    for load in loads:
        load.start()
    lev_row = rows((16, LW))
    kf = lev_row.astype(F32)
    factor = ROOT * thickness(kf)

    def flux(t_from, t_to, vel, lev):
        value = GRAD * (t_to - t_from) - (ADV * vel) * (t_from + t_to)
        return jnp.where((lev_row < KL) & (lev > kf), value, 0.0)

    tr = slice(R_TR, R_TR + 16)
    ve = slice(R_VE, R_VE + 16)
    lev_n = jnp.minimum(lev_ref[H - 1 : H, :], from_n[R_LEV : R_LEV + 1, :])
    lev_s = jnp.minimum(lev_ref[0:1, :], from_s[R_LEV + 15 : R_LEV + 16, :])
    f_n = flux(own_n[tr, :], from_n[tr, :], own_n[ve, :], lev_n)
    f_s = flux(from_s[tr, :], own_s[tr, :], from_s[ve, :], lev_s)
    c_n = jnp.sum(factor * f_n, axis=0, keepdims=True)
    c_s = jnp.sum(factor * f_s, axis=0, keepdims=True)

    row = rows((8, LW))
    ninth = jnp.where(row == 7, from_s[R_LEV : R_LEV + 8, :], 0.0)
    ninth = jnp.where(row == 0, from_n[R_LEV + 8 : R_LEV + 16, :], ninth)
    tiles(lev_x, slice(0, H), lev_ref[...])
    tiles(lev_x, slice(H, H + 8), from_n[R_LEV : R_LEV + 8, :])
    tiles(lev_x, slice(H + 8, H + 16), ninth)
    tiles(lev_x, slice(H + 16, EH), from_s[R_LEV + 8 : R_LEV + 16, :])
    tiles(rhs_x, slice(0, 8), rhs_ref[0:8, :] - jnp.where(row == 0, c_s, 0.0))
    tiles(rhs_x, slice(8, H - 8), rhs_ref[8 : H - 8, :])
    tiles(rhs_x, slice(H - 8, H), rhs_ref[H - 8 : H, :] + jnp.where(row == 7, c_n, 0.0))
    tiles(rhs_x, slice(H, H + 8), from_n[0:8, :] - jnp.where(row == 0, c_n, 0.0))
    tiles(rhs_x, slice(H + 8, H + 16), jnp.zeros((8, LW), F32))
    tiles(rhs_x, slice(H + 16, EH), from_s[0:8, :] + jnp.where(row == 7, c_s, 0.0))

    def depth_of(i):
        lev = strided(lev_x, i, EB)
        return lev + lev * (lev - 1.0) * (0.25 / KL)

    def face(d, other):
        return jnp.where((d > 0.0) & (other > 0.0), 0.5 * (d + other), 0.0)

    lane = lanes((8, LW))
    first = depth_of(0)
    last = depth_of(EB - 1)
    beyond = roll(first, -1, 0)
    n_last = face(last, beyond)
    s = roll(n_last, 1, 0)
    lone = jnp.zeros((8, LW), F32)
    d = first
    for i in range(EB):
        if i < EB - 1:
            d_n = last if i == EB - 2 else depth_of(i + 1)
            n = face(d, d_n)
        else:
            d_n, n = beyond, n_last
        e = face(d, roll(d, -1, 1))
        w = roll(e, 1, 1)
        faces = (e + w) + (n + s)
        dg = jnp.where(d > 0.0, SHIFT * d + faces, 1.0)
        inv = 1.0 / dg
        z = strided(rhs_x, i, EB) * inv
        basis[0, i] = z
        inv = 2.0 * inv
        w_e[i] = e * inv
        w_w[i] = w * inv
        w_n[i] = n * inv
        w_s[i] = s * inv
        diag[i] = dg
        own = (lane < W) & (row * EB + i < H)
        own = jnp.where(own, dg, 0.0)
        joined = faces > 0.0
        weight[i] = jnp.where(joined, own, 0.0)
        lone = lone + jnp.where(joined, 0.0, own * z * z)
        d, s = d_n, n

    def fold(x):
        return jnp.sum(x[:, :128] + x[:, 128:256] + x[:, 256:], axis=0, keepdims=True)

    parts[...] = jnp.zeros((24, 128), F32)
    parts[16:17, :] = fold(lone)

    def step(k, older):
        now = basis.at[k - 1]
        even = jnp.zeros((8, LW), F32)
        odd = jnp.zeros((8, LW), F32)
        first = now[0]
        last = now[EB - 1]
        beyond = roll(first, -1, 0)
        c_s = roll(last, 1, 0)
        c = first
        for i in range(EB):
            if i < EB - 1:
                c_n = last if i == EB - 2 else now[i + 1]
            else:
                c_n = beyond
            image = w_e[i] * roll(c, -1, 1) + w_w[i] * roll(c, 1, 1)
            image = image + (w_n[i] * c_n + w_s[i] * c_s)
            value = 0.5 * image if older is None else image - basis[older, i]
            basis[k, i] = value
            scaled = weight[i] * c
            even = even + scaled * c
            odd = odd + scaled * value
            c_s, c = c, c_n
        parts[2 * k - 2 : 2 * k - 1, :] = fold(even)
        parts[2 * k - 1 : 2 * k, :] = fold(odd)

    step(1, None)
    row360 = rows((8, W))
    for load in loads:
        load.wait()
    for k in range(KL):
        at_n = jnp.where(row360 == 7, f_n[k : k + 1, :W], 0.0)
        at_s = jnp.where(row360 == 0, f_s[k : k + 1, :W], 0.0)
        slab_n[k] = slab_n[k] + at_n
        slab_s[k] = slab_s[k] - at_s
    for store in stores:
        store.start()
    for k in range(2, ITERS + 1):
        step(k, k - 2)

    total = jnp.sum(parts[...], axis=1, keepdims=True)
    prow = rows((24, 128))
    plane = lanes((24, 128))
    place = (prow < 16) & ((plane == prow) | (plane == 128 - prow)) | (prow == 16) & (plane == 64)
    line = jnp.sum(jnp.where(place, total, 0.0), axis=0, keepdims=True)
    sums[...] = jnp.broadcast_to(line, sums.shape)
    for store in stores:
        store.wait()


def basis_part(from_s, from_n, own_n, own_s, rhs, lev, partial, count):
    vmem = pl.BlockSpec(memory_space=pltpu.VMEM)
    hbm = pl.BlockSpec(memory_space=pltpu.HBM)
    shape = jax.ShapeDtypeStruct
    return pl.pallas_call(
        basis_kernel,
        out_shape=[
            shape((ITERS + 1, EB, 8, LW), F32),
            shape((EB, 8, LW), F32),
            shape((count, 128), F32),
            shape((KL, H, W), F32),
        ],
        in_specs=[vmem] * 6 + [hbm],
        out_specs=[vmem] * 3 + [hbm],
        input_output_aliases={6: 3},
        scratch_shapes=[pltpu.VMEM((3, EH, 128), F32)] * 2
        + [pltpu.VMEM((EB, 8, LW), F32)] * 5
        + [pltpu.VMEM((24, 128), F32)]
        + [pltpu.VMEM((KL, 8, W), F32)] * 2
        + [pltpu.SemaphoreType.DMA((4,))],
        compiler_params=pltpu.CompilerParams(vmem_limit_bytes=VMEM_LIMIT),
        name="basis",
    )(from_s, from_n, own_n, own_s, rhs, lev, partial)


def polynomials(gathered):
    sums = jnp.broadcast_to(jnp.sum(gathered, axis=0, keepdims=True), (8, 128))

    def pick(lane):
        return jnp.broadcast_to(sums[:, lane : lane + 1], (8, 128))

    moments = [pick(j) for j in range(2 * ITERS)]
    alone = pick(64)
    now = [x if j < 2 else 2.0 * x - moments[j % 2] for j, x in enumerate(moments)]
    before = [0.0] * len(now)
    one = jnp.ones((8, 128), F32)
    rest, rest_before = [one], []
    lift, lift_before = [], []
    at0, at0_before = alone, 0.0
    at1, at1_before = one, 0.0

    def coefficient(p, j):
        return p[j] if 0 <= j < len(p) else None

    def total(terms):
        terms = [x for x in terms if x is not None]
        return sum(terms[1:], terms[0]) if terms else jnp.zeros((8, 128), F32)

    def advance(p, p_before, a, b, count, constant=None):
        out = []
        for j in range(count):
            terms = [constant if j == 0 else None]
            below, above = coefficient(p, j - 1), coefficient(p, j + 1)
            if below is not None:
                terms.append(below if j == 1 else 0.5 * below)
            if above is not None:
                terms.append(0.5 * above)
            if coefficient(p, j) is not None:
                terms.append(-(a * p[j]))
            if coefficient(p_before, j) is not None:
                terms.append(-(b * p_before[j]))
            out.append(total(terms))
        return out

    def lone_part(j):
        return (at0, None, -at0, None)[j % 4]

    last_inv = last_ratio = None
    for k in range(ITERS):
        size = total([now[k], lone_part(k)])
        cross = total([now[k + 1], lone_part(k + 1)])
        inv = 1.0 / size
        ratio = cross * inv * (1.0 if k == 0 else 0.5)
        if k == 0:
            a, b = ratio, jnp.zeros((8, 128), F32)
        else:
            a, b = ratio - last_ratio, size * last_inv * (1.0 if k == 1 else 0.5)
        last_inv, last_ratio = inv, ratio
        after = [None] * len(now)
        for j in range(k + 1, 2 * ITERS - 1 - k):
            after[j] = 0.5 * (now[j - 1] + now[j + 1]) - a * now[j] - b * before[j]
        before, now = now, after
        lift, lift_before = advance(lift, lift_before, a, b, k + 1, at1), lift
        rest, rest_before = advance(rest, rest_before, a, b, k + 2), rest
        at0, at0_before = -(a * at0) - b * at0_before, at0
        at1, at1_before = (1.0 - a) * at1 - b * at1_before, at1
    scale = 1.0 / at1
    return [x * scale for x in lift], [x * scale for x in rest]


def finish_kernel(gathered, basis, diag, sea, residual, sea_t, residual_t):
    lift, rest = polynomials(gathered[...])
    for i in range(EB):
        for j in range(3):
            here = slice(128 * j, 128 * j + 128)
            c = basis[0, i, :, here]
            a, b = lift[0] * c, rest[0] * c
            for k in range(1, ITERS + 1):
                c = basis[k, i, :, here]
                b = b + rest[k] * c
                if k < ITERS:
                    a = a + lift[k] * c
            sea_t[j, pl.ds(i, 8, EB), :] = a
            residual_t[j, pl.ds(i, 8, EB), :] = diag[i, :, here] * b
    for out, by_tile in ((sea, sea_t), (residual, residual_t)):
        out[:, 0:128] = by_tile[0, :H, :]
        out[:, 128:256] = by_tile[1, :H, :]
        out[:, 256:W] = by_tile[2, :H, : W - 256]


def finish_part(gathered, basis, diag):
    vmem = pl.BlockSpec(memory_space=pltpu.VMEM)
    shape = jax.ShapeDtypeStruct
    return pl.pallas_call(
        finish_kernel,
        out_shape=[shape((H, W), F32), shape((H, W), F32)],
        in_specs=[vmem] * 3,
        out_specs=[vmem] * 2,
        scratch_shapes=[pltpu.VMEM((3, EH, 128), F32)] * 2,
        compiler_params=pltpu.CompilerParams(vmem_limit_bytes=VMEM_LIMIT),
        name="finish",
    )(gathered, basis, diag)


def edges_kernel(partial, flux_e, flux_w, dst, level, sem):
    def store(k):
        return pltpu.make_async_copy(level.at[k], dst.at[k], sem.at[k])

    lane = lanes((8, 128))
    lane_e = lanes((8, W - 256))
    for k in range(KL):
        for r in range(0, H, 8):
            here = slice(r, r + 8)
            at_w = jnp.where(lane == 0, roll(flux_w[here, :], -TR0 - k, 1), 0.0)
            at_e = roll(flux_e[here, :], W - 257 - TR0 - k, 1)[:, : W - 256]
            at_e = jnp.where(lane_e == W - 257, at_e, 0.0)
            level[k, here, :128] = partial[k, here, :128] - at_w
            level[k, here, 128:256] = partial[k, here, 128:256]
            level[k, here, 256:W] = partial[k, here, 256:W] + at_e
        store(k).start()
    for k in range(KL):
        store(k).wait()


def edges_part(partial, flux_e, flux_w):
    vmem = pl.BlockSpec(memory_space=pltpu.VMEM)
    hbm = pl.BlockSpec(memory_space=pltpu.HBM)
    return pl.pallas_call(
        edges_kernel,
        out_shape=jax.ShapeDtypeStruct((KL, H, W), F32),
        in_specs=[vmem] * 3,
        out_specs=hbm,
        scratch_shapes=[pltpu.VMEM((KL, H, W), F32), pltpu.SemaphoreType.DMA((KL,))],
        compiler_params=pltpu.CompilerParams(vmem_limit_bytes=VMEM_LIMIT),
        name="edges",
    )(partial, flux_e, flux_w)


def shards(tracer, east_velocity, north_velocity, kmt, block_mask, surface_forcing):
    nx, ny = lax.axis_size("gx"), lax.axis_size("gy")
    *fields, lev, min_e, min_n, msg_e, msg_w, out_e, out_w, row_n, row_s = outer_part(
        block_mask, kmt, surface_forcing, tracer, east_velocity, north_velocity
    )
    from_w = lax.ppermute(out_e, "gx", [(i, (i + 1) % nx) for i in range(nx)])
    from_e = lax.ppermute(out_w, "gx", [((i + 1) % nx, i) for i in range(nx)])
    partial, rhs = tracer_part(*fields, lev, min_e, min_n)
    rhs_x, lev_x, msg_n, msg_s, flux_e, flux_w = sides_part(
        from_w, from_e, msg_e, msg_w, rhs, lev, row_n, row_s
    )
    from_s = lax.ppermute(msg_n, "gy", [(i, (i + 1) % ny) for i in range(ny)])
    from_n = lax.ppermute(msg_s, "gy", [((i + 1) % ny, i) for i in range(ny)])
    partial = edges_part(partial, flux_e, flux_w)
    basis, diag, sums, updated = basis_part(
        from_s, from_n, msg_n, msg_s, rhs_x, lev_x, partial, nx * ny
    )
    gathered = lax.all_to_all(sums, ("gx", "gy"), 0, 0, tiled=True)
    sea_level, residual = finish_part(gathered, basis, diag)
    return (updated, sea_level, residual)


def solution(mesh):
    in_specs = (
        P(None, "gy", "gx"),
        P(None, "gy", "gx"),
        P(None, "gy", "gx"),
        P("gy", "gx"),
        P("gy", "gx"),
        P("gy", "gx"),
    )
    out_specs = (P(None, "gy", "gx"), P("gy", "gx"), P("gy", "gx"))
    return jax.shard_map(shards, mesh=mesh, in_specs=in_specs, out_specs=out_specs, check_vma=False)
```

```python
import math

import jax
import jax.numpy as jnp
from jax import lax
from jax.experimental import pallas as pl
from jax.experimental.pallas import tpu as pltpu
from jax.sharding import PartitionSpec as P

BSX = 90
BSY = 60
KL = 12
ITERS = 8

DT_STEP = 0.2
KAPPA_H = 0.2
KAPPA_V = 0.3
SHIFT = 0.002

H = 120
W = 360
LW = 384
EH = 144

EB = EH // 8

GRAD = DT_STEP * KAPPA_H
ADV = DT_STEP * 0.5
VERT = DT_STEP * KAPPA_V
ROOT = 1.0 / math.sqrt(KL)

LEV0 = 8
TR0 = 17
VE0 = 29
C_T0 = 48
C_T1 = 56
C_V1 = 64

THIRD = H // 3
WIDTH = 42

CHUNKS = (0, 1, 3, 6, 9, 12)
EARLY = 8

R_LEV = 8
R_TR = 16
R_NINTH = 28
R_VE = 32

F32 = jnp.float32
VMEM_LIMIT = 40 * 1024 * 1024


def lanes(shape):
    return lax.broadcasted_iota(jnp.int32, shape, 1)


def rows(shape):
    return lax.broadcasted_iota(jnp.int32, shape, 0)


def widen(x, width):
    return jnp.concatenate([x, jnp.zeros((x.shape[0], width - x.shape[1]), x.dtype)], axis=1)


def roll(x, shift, axis):
    shift = shift % x.shape[axis]
    return x if shift == 0 else pltpu.roll(x, shift, axis)


def strided(ref, i, step):
    return jnp.concatenate([ref[j, pl.ds(i, 8, step), :] for j in range(3)], axis=1)


def put_strided(ref, i, step, value):
    for j in range(3):
        ref[j, pl.ds(i, 8, step), :] = value[:, 128 * j : 128 * j + 128]


def tiles(ref, here, value):
    for j in range(3):
        ref[j, here, :] = value[:, 128 * j : 128 * j + 128]


def thickness(level):
    return 1.0 + (0.5 / KL) * level


def strip(ref, *at):
    last = ref[(*at, slice(256, ref.shape[-1]))]
    if ref.shape[-1] < LW:
        last = widen(last, 128)
    return jnp.where(lanes((8, 128)) < 64, ref[(*at, slice(0, 128))], last)


def outer_kernel(
    mask_hbm, kmt_hbm, forcing_hbm, t_hbm, u_hbm, v_hbm,
    t_s, u_s, v_s, forcing, lev_ref, min_e, min_n, msg_e, msg_w, out_e, out_w, row_n, row_s,
    kmt, mask, t_x, u_x, lev_x, min_ex, min_nx, col, drop, sem_in, sem_2d,
):
    def load(i, k):
        src, dst = ((t_hbm, t_s), (u_hbm, u_s), (v_hbm, v_s))[i]
        here = slice(CHUNKS[k], CHUNKS[k + 1])
        return pltpu.make_async_copy(src.at[here], dst.at[here], sem_in.at[i, k])

    load_mask = pltpu.make_async_copy(mask_hbm, mask, sem_2d.at[0])
    load_kmt = pltpu.make_async_copy(kmt_hbm, kmt, sem_2d.at[1])
    load_forcing = pltpu.make_async_copy(forcing_hbm, forcing, sem_2d.at[2])
    load_mask.start()
    load_kmt.start()
    for k in range(len(CHUNKS) - 1):
        for i in range(3):
            load(i, k).start(priority=0 if k == 0 else 1)
    load_forcing.start(priority=1)

    lane = lanes((8, LW))
    row = rows((8, LW))
    load_mask.wait()
    load_kmt.wait()
    for r in range(0, H, 8):
        keep = jnp.zeros((8, LW), jnp.int32)
        for b in range(W // BSX):
            inside = (lane >= b * BSX) & (lane < (b + 1) * BSX)
            upper = jnp.where(row + r < BSY, mask[0, b], mask[1, b])
            keep = jnp.where(inside, upper, keep)
        lev = widen(kmt[r : r + 8, :], LW) * keep
        lev_ref[r : r + 8, :] = lev.astype(F32)
    for r in range(0, H, 8):
        here = slice(r, r + 8)
        lev = lev_ref[here, :]
        if r + 8 < H:
            north = lev_ref[r + 1 : r + 9, :]
        else:
            north = jnp.where(row == 7, 0.0, roll(lev, -1, 0))
        min_e[here, :] = jnp.minimum(lev, roll(lev, -1, 1))
        min_n[here, :] = jnp.minimum(lev, north)
        lev_x[here, :] = strip(lev_ref, here)
        min_ex[here, :] = strip(min_e, here)
        min_nx[here, :] = strip(min_n, here)
    row_n[...] = jnp.zeros((32, LW), F32)
    row_s[...] = jnp.zeros((16, LW), F32)

    lane = lanes((8, 128))
    row = rows((8, 128))

    def pack(levels, r, east, west):
        here = slice(r, r + 8)
        for k in levels:
            t = t_x[k, here, :]
            east = jnp.where(lane == TR0 + k, roll(t, TR0 + k - 103, 1), east)
            east = jnp.where(lane == VE0 + k, roll(u_x[k, here, :], VE0 + k - 103, 1), east)
            west = jnp.where(lane == TR0 + k, roll(t, TR0 + k, 1), west)
        return east, west

    load(0, 0).wait()
    for r in range(0, H, 8):
        t_x[0, r : r + 8, :] = strip(t_s, 0, slice(r, r + 8))
    for k in range(KL):
        if k + 1 in CHUNKS[:-1]:
            load(0, CHUNKS.index(k + 1)).wait()
        if k in CHUNKS:
            load(1, CHUNKS.index(k)).wait()
            load(2, CHUNKS.index(k)).wait()
        if k == EARLY:
            for r in range(0, H, 8):
                zero = jnp.zeros((8, 128), F32)
                msg_e[r : r + 8, :], msg_w[r : r + 8, :] = pack(range(EARLY), r, zero, zero)
        kf = float(k)
        f_low = jnp.zeros((8, 128), F32)
        t = t_x[k, 0:8, :]
        t_turned = roll(t, -1, 0)
        for r in range(0, H, 8):
            here = slice(r, r + 8)
            if r + 8 < H:
                ahead = t_x[k, r + 8 : r + 16, :]
                ahead_turned = roll(ahead, -1, 0)
                t_n = jnp.where(row == 7, ahead_turned, t_turned)
            else:
                ahead = ahead_turned = None
                t_n = t_turned
            t_e = roll(t, -1, 1)
            u = strip(u_s, k, here)
            u_x[k, here, :] = u
            f_e = (t_e - t) - (ADV / GRAD * u) * (t + t_e)
            f_n = (t_n - t) - (ADV / GRAD * strip(v_s, k, here)) * (t + t_n)
            f_e = jnp.where(min_ex[here, :] > kf, f_e, 0.0)
            f_n = jnp.where(min_nx[here, :] > kf, f_n, 0.0)
            f_w = roll(f_e, 1, 1)
            f_turned = roll(f_n, 1, 0)
            f_s = jnp.where(row == 0, f_low, f_turned)
            f_low = f_turned
            lev = lev_x[here, :]
            gain = (f_e - f_w) + (f_n - f_s)
            if k + 1 < KL:
                above = strip(t_s, k + 1, here)
                t_x[k + 1, here, :] = above
                step = jnp.where(lev > kf + 1.0, VERT / GRAD * (above - t), 0.0)
                gain = gain + step
            if k > 0:
                gain = gain - drop[here, :]
            if k + 1 < KL:
                drop[here, :] = step
            share = jnp.where(lev > kf, thickness(kf) * (t + GRAD * gain), 0.0)
            col[here, :] = share if k == 0 else col[here, :] + share
            t, t_turned = ahead, ahead_turned
        row_s[k : k + 1, :] = widen(t_s[k, 0:1, :], LW)
        row_n[k : k + 1, :] = widen(t_s[k, H - 1 : H, :], LW)
        row_n[16 + k : 17 + k, :] = widen(v_s[k, H - 1 : H, :], LW)

    load_forcing.wait()
    for r in range(0, H, 8):
        here = slice(r, r + 8)
        lev = lev_x[here, :]
        rhs = jnp.where(lev > 0.0, ROOT * col[here, :] + strip(forcing, here), 0.0)
        east, west = pack(range(EARLY, KL), r, msg_e[here, :], msg_w[here, :])
        head_e = jnp.where(lane < LEV0, roll(rhs, 32, 1), roll(lev, LEV0 - 95, 1))
        head_w = jnp.where(lane < LEV0, rhs, roll(lev, LEV0, 1))
        east = jnp.where(lane < TR0, head_e, east)
        west = jnp.where(lane < TR0, head_w, west)
        if r < 16:
            for at, src, base in ((C_T0, row_s, 0), (C_T1, row_n, 0), (C_V1, row_n, 16)):
                inside = (lane >= at) & (lane < at + 8)
                piece = src[base + r : base + r + 8, :]
                east = jnp.where(inside, roll(piece[:, 256:], at - 96, 1), east)
                west = jnp.where(inside, roll(piece[:, :128], at, 1), west)
        msg_e[here, :] = east
        msg_w[here, :] = west
    for dst, src in ((out_e, msg_e), (out_w, msg_w)):
        for r in range(0, THIRD, 8):
            value = src[r : r + 8, :]
            for i in (1, 2):
                part = roll(src[r + THIRD * i : r + THIRD * i + 8, :], WIDTH * i, 1)
                value = jnp.where(lane < WIDTH * i, value, part)
            dst[r : r + 8, :] = value
        dst[THIRD : THIRD + 16, :] = src[0:16, :]


def outer_part(mask, kmt, forcing, tracer, east, north):
    vmem = pl.BlockSpec(memory_space=pltpu.VMEM)
    hbm = pl.BlockSpec(memory_space=pltpu.HBM)
    shape = jax.ShapeDtypeStruct
    return pl.pallas_call(
        outer_kernel,
        out_shape=[shape((KL, H, W), F32)] * 3
        + [shape((H, W), F32)]
        + [shape((H, LW), F32)] * 3
        + [shape((H, 128), F32)] * 2
        + [shape((THIRD + 16, 128), F32)] * 2
        + [shape((32, LW), F32), shape((16, LW), F32)],
        in_specs=[hbm] * 6,
        out_specs=[vmem] * 13,
        scratch_shapes=[pltpu.VMEM((H, W), jnp.int32), pltpu.SMEM(mask.shape, jnp.int32)]
        + [pltpu.VMEM((KL, H, 128), F32)] * 2
        + [pltpu.VMEM((H, 128), F32)] * 5
        + [pltpu.SemaphoreType.DMA((3, len(CHUNKS) - 1)), pltpu.SemaphoreType.DMA((3,))],
        compiler_params=pltpu.CompilerParams(vmem_limit_bytes=VMEM_LIMIT),
        name="outer",
    )(*(pltpu.with_memory_space_constraint(x, pltpu.HBM) for x in (mask, kmt, forcing, tracer, east, north)))


def tracer_kernel(t_s, u_s, v_s, forcing, lev_ref, min_e, min_n, partial, rhs_ref, col, drop):
    row = rows((8, W))
    for r in range(0, H, 8):
        col[r : r + 8, :] = jnp.zeros((8, W), F32)
        drop[r : r + 8, :] = jnp.zeros((8, W), F32)

    def level(k, carry):
        kf = k.astype(F32)
        thick = thickness(kf)
        above = jnp.minimum(k + 1, KL - 1)
        f_low = jnp.zeros((8, W), F32)
        t = t_s[k, 0:8, :]
        t_turned = roll(t, -1, 0)
        for r in range(0, H, 8):
            here = slice(r, r + 8)
            if r + 8 < H:
                ahead = t_s[k, r + 8 : r + 16, :]
                ahead_turned = roll(ahead, -1, 0)
                t_n = jnp.where(row == 7, ahead_turned, t_turned)
            else:
                ahead = ahead_turned = None
                t_n = t_turned
            t_e = roll(widen(t, LW), -1, 1)[:, :W]
            f_e = (t_e - t) - (ADV / GRAD * u_s[k, here, :]) * (t + t_e)
            f_n = (t_n - t) - (ADV / GRAD * v_s[k, here, :]) * (t + t_n)
            f_e = jnp.where(min_e[here, :W] > kf, f_e, 0.0)
            f_n = jnp.where(min_n[here, :W] > kf, f_n, 0.0)
            f_w = roll(widen(f_e, LW), 1, 1)[:, :W]
            f_turned = roll(f_n, 1, 0)
            f_s = jnp.where(row == 0, f_low, f_turned)
            f_low = f_turned
            lev = lev_ref[here, :W]
            step = VERT / GRAD * (t_s[above, here, :] - t)
            step = jnp.where(lev > kf + 1.0, step, 0.0)
            gain = (f_e - f_w) + (f_n - f_s) + (step - drop[here, :])
            drop[here, :] = step
            updated = t + GRAD * gain
            partial[k, here, :] = updated
            col[here, :] += jnp.where(lev > kf, thick * updated, 0.0)
            t, t_turned = ahead, ahead_turned
        return carry

    lax.fori_loop(0, KL, level, 0)
    for r in range(0, H, 8):
        here = slice(r, r + 8)
        rhs = ROOT * col[here, :] + forcing[here, :]
        rhs_ref[here, :] = widen(jnp.where(lev_ref[here, :W] > 0.0, rhs, 0.0), LW)


def tracer_part(t_s, u_s, v_s, forcing, lev, min_e, min_n):
    vmem = pl.BlockSpec(memory_space=pltpu.VMEM)
    shape = jax.ShapeDtypeStruct
    return pl.pallas_call(
        tracer_kernel,
        out_shape=[shape((KL, H, W), F32), shape((H, LW), F32)],
        in_specs=[vmem] * 7,
        out_specs=[vmem] * 2,
        scratch_shapes=[pltpu.VMEM((H, W), F32)] * 2,
        compiler_params=pltpu.CompilerParams(vmem_limit_bytes=VMEM_LIMIT),
        name="tracer",
    )(t_s, u_s, v_s, forcing, lev, min_e, min_n)


def sides_kernel(
    sent_w, sent_e, own_e, own_w, rhs_ref, lev_ref, row_n, row_s,
    rhs_x, lev_x, msg_n, msg_s, flux_e, flux_w,
    from_w, from_e, sum_e, sum_w,
):
    for dst, src in ((from_w, sent_w), (from_e, sent_e)):
        for i in range(3):
            dst[THIRD * i : THIRD * i + THIRD, :] = roll(src[0:THIRD, :], -WIDTH * i, 1)
    from_lane = rows((128, 128))

    def spread(x, first, count, precision):
        chosen = (from_lane >= first) & (from_lane < first + count)
        return jnp.dot(
            x, jnp.where(chosen, 1.0, 0.0), precision=precision, preferred_element_type=F32
        )

    def level_at(ref, at):
        return spread(ref[...], at, 1, lax.Precision.DEFAULT)

    lane = lanes((H, 128))
    kf = (lane - TR0).astype(F32)
    inside = (lane >= TR0) & (lane < TR0 + KL)
    weight = ROOT * thickness(kf)
    lev_w = jnp.minimum(level_at(from_w, LEV0 + 8), level_at(own_w, LEV0))
    lev_e = jnp.minimum(level_at(from_e, LEV0), level_at(own_e, LEV0 + 8))
    mw, me, mine_w, mine_e = from_w[...], from_e[...], own_w[...], own_e[...]
    f_w = GRAD * (mine_w - mw) - (ADV * roll(mw, TR0 - VE0, 1)) * (mine_w + mw)
    f_e = GRAD * (me - mine_e) - (ADV * roll(mine_e, TR0 - VE0, 1)) * (me + mine_e)
    f_w = jnp.where(inside & (lev_w > kf), f_w, 0.0)
    f_e = jnp.where(inside & (lev_e > kf), f_e, 0.0)
    flux_w[...] = f_w
    flux_e[...] = f_e
    sum_w[...] = spread(weight * f_w, TR0, KL, lax.Precision.HIGHEST)
    sum_e[...] = spread(weight * f_e, TR0, KL, lax.Precision.HIGHEST)
    lane = lanes((8, 128))
    for r in range(0, H, 8):
        here = slice(r, r + 8)
        mw, me = from_w[here, :], from_e[here, :]
        c_w, c_e = sum_w[here, :], sum_e[here, :]
        rhs_x[here, :128] = rhs_ref[here, :128] - jnp.where(lane == 0, c_w, 0.0)
        rhs_x[here, 128:256] = rhs_ref[here, 128:256]
        last = rhs_ref[here, 256:]
        last = jnp.where((lane >= 104) & (lane < 112), roll(me, 104, 1), last)
        last = jnp.where(lane >= 120, roll(mw, 120, 1), last)
        last = last + jnp.where(lane == 103, c_e, 0.0) - jnp.where(lane == 104, c_e, 0.0)
        rhs_x[here, 256:] = last + jnp.where(lane == 127, c_w, 0.0)
        lev_x[here, :256] = lev_ref[here, :256]
        last = lev_ref[here, 256:]
        last = jnp.where((lane >= 104) & (lane < 113), roll(me, 104 - LEV0, 1), last)
        last = jnp.where(lane >= 119, roll(mw, 119 - LEV0, 1), last)
        lev_x[here, 256:] = last
    msg_n[0:8, :] = rhs_x[H - 8 : H, :]
    msg_s[0:8, :] = rhs_x[0:8, :]
    msg_n[R_LEV : R_LEV + 8, :] = lev_x[H - 8 : H, :]
    msg_s[R_LEV : R_LEV + 8, :] = lev_x[0:8, :]
    for dst, at, src, base, lane0 in (
        (msg_s, R_TR, row_s, 0, C_T0), (msg_n, R_TR, row_n, 0, C_T1), (msg_n, R_VE, row_n, 16, C_V1),
    ):
        for r in (0, 8):
            corner = slice(THIRD + r, THIRD + r + 8)
            mw, me = sent_w[corner, :], sent_e[corner, :]
            piece = src[base + r : base + r + 8, :]
            last = piece[:, 256:]
            last = jnp.where((lane >= 104) & (lane < 112), roll(me, 104 - lane0, 1), last)
            last = jnp.where(lane >= 120, roll(mw, 120 - lane0, 1), last)
            dst[at + r : at + r + 8, :256] = piece[:, :256]
            dst[at + r : at + r + 8, 256:] = last
    msg_n[R_NINTH : R_NINTH + 1, :] = lev_x[H - 9 : H - 8, :]
    msg_s[R_NINTH : R_NINTH + 1, :] = lev_x[8:9, :]


def sides_part(from_w, from_e, own_e, own_w, rhs, lev, row_n, row_s):
    vmem = pl.BlockSpec(memory_space=pltpu.VMEM)
    shape = jax.ShapeDtypeStruct
    return pl.pallas_call(
        sides_kernel,
        out_shape=[
            shape((H, LW), F32),
            shape((H, LW), F32),
            shape((48, LW), F32),
            shape((32, LW), F32),
            shape((H, 128), F32),
            shape((H, 128), F32),
        ],
        in_specs=[vmem] * 8,
        out_specs=[vmem] * 6,
        scratch_shapes=[pltpu.VMEM((H, 128), F32)] * 4,
        compiler_params=pltpu.CompilerParams(vmem_limit_bytes=VMEM_LIMIT),
        name="sides",
    )(from_w, from_e, own_e, own_w, rhs, lev, row_n, row_s)


def basis_kernel(
    from_s, from_n, own_n, own_s, rhs_ref, lev_ref, partial,
    basis, diag, sums, updated,
    lev_x, rhs_x, w_e, w_w, w_n, w_s, weight, parts, slab_n, slab_s, sem,
):
    high, low = pl.ds(H - 8, 8), pl.ds(0, 8)
    loads = (
        pltpu.make_async_copy(partial.at[:, high, :], slab_n, sem.at[0]),
        pltpu.make_async_copy(partial.at[:, low, :], slab_s, sem.at[1]),
    )
    stores = (
        pltpu.make_async_copy(slab_n, updated.at[:, high, :], sem.at[2]),
        pltpu.make_async_copy(slab_s, updated.at[:, low, :], sem.at[3]),
    )
    for load in loads:
        load.start()
    lev_row = rows((16, LW))
    kf = lev_row.astype(F32)
    factor = ROOT * thickness(kf)

    def flux(t_from, t_to, vel, lev):
        value = GRAD * (t_to - t_from) - (ADV * vel) * (t_from + t_to)
        return jnp.where((lev_row < KL) & (lev > kf), value, 0.0)

    tr = slice(R_TR, R_TR + 16)
    ve = slice(R_VE, R_VE + 16)
    lev_n = jnp.minimum(lev_ref[H - 1 : H, :], from_n[R_LEV : R_LEV + 1, :])
    lev_s = jnp.minimum(lev_ref[0:1, :], from_s[R_LEV + 7 : R_LEV + 8, :])
    f_n = flux(own_n[tr, :], from_n[tr, :], own_n[ve, :], lev_n)
    f_s = flux(from_s[tr, :], own_s[tr, :], from_s[ve, :], lev_s)
    c_n = jnp.sum(factor * f_n, axis=0, keepdims=True)
    c_s = jnp.sum(factor * f_s, axis=0, keepdims=True)

    row = rows((8, LW))
    ninth = jnp.where(row == 7, from_s[R_NINTH : R_NINTH + 1, :], 0.0)
    ninth = jnp.where(row == 0, from_n[R_NINTH : R_NINTH + 1, :], ninth)
    tiles(lev_x, slice(0, H), lev_ref[...])
    tiles(lev_x, slice(H, H + 8), from_n[R_LEV : R_LEV + 8, :])
    tiles(lev_x, slice(H + 8, H + 16), ninth)
    tiles(lev_x, slice(H + 16, EH), from_s[R_LEV : R_LEV + 8, :])
    tiles(rhs_x, slice(0, 8), rhs_ref[0:8, :] - jnp.where(row == 0, c_s, 0.0))
    tiles(rhs_x, slice(8, H - 8), rhs_ref[8 : H - 8, :])
    tiles(rhs_x, slice(H - 8, H), rhs_ref[H - 8 : H, :] + jnp.where(row == 7, c_n, 0.0))
    tiles(rhs_x, slice(H, H + 8), from_n[0:8, :] - jnp.where(row == 0, c_n, 0.0))
    tiles(rhs_x, slice(H + 8, H + 16), jnp.zeros((8, LW), F32))
    tiles(rhs_x, slice(H + 16, EH), from_s[0:8, :] + jnp.where(row == 7, c_s, 0.0))

    def depth_of(i):
        lev = strided(lev_x, i, EB)
        return lev + lev * (lev - 1.0) * (0.25 / KL)

    def face(d, other):
        return jnp.where((d > 0.0) & (other > 0.0), 0.5 * (d + other), 0.0)

    lane = lanes((8, LW))
    first = depth_of(0)
    last = depth_of(EB - 1)
    beyond = roll(first, -1, 0)
    n_last = face(last, beyond)
    s = roll(n_last, 1, 0)
    lone = jnp.zeros((8, LW), F32)
    d = first
    for i in range(EB):
        if i < EB - 1:
            d_n = last if i == EB - 2 else depth_of(i + 1)
            n = face(d, d_n)
        else:
            d_n, n = beyond, n_last
        e = face(d, roll(d, -1, 1))
        w = roll(e, 1, 1)
        faces = (e + w) + (n + s)
        dg = jnp.where(d > 0.0, SHIFT * d + faces, 1.0)
        inv = 1.0 / dg
        z = strided(rhs_x, i, EB) * inv
        basis[0, i] = z
        inv = 2.0 * inv
        w_e[i] = e * inv
        w_w[i] = w * inv
        w_n[i] = n * inv
        w_s[i] = s * inv
        diag[i] = dg
        own = (lane < W) & (row * EB + i < H)
        own = jnp.where(own, dg, 0.0)
        joined = faces > 0.0
        weight[i] = jnp.where(joined, own, 0.0)
        lone = lone + jnp.where(joined, 0.0, own * z * z)
        d, s = d_n, n

    def fold(x):
        return jnp.sum(x[:, :128] + x[:, 128:256] + x[:, 256:], axis=0, keepdims=True)

    parts[...] = jnp.zeros((24, 128), F32)
    parts[16:17, :] = fold(lone)

    def step(k, older):
        now = basis.at[k - 1]
        even = jnp.zeros((8, LW), F32)
        odd = jnp.zeros((8, LW), F32)
        first = now[0]
        last = now[EB - 1]
        beyond = roll(first, -1, 0)
        c_s = roll(last, 1, 0)
        c = first
        for i in range(EB):
            if i < EB - 1:
                c_n = last if i == EB - 2 else now[i + 1]
            else:
                c_n = beyond
            image = w_e[i] * roll(c, -1, 1) + w_w[i] * roll(c, 1, 1)
            image = image + (w_n[i] * c_n + w_s[i] * c_s)
            value = 0.5 * image if older is None else image - basis[older, i]
            basis[k, i] = value
            scaled = weight[i] * c
            even = even + scaled * c
            odd = odd + scaled * value
            c_s, c = c, c_n
        parts[2 * k - 2 : 2 * k - 1, :] = fold(even)
        parts[2 * k - 1 : 2 * k, :] = fold(odd)

    step(1, None)
    row360 = rows((8, W))
    for load in loads:
        load.wait()
    for k in range(KL):
        at_n = jnp.where(row360 == 7, f_n[k : k + 1, :W], 0.0)
        at_s = jnp.where(row360 == 0, f_s[k : k + 1, :W], 0.0)
        slab_n[k] = slab_n[k] + at_n
        slab_s[k] = slab_s[k] - at_s
    for store in stores:
        store.start()
    for k in range(2, ITERS + 1):
        step(k, k - 2)

    total = jnp.sum(parts[...], axis=1, keepdims=True)
    prow = rows((24, 128))
    plane = lanes((24, 128))
    place = (prow < 16) & ((plane == prow) | (plane == 128 - prow)) | (prow == 16) & (plane == 64)
    line = jnp.sum(jnp.where(place, total, 0.0), axis=0, keepdims=True)
    sums[...] = jnp.broadcast_to(line, sums.shape)
    for store in stores:
        store.wait()


def basis_part(from_s, from_n, own_n, own_s, rhs, lev, partial, count):
    vmem = pl.BlockSpec(memory_space=pltpu.VMEM)
    hbm = pl.BlockSpec(memory_space=pltpu.HBM)
    shape = jax.ShapeDtypeStruct
    return pl.pallas_call(
        basis_kernel,
        out_shape=[
            shape((ITERS + 1, EB, 8, LW), F32),
            shape((EB, 8, LW), F32),
            shape((count, 128), F32),
            shape((KL, H, W), F32),
        ],
        in_specs=[vmem] * 6 + [hbm],
        out_specs=[vmem] * 3 + [hbm],
        input_output_aliases={6: 3},
        scratch_shapes=[pltpu.VMEM((3, EH, 128), F32)] * 2
        + [pltpu.VMEM((EB, 8, LW), F32)] * 5
        + [pltpu.VMEM((24, 128), F32)]
        + [pltpu.VMEM((KL, 8, W), F32)] * 2
        + [pltpu.SemaphoreType.DMA((4,))],
        compiler_params=pltpu.CompilerParams(vmem_limit_bytes=VMEM_LIMIT),
        name="basis",
    )(from_s, from_n, own_n, own_s, rhs, lev, partial)


def polynomials(gathered):
    sums = jnp.broadcast_to(jnp.sum(gathered, axis=0, keepdims=True), (8, 128))

    def pick(lane):
        return jnp.broadcast_to(sums[:, lane : lane + 1], (8, 128))

    moments = [pick(j) for j in range(2 * ITERS)]
    alone = pick(64)
    now = [x if j < 2 else 2.0 * x - moments[j % 2] for j, x in enumerate(moments)]
    before = [0.0] * len(now)
    one = jnp.ones((8, 128), F32)
    rest, rest_before = [one], []
    lift, lift_before = [], []
    at0, at0_before = alone, 0.0
    at1, at1_before = one, 0.0

    def coefficient(p, j):
        return p[j] if 0 <= j < len(p) else None

    def total(terms):
        terms = [x for x in terms if x is not None]
        return sum(terms[1:], terms[0]) if terms else jnp.zeros((8, 128), F32)

    def advance(p, p_before, a, b, count, constant=None):
        out = []
        for j in range(count):
            terms = [constant if j == 0 else None]
            below, above = coefficient(p, j - 1), coefficient(p, j + 1)
            if below is not None:
                terms.append(below if j == 1 else 0.5 * below)
            if above is not None:
                terms.append(0.5 * above)
            if coefficient(p, j) is not None:
                terms.append(-(a * p[j]))
            if coefficient(p_before, j) is not None:
                terms.append(-(b * p_before[j]))
            out.append(total(terms))
        return out

    def lone_part(j):
        return (at0, None, -at0, None)[j % 4]

    last_inv = last_ratio = None
    for k in range(ITERS):
        size = total([now[k], lone_part(k)])
        cross = total([now[k + 1], lone_part(k + 1)])
        inv = jnp.where(size == 0.0, 0.0, 1.0 / size)
        ratio = cross * inv * (1.0 if k == 0 else 0.5)
        if k == 0:
            a, b = ratio, jnp.zeros((8, 128), F32)
        else:
            a, b = ratio - last_ratio, size * last_inv * (1.0 if k == 1 else 0.5)
        last_inv, last_ratio = inv, ratio
        after = [None] * len(now)
        for j in range(k + 1, 2 * ITERS - 1 - k):
            after[j] = 0.5 * (now[j - 1] + now[j + 1]) - a * now[j] - b * before[j]
        before, now = now, after
        lift, lift_before = advance(lift, lift_before, a, b, k + 1, at1), lift
        rest, rest_before = advance(rest, rest_before, a, b, k + 2), rest
        at0, at0_before = -(a * at0) - b * at0_before, at0
        at1, at1_before = (1.0 - a) * at1 - b * at1_before, at1
    scale = 1.0 / at1
    return [x * scale for x in lift], [x * scale for x in rest]


def finish_kernel(gathered, basis, diag, sea, residual, sea_t, residual_t):
    lift, rest = polynomials(gathered[...])
    for i in range(EB):
        for j in range(3):
            here = slice(128 * j, 128 * j + 128)
            c = basis[0, i, :, here]
            a, b = lift[0] * c, rest[0] * c
            for k in range(1, ITERS + 1):
                c = basis[k, i, :, here]
                b = b + rest[k] * c
                if k < ITERS:
                    a = a + lift[k] * c
            sea_t[j, pl.ds(i, 8, EB), :] = a
            residual_t[j, pl.ds(i, 8, EB), :] = diag[i, :, here] * b
    for out, by_tile in ((sea, sea_t), (residual, residual_t)):
        out[:, 0:128] = by_tile[0, :H, :]
        out[:, 128:256] = by_tile[1, :H, :]
        out[:, 256:W] = by_tile[2, :H, : W - 256]


def finish_part(gathered, basis, diag):
    vmem = pl.BlockSpec(memory_space=pltpu.VMEM)
    shape = jax.ShapeDtypeStruct
    return pl.pallas_call(
        finish_kernel,
        out_shape=[shape((H, W), F32), shape((H, W), F32)],
        in_specs=[vmem] * 3,
        out_specs=[vmem] * 2,
        scratch_shapes=[pltpu.VMEM((3, EH, 128), F32)] * 2,
        compiler_params=pltpu.CompilerParams(vmem_limit_bytes=VMEM_LIMIT),
        name="finish",
    )(gathered, basis, diag)


def edges_kernel(partial, flux_e, flux_w, dst, level, sem):
    def store(k):
        return pltpu.make_async_copy(level.at[k], dst.at[k], sem.at[k])

    lane = lanes((8, 128))
    lane_e = lanes((8, W - 256))
    for k in range(KL):
        for r in range(0, H, 8):
            here = slice(r, r + 8)
            at_w = jnp.where(lane == 0, roll(flux_w[here, :], -TR0 - k, 1), 0.0)
            at_e = roll(flux_e[here, :], W - 257 - TR0 - k, 1)[:, : W - 256]
            at_e = jnp.where(lane_e == W - 257, at_e, 0.0)
            level[k, here, :128] = partial[k, here, :128] - at_w
            level[k, here, 128:256] = partial[k, here, 128:256]
            level[k, here, 256:W] = partial[k, here, 256:W] + at_e
        store(k).start()
    for k in range(KL):
        store(k).wait()


def edges_part(partial, flux_e, flux_w):
    vmem = pl.BlockSpec(memory_space=pltpu.VMEM)
    hbm = pl.BlockSpec(memory_space=pltpu.HBM)
    return pl.pallas_call(
        edges_kernel,
        out_shape=jax.ShapeDtypeStruct((KL, H, W), F32),
        in_specs=[vmem] * 3,
        out_specs=hbm,
        scratch_shapes=[pltpu.VMEM((KL, H, W), F32), pltpu.SemaphoreType.DMA((KL,))],
        compiler_params=pltpu.CompilerParams(vmem_limit_bytes=VMEM_LIMIT),
        name="edges",
    )(partial, flux_e, flux_w)


def shards(tracer, east_velocity, north_velocity, kmt, block_mask, surface_forcing):
    nx, ny = lax.axis_size("gx"), lax.axis_size("gy")
    *fields, lev, min_e, min_n, msg_e, msg_w, out_e, out_w, row_n, row_s = outer_part(
        block_mask, kmt, surface_forcing, tracer, east_velocity, north_velocity
    )
    from_w = lax.ppermute(out_e, "gx", [(i, (i + 1) % nx) for i in range(nx)])
    from_e = lax.ppermute(out_w, "gx", [((i + 1) % nx, i) for i in range(nx)])
    partial, rhs = tracer_part(*fields, lev, min_e, min_n)
    rhs_x, lev_x, msg_n, msg_s, flux_e, flux_w = sides_part(
        from_w, from_e, msg_e, msg_w, rhs, lev, row_n, row_s
    )
    from_s = lax.ppermute(msg_n, "gy", [(i, (i + 1) % ny) for i in range(ny)])
    from_n = lax.ppermute(msg_s, "gy", [((i + 1) % ny, i) for i in range(ny)])
    partial = edges_part(partial, flux_e, flux_w)
    basis, diag, sums, updated = basis_part(
        from_s, from_n, msg_n, msg_s, rhs_x, lev_x, partial, nx * ny
    )
    gathered = lax.all_to_all(sums, ("gx", "gy"), 0, 0, tiled=True)
    sea_level, residual = finish_part(gathered, basis, diag)
    return (updated, sea_level, residual)


def solution(mesh):
    in_specs = (
        P(None, "gy", "gx"),
        P(None, "gy", "gx"),
        P(None, "gy", "gx"),
        P("gy", "gx"),
        P("gy", "gx"),
        P("gy", "gx"),
    )
    out_specs = (P(None, "gy", "gx"), P("gy", "gx"), P("gy", "gx"))
    return jax.shard_map(shards, mesh=mesh, in_specs=in_specs, out_specs=out_specs, check_vma=False)
```

```python
import math

import jax
import jax.numpy as jnp
from jax import lax
from jax.experimental import pallas as pl
from jax.experimental.pallas import tpu as pltpu
from jax.sharding import PartitionSpec as P

BSX = 90
BSY = 60
KL = 12
ITERS = 8

DT_STEP = 0.2
KAPPA_H = 0.2
KAPPA_V = 0.3
SHIFT = 0.002

H = 120
W = 360
LW = 384
EH = 144

EB = EH // 8

GRAD = DT_STEP * KAPPA_H
ADV = DT_STEP * 0.5
VERT = DT_STEP * KAPPA_V
ROOT = 1.0 / math.sqrt(KL)

LEV0 = 8
TR0 = 17
VE0 = 29
C_T0 = 48
C_T1 = 56
C_V1 = 64

THIRD = H // 3
WIDTH = 42

CHUNKS = (0, 1, 3, 6, 9, 12)
EARLY = 8

R_LEV = 8
R_TR = 16
R_NINTH = 28
R_VE = 32

F32 = jnp.float32
VMEM_LIMIT = 40 * 1024 * 1024


def lanes(shape):
    return lax.broadcasted_iota(jnp.int32, shape, 1)


def rows(shape):
    return lax.broadcasted_iota(jnp.int32, shape, 0)


def widen(x, width):
    return jnp.concatenate([x, jnp.zeros((x.shape[0], width - x.shape[1]), x.dtype)], axis=1)


def roll(x, shift, axis):
    shift = shift % x.shape[axis]
    return x if shift == 0 else pltpu.roll(x, shift, axis)


def strided(ref, i, step):
    return jnp.concatenate([ref[j, pl.ds(i, 8, step), :] for j in range(3)], axis=1)


def put_strided(ref, i, step, value):
    for j in range(3):
        ref[j, pl.ds(i, 8, step), :] = value[:, 128 * j : 128 * j + 128]


def tiles(ref, here, value):
    for j in range(3):
        ref[j, here, :] = value[:, 128 * j : 128 * j + 128]


def thickness(level):
    return 1.0 + (0.5 / KL) * level


def strip(ref, *at):
    last = ref[(*at, slice(256, ref.shape[-1]))]
    if ref.shape[-1] < LW:
        last = widen(last, 128)
    return jnp.where(lanes((8, 128)) < 64, ref[(*at, slice(0, 128))], last)


def outer_kernel(
    mask_hbm, kmt_hbm, forcing_hbm, t_hbm, u_hbm, v_hbm,
    t_s, u_s, v_s, forcing, lev_ref, min_e, min_n, msg_e, msg_w, out_e, out_w, row_n, row_s,
    kmt, mask, t_x, u_x, lev_x, min_ex, min_nx, col, drop, sem_in, sem_2d,
):
    def load(i, k):
        src, dst = ((t_hbm, t_s), (u_hbm, u_s), (v_hbm, v_s))[i]
        here = slice(CHUNKS[k], CHUNKS[k + 1])
        return pltpu.make_async_copy(src.at[here], dst.at[here], sem_in.at[i, k])

    load_mask = pltpu.make_async_copy(mask_hbm, mask, sem_2d.at[0])
    load_kmt = pltpu.make_async_copy(kmt_hbm, kmt, sem_2d.at[1])
    load_forcing = pltpu.make_async_copy(forcing_hbm, forcing, sem_2d.at[2])
    load_mask.start()
    load_kmt.start()
    for k in range(len(CHUNKS) - 1):
        for i in range(3):
            load(i, k).start(priority=0 if k == 0 else 1)
    load_forcing.start(priority=1)

    lane = lanes((8, LW))
    row = rows((8, LW))
    load_mask.wait()
    load_kmt.wait()
    for r in range(0, H, 8):
        keep = jnp.zeros((8, LW), jnp.int32)
        for b in range(W // BSX):
            inside = (lane >= b * BSX) & (lane < (b + 1) * BSX)
            upper = jnp.where(row + r < BSY, mask[0, b], mask[1, b])
            keep = jnp.where(inside, upper, keep)
        lev = widen(kmt[r : r + 8, :], LW) * keep
        lev_ref[r : r + 8, :] = lev.astype(F32)
    for r in range(0, H, 8):
        here = slice(r, r + 8)
        lev = lev_ref[here, :]
        if r + 8 < H:
            north = lev_ref[r + 1 : r + 9, :]
        else:
            north = jnp.where(row == 7, 0.0, roll(lev, -1, 0))
        min_e[here, :] = jnp.minimum(lev, roll(lev, -1, 1))
        min_n[here, :] = jnp.minimum(lev, north)
        lev_x[here, :] = strip(lev_ref, here)
        min_ex[here, :] = strip(min_e, here)
        min_nx[here, :] = strip(min_n, here)
    row_n[...] = jnp.zeros((32, LW), F32)
    row_s[...] = jnp.zeros((16, LW), F32)

    lane = lanes((8, 128))
    row = rows((8, 128))

    def pack(levels, r, east, west):
        here = slice(r, r + 8)
        for k in levels:
            t = t_x[k, here, :]
            east = jnp.where(lane == TR0 + k, roll(t, TR0 + k - 103, 1), east)
            east = jnp.where(lane == VE0 + k, roll(u_x[k, here, :], VE0 + k - 103, 1), east)
            west = jnp.where(lane == TR0 + k, roll(t, TR0 + k, 1), west)
        return east, west

    load(0, 0).wait()
    for r in range(0, H, 8):
        t_x[0, r : r + 8, :] = strip(t_s, 0, slice(r, r + 8))
    for k in range(KL):
        if k + 1 in CHUNKS[:-1]:
            load(0, CHUNKS.index(k + 1)).wait()
        if k in CHUNKS:
            load(1, CHUNKS.index(k)).wait()
            load(2, CHUNKS.index(k)).wait()
        if k == EARLY:
            for r in range(0, H, 8):
                zero = jnp.zeros((8, 128), F32)
                msg_e[r : r + 8, :], msg_w[r : r + 8, :] = pack(range(EARLY), r, zero, zero)
        kf = float(k)
        f_low = jnp.zeros((8, 128), F32)
        t = t_x[k, 0:8, :]
        t_turned = roll(t, -1, 0)
        for r in range(0, H, 8):
            here = slice(r, r + 8)
            if r + 8 < H:
                ahead = t_x[k, r + 8 : r + 16, :]
                ahead_turned = roll(ahead, -1, 0)
                t_n = jnp.where(row == 7, ahead_turned, t_turned)
            else:
                ahead = ahead_turned = None
                t_n = t_turned
            t_e = roll(t, -1, 1)
            u = strip(u_s, k, here)
            u_x[k, here, :] = u
            f_e = (t_e - t) - (ADV / GRAD * u) * (t + t_e)
            f_n = (t_n - t) - (ADV / GRAD * strip(v_s, k, here)) * (t + t_n)
            f_e = jnp.where(min_ex[here, :] > kf, f_e, 0.0)
            f_n = jnp.where(min_nx[here, :] > kf, f_n, 0.0)
            f_w = roll(f_e, 1, 1)
            f_turned = roll(f_n, 1, 0)
            f_s = jnp.where(row == 0, f_low, f_turned)
            f_low = f_turned
            lev = lev_x[here, :]
            gain = (f_e - f_w) + (f_n - f_s)
            if k + 1 < KL:
                above = strip(t_s, k + 1, here)
                t_x[k + 1, here, :] = above
                step = jnp.where(lev > kf + 1.0, VERT / GRAD * (above - t), 0.0)
                gain = gain + step
            if k > 0:
                gain = gain - drop[here, :]
            if k + 1 < KL:
                drop[here, :] = step
            share = jnp.where(lev > kf, thickness(kf) * (t + GRAD * gain), 0.0)
            col[here, :] = share if k == 0 else col[here, :] + share
            t, t_turned = ahead, ahead_turned
        row_s[k : k + 1, :] = widen(t_s[k, 0:1, :], LW)
        row_n[k : k + 1, :] = widen(t_s[k, H - 1 : H, :], LW)
        row_n[16 + k : 17 + k, :] = widen(v_s[k, H - 1 : H, :], LW)

    load_forcing.wait()
    for r in range(0, H, 8):
        here = slice(r, r + 8)
        lev = lev_x[here, :]
        rhs = jnp.where(lev > 0.0, ROOT * col[here, :] + strip(forcing, here), 0.0)
        east, west = pack(range(EARLY, KL), r, msg_e[here, :], msg_w[here, :])
        head_e = jnp.where(lane < LEV0, roll(rhs, 32, 1), roll(lev, LEV0 - 95, 1))
        head_w = jnp.where(lane < LEV0, rhs, roll(lev, LEV0, 1))
        east = jnp.where(lane < TR0, head_e, east)
        west = jnp.where(lane < TR0, head_w, west)
        if r < 16:
            for at, src, base in ((C_T0, row_s, 0), (C_T1, row_n, 0), (C_V1, row_n, 16)):
                inside = (lane >= at) & (lane < at + 8)
                piece = src[base + r : base + r + 8, :]
                east = jnp.where(inside, roll(piece[:, 256:], at - 96, 1), east)
                west = jnp.where(inside, roll(piece[:, :128], at, 1), west)
        msg_e[here, :] = east
        msg_w[here, :] = west
    for dst, src in ((out_e, msg_e), (out_w, msg_w)):
        for r in range(0, THIRD, 8):
            value = src[r : r + 8, :]
            for i in (1, 2):
                part = roll(src[r + THIRD * i : r + THIRD * i + 8, :], WIDTH * i, 1)
                value = jnp.where(lane < WIDTH * i, value, part)
            dst[r : r + 8, :] = value
        dst[THIRD : THIRD + 16, :] = src[0:16, :]


def outer_part(mask, kmt, forcing, tracer, east, north):
    vmem = pl.BlockSpec(memory_space=pltpu.VMEM)
    hbm = pl.BlockSpec(memory_space=pltpu.HBM)
    shape = jax.ShapeDtypeStruct
    return pl.pallas_call(
        outer_kernel,
        out_shape=[shape((KL, H, W), F32)] * 3
        + [shape((H, W), F32)]
        + [shape((H, LW), F32)] * 3
        + [shape((H, 128), F32)] * 2
        + [shape((THIRD + 16, 128), F32)] * 2
        + [shape((32, LW), F32), shape((16, LW), F32)],
        in_specs=[hbm] * 6,
        out_specs=[vmem] * 13,
        scratch_shapes=[pltpu.VMEM((H, W), jnp.int32), pltpu.SMEM(mask.shape, jnp.int32)]
        + [pltpu.VMEM((KL, H, 128), F32)] * 2
        + [pltpu.VMEM((H, 128), F32)] * 5
        + [pltpu.SemaphoreType.DMA((3, len(CHUNKS) - 1)), pltpu.SemaphoreType.DMA((3,))],
        compiler_params=pltpu.CompilerParams(vmem_limit_bytes=VMEM_LIMIT),
        name="outer",
    )(*(pltpu.with_memory_space_constraint(x, pltpu.HBM) for x in (mask, kmt, forcing, tracer, east, north)))


def tracer_kernel(t_s, u_s, v_s, forcing, lev_ref, min_e, min_n, partial, rhs_ref, col, drop):
    row = rows((8, W))
    for r in range(0, H, 8):
        col[r : r + 8, :] = jnp.zeros((8, W), F32)
        drop[r : r + 8, :] = jnp.zeros((8, W), F32)

    def level(k, carry):
        kf = k.astype(F32)
        thick = thickness(kf)
        above = jnp.minimum(k + 1, KL - 1)
        f_low = jnp.zeros((8, W), F32)
        t = t_s[k, 0:8, :]
        t_turned = roll(t, -1, 0)
        for r in range(0, H, 8):
            here = slice(r, r + 8)
            if r + 8 < H:
                ahead = t_s[k, r + 8 : r + 16, :]
                ahead_turned = roll(ahead, -1, 0)
                t_n = jnp.where(row == 7, ahead_turned, t_turned)
            else:
                ahead = ahead_turned = None
                t_n = t_turned
            t_e = roll(widen(t, LW), -1, 1)[:, :W]
            f_e = (t_e - t) - (ADV / GRAD * u_s[k, here, :]) * (t + t_e)
            f_n = (t_n - t) - (ADV / GRAD * v_s[k, here, :]) * (t + t_n)
            f_e = jnp.where(min_e[here, :W] > kf, f_e, 0.0)
            f_n = jnp.where(min_n[here, :W] > kf, f_n, 0.0)
            f_w = roll(widen(f_e, LW), 1, 1)[:, :W]
            f_turned = roll(f_n, 1, 0)
            f_s = jnp.where(row == 0, f_low, f_turned)
            f_low = f_turned
            lev = lev_ref[here, :W]
            step = VERT / GRAD * (t_s[above, here, :] - t)
            step = jnp.where(lev > kf + 1.0, step, 0.0)
            gain = (f_e - f_w) + (f_n - f_s) + (step - drop[here, :])
            drop[here, :] = step
            updated = t + GRAD * gain
            partial[k, here, :] = updated
            col[here, :] += jnp.where(lev > kf, thick * updated, 0.0)
            t, t_turned = ahead, ahead_turned
        return carry

    lax.fori_loop(0, KL, level, 0)
    for r in range(0, H, 8):
        here = slice(r, r + 8)
        rhs = ROOT * col[here, :] + forcing[here, :]
        rhs_ref[here, :] = widen(jnp.where(lev_ref[here, :W] > 0.0, rhs, 0.0), LW)


def tracer_part(t_s, u_s, v_s, forcing, lev, min_e, min_n):
    vmem = pl.BlockSpec(memory_space=pltpu.VMEM)
    shape = jax.ShapeDtypeStruct
    return pl.pallas_call(
        tracer_kernel,
        out_shape=[shape((KL, H, W), F32), shape((H, LW), F32)],
        in_specs=[vmem] * 7,
        out_specs=[vmem] * 2,
        scratch_shapes=[pltpu.VMEM((H, W), F32)] * 2,
        compiler_params=pltpu.CompilerParams(vmem_limit_bytes=VMEM_LIMIT),
        name="tracer",
    )(t_s, u_s, v_s, forcing, lev, min_e, min_n)


def sides_kernel(
    sent_w, sent_e, own_e, own_w, rhs_ref, lev_ref, row_n, row_s,
    rhs_x, lev_x, msg_n, msg_s, flux_e, flux_w,
    from_w, from_e, sum_e, sum_w,
):
    for dst, src in ((from_w, sent_w), (from_e, sent_e)):
        for i in range(3):
            dst[THIRD * i : THIRD * i + THIRD, :] = roll(src[0:THIRD, :], -WIDTH * i, 1)
    from_lane = rows((128, 128))

    def spread(x, first, count, precision):
        chosen = (from_lane >= first) & (from_lane < first + count)
        return jnp.dot(
            x, jnp.where(chosen, 1.0, 0.0), precision=precision, preferred_element_type=F32
        )

    def level_at(ref, at):
        return spread(ref[...], at, 1, lax.Precision.DEFAULT)

    lane = lanes((H, 128))
    kf = (lane - TR0).astype(F32)
    inside = (lane >= TR0) & (lane < TR0 + KL)
    weight = ROOT * thickness(kf)
    lev_w = jnp.minimum(level_at(from_w, LEV0 + 8), level_at(own_w, LEV0))
    lev_e = jnp.minimum(level_at(from_e, LEV0), level_at(own_e, LEV0 + 8))
    mw, me, mine_w, mine_e = from_w[...], from_e[...], own_w[...], own_e[...]
    f_w = GRAD * (mine_w - mw) - (ADV * roll(mw, TR0 - VE0, 1)) * (mine_w + mw)
    f_e = GRAD * (me - mine_e) - (ADV * roll(mine_e, TR0 - VE0, 1)) * (me + mine_e)
    f_w = jnp.where(inside & (lev_w > kf), f_w, 0.0)
    f_e = jnp.where(inside & (lev_e > kf), f_e, 0.0)
    flux_w[...] = f_w
    flux_e[...] = f_e
    sum_w[...] = spread(weight * f_w, TR0, KL, lax.Precision.HIGHEST)
    sum_e[...] = spread(weight * f_e, TR0, KL, lax.Precision.HIGHEST)
    lane = lanes((8, 128))
    for r in range(0, H, 8):
        here = slice(r, r + 8)
        mw, me = from_w[here, :], from_e[here, :]
        c_w, c_e = sum_w[here, :], sum_e[here, :]
        rhs_x[here, :128] = rhs_ref[here, :128] - jnp.where(lane == 0, c_w, 0.0)
        rhs_x[here, 128:256] = rhs_ref[here, 128:256]
        last = rhs_ref[here, 256:]
        last = jnp.where((lane >= 104) & (lane < 112), roll(me, 104, 1), last)
        last = jnp.where(lane >= 120, roll(mw, 120, 1), last)
        last = last + jnp.where(lane == 103, c_e, 0.0) - jnp.where(lane == 104, c_e, 0.0)
        rhs_x[here, 256:] = last + jnp.where(lane == 127, c_w, 0.0)
        lev_x[here, :256] = lev_ref[here, :256]
        last = lev_ref[here, 256:]
        last = jnp.where((lane >= 104) & (lane < 113), roll(me, 104 - LEV0, 1), last)
        last = jnp.where(lane >= 119, roll(mw, 119 - LEV0, 1), last)
        lev_x[here, 256:] = last
    msg_n[0:8, :] = rhs_x[H - 8 : H, :]
    msg_s[0:8, :] = rhs_x[0:8, :]
    msg_n[R_LEV : R_LEV + 8, :] = lev_x[H - 8 : H, :]
    msg_s[R_LEV : R_LEV + 8, :] = lev_x[0:8, :]
    for dst, at, src, base, lane0 in (
        (msg_s, R_TR, row_s, 0, C_T0), (msg_n, R_TR, row_n, 0, C_T1), (msg_n, R_VE, row_n, 16, C_V1),
    ):
        for r in (0, 8):
            corner = slice(THIRD + r, THIRD + r + 8)
            mw, me = sent_w[corner, :], sent_e[corner, :]
            piece = src[base + r : base + r + 8, :]
            last = piece[:, 256:]
            last = jnp.where((lane >= 104) & (lane < 112), roll(me, 104 - lane0, 1), last)
            last = jnp.where(lane >= 120, roll(mw, 120 - lane0, 1), last)
            dst[at + r : at + r + 8, :256] = piece[:, :256]
            dst[at + r : at + r + 8, 256:] = last
    msg_n[R_NINTH : R_NINTH + 1, :] = lev_x[H - 9 : H - 8, :]
    msg_s[R_NINTH : R_NINTH + 1, :] = lev_x[8:9, :]


def sides_part(from_w, from_e, own_e, own_w, rhs, lev, row_n, row_s):
    vmem = pl.BlockSpec(memory_space=pltpu.VMEM)
    shape = jax.ShapeDtypeStruct
    return pl.pallas_call(
        sides_kernel,
        out_shape=[
            shape((H, LW), F32),
            shape((H, LW), F32),
            shape((48, LW), F32),
            shape((32, LW), F32),
            shape((H, 128), F32),
            shape((H, 128), F32),
        ],
        in_specs=[vmem] * 8,
        out_specs=[vmem] * 6,
        scratch_shapes=[pltpu.VMEM((H, 128), F32)] * 4,
        compiler_params=pltpu.CompilerParams(vmem_limit_bytes=VMEM_LIMIT),
        name="sides",
    )(from_w, from_e, own_e, own_w, rhs, lev, row_n, row_s)


def basis_kernel(
    from_s, from_n, own_n, own_s, rhs_ref, lev_ref, partial,
    basis, diag, sums, updated,
    lev_x, rhs_x, w_e, w_w, w_n, w_s, weight, parts, slab_n, slab_s, sem,
):
    high, low = pl.ds(H - 8, 8), pl.ds(0, 8)
    loads = (
        pltpu.make_async_copy(partial.at[:, high, :], slab_n, sem.at[0]),
        pltpu.make_async_copy(partial.at[:, low, :], slab_s, sem.at[1]),
    )
    stores = (
        pltpu.make_async_copy(slab_n, updated.at[:, high, :], sem.at[2]),
        pltpu.make_async_copy(slab_s, updated.at[:, low, :], sem.at[3]),
    )
    for load in loads:
        load.start()
    lev_row = rows((16, LW))
    kf = lev_row.astype(F32)
    factor = ROOT * thickness(kf)

    def flux(t_from, t_to, vel, lev):
        value = GRAD * (t_to - t_from) - (ADV * vel) * (t_from + t_to)
        return jnp.where((lev_row < KL) & (lev > kf), value, 0.0)

    tr = slice(R_TR, R_TR + 16)
    ve = slice(R_VE, R_VE + 16)
    lev_n = jnp.minimum(lev_ref[H - 1 : H, :], from_n[R_LEV : R_LEV + 1, :])
    lev_s = jnp.minimum(lev_ref[0:1, :], from_s[R_LEV + 7 : R_LEV + 8, :])
    f_n = flux(own_n[tr, :], from_n[tr, :], own_n[ve, :], lev_n)
    f_s = flux(from_s[tr, :], own_s[tr, :], from_s[ve, :], lev_s)
    c_n = jnp.sum(factor * f_n, axis=0, keepdims=True)
    c_s = jnp.sum(factor * f_s, axis=0, keepdims=True)

    row = rows((8, LW))
    ninth = jnp.where(row == 7, from_s[R_NINTH : R_NINTH + 1, :], 0.0)
    ninth = jnp.where(row == 0, from_n[R_NINTH : R_NINTH + 1, :], ninth)
    tiles(lev_x, slice(0, H), lev_ref[...])
    tiles(lev_x, slice(H, H + 8), from_n[R_LEV : R_LEV + 8, :])
    tiles(lev_x, slice(H + 8, H + 16), ninth)
    tiles(lev_x, slice(H + 16, EH), from_s[R_LEV : R_LEV + 8, :])
    tiles(rhs_x, slice(0, 8), rhs_ref[0:8, :] - jnp.where(row == 0, c_s, 0.0))
    tiles(rhs_x, slice(8, H - 8), rhs_ref[8 : H - 8, :])
    tiles(rhs_x, slice(H - 8, H), rhs_ref[H - 8 : H, :] + jnp.where(row == 7, c_n, 0.0))
    tiles(rhs_x, slice(H, H + 8), from_n[0:8, :] - jnp.where(row == 0, c_n, 0.0))
    tiles(rhs_x, slice(H + 8, H + 16), jnp.zeros((8, LW), F32))
    tiles(rhs_x, slice(H + 16, EH), from_s[0:8, :] + jnp.where(row == 7, c_s, 0.0))

    def depth_of(i):
        lev = strided(lev_x, i, EB)
        return lev + lev * (lev - 1.0) * (0.25 / KL)

    def face(d, other):
        return jnp.where((d > 0.0) & (other > 0.0), 0.5 * (d + other), 0.0)

    lane = lanes((8, LW))
    first = depth_of(0)
    last = depth_of(EB - 1)
    beyond = roll(first, -1, 0)
    n_last = face(last, beyond)
    s = roll(n_last, 1, 0)
    lone = jnp.zeros((8, LW), F32)
    d = first
    for i in range(EB):
        if i < EB - 1:
            d_n = last if i == EB - 2 else depth_of(i + 1)
            n = face(d, d_n)
        else:
            d_n, n = beyond, n_last
        e = face(d, roll(d, -1, 1))
        w = roll(e, 1, 1)
        faces = (e + w) + (n + s)
        dg = jnp.where(d > 0.0, SHIFT * d + faces, 1.0)
        inv = 1.0 / dg
        z = strided(rhs_x, i, EB) * inv
        basis[0, i] = z
        inv = 2.0 * inv
        w_e[i] = e * inv
        w_w[i] = w * inv
        w_n[i] = n * inv
        w_s[i] = s * inv
        diag[i] = dg
        own = (lane < W) & (row * EB + i < H)
        own = jnp.where(own, dg, 0.0)
        joined = faces > 0.0
        weight[i] = jnp.where(joined, own, 0.0)
        lone = lone + jnp.where(joined, 0.0, own * z * z)
        d, s = d_n, n

    def fold(x):
        return jnp.sum(x[:, :128] + x[:, 128:256] + x[:, 256:], axis=0, keepdims=True)

    parts[...] = jnp.zeros((24, 128), F32)
    parts[16:17, :] = fold(lone)

    def step(k, older):
        now = basis.at[k - 1]
        even = jnp.zeros((8, LW), F32)
        odd = jnp.zeros((8, LW), F32)
        first = now[0]
        last = now[EB - 1]
        beyond = roll(first, -1, 0)
        c_s = roll(last, 1, 0)
        c = first
        for i in range(EB):
            if i < EB - 1:
                c_n = last if i == EB - 2 else now[i + 1]
            else:
                c_n = beyond
            image = w_e[i] * roll(c, -1, 1) + w_w[i] * roll(c, 1, 1)
            image = image + (w_n[i] * c_n + w_s[i] * c_s)
            value = 0.5 * image if older is None else image - basis[older, i]
            basis[k, i] = value
            scaled = weight[i] * c
            even = even + scaled * c
            odd = odd + scaled * value
            c_s, c = c, c_n
        parts[2 * k - 2 : 2 * k - 1, :] = fold(even)
        parts[2 * k - 1 : 2 * k, :] = fold(odd)

    step(1, None)
    for k in range(2, 4):
        step(k, k - 2)
    row360 = rows((8, W))
    for load in loads:
        load.wait()
    for k in range(KL):
        at_n = jnp.where(row360 == 7, f_n[k : k + 1, :W], 0.0)
        at_s = jnp.where(row360 == 0, f_s[k : k + 1, :W], 0.0)
        slab_n[k] = slab_n[k] + at_n
        slab_s[k] = slab_s[k] - at_s
    for store in stores:
        store.start()
    for k in range(4, ITERS + 1):
        step(k, k - 2)

    total = jnp.sum(parts[...], axis=1, keepdims=True)
    prow = rows((24, 128))
    plane = lanes((24, 128))
    place = (prow < 16) & ((plane == prow) | (plane == 128 - prow)) | (prow == 16) & (plane == 64)
    line = jnp.sum(jnp.where(place, total, 0.0), axis=0, keepdims=True)
    sums[...] = jnp.broadcast_to(line, sums.shape)
    for store in stores:
        store.wait()


def basis_part(from_s, from_n, own_n, own_s, rhs, lev, partial, count):
    vmem = pl.BlockSpec(memory_space=pltpu.VMEM)
    hbm = pl.BlockSpec(memory_space=pltpu.HBM)
    shape = jax.ShapeDtypeStruct
    return pl.pallas_call(
        basis_kernel,
        out_shape=[
            shape((ITERS + 1, EB, 8, LW), F32),
            shape((EB, 8, LW), F32),
            shape((count, 128), F32),
            shape((KL, H, W), F32),
        ],
        in_specs=[vmem] * 6 + [hbm],
        out_specs=[vmem] * 3 + [hbm],
        input_output_aliases={6: 3},
        scratch_shapes=[pltpu.VMEM((3, EH, 128), F32)] * 2
        + [pltpu.VMEM((EB, 8, LW), F32)] * 5
        + [pltpu.VMEM((24, 128), F32)]
        + [pltpu.VMEM((KL, 8, W), F32)] * 2
        + [pltpu.SemaphoreType.DMA((4,))],
        compiler_params=pltpu.CompilerParams(vmem_limit_bytes=VMEM_LIMIT),
        name="basis",
    )(from_s, from_n, own_n, own_s, rhs, lev, partial)


def polynomials(gathered):
    sums = jnp.broadcast_to(jnp.sum(gathered, axis=0, keepdims=True), (8, 128))

    def pick(lane):
        return jnp.broadcast_to(sums[:, lane : lane + 1], (8, 128))

    moments = [pick(j) for j in range(2 * ITERS)]
    alone = pick(64)
    now = [x if j < 2 else 2.0 * x - moments[j % 2] for j, x in enumerate(moments)]
    before = [0.0] * len(now)
    one = jnp.ones((8, 128), F32)
    rest, rest_before = [one], []
    lift, lift_before = [], []
    at0, at0_before = alone, 0.0
    at1, at1_before = one, 0.0

    def coefficient(p, j):
        return p[j] if 0 <= j < len(p) else None

    def total(terms):
        terms = [x for x in terms if x is not None]
        return sum(terms[1:], terms[0]) if terms else jnp.zeros((8, 128), F32)

    def advance(p, p_before, a, b, count, constant=None):
        out = []
        for j in range(count):
            terms = [constant if j == 0 else None]
            below, above = coefficient(p, j - 1), coefficient(p, j + 1)
            if below is not None:
                terms.append(below if j == 1 else 0.5 * below)
            if above is not None:
                terms.append(0.5 * above)
            if coefficient(p, j) is not None:
                terms.append(-(a * p[j]))
            if coefficient(p_before, j) is not None:
                terms.append(-(b * p_before[j]))
            out.append(total(terms))
        return out

    def lone_part(j):
        return (at0, None, -at0, None)[j % 4]

    last_inv = last_ratio = None
    for k in range(ITERS):
        size = total([now[k], lone_part(k)])
        cross = total([now[k + 1], lone_part(k + 1)])
        inv = jnp.where(size == 0.0, 0.0, 1.0 / size)
        ratio = cross * inv * (1.0 if k == 0 else 0.5)
        if k == 0:
            a, b = ratio, jnp.zeros((8, 128), F32)
        else:
            a, b = ratio - last_ratio, size * last_inv * (1.0 if k == 1 else 0.5)
        last_inv, last_ratio = inv, ratio
        after = [None] * len(now)
        for j in range(k + 1, 2 * ITERS - 1 - k):
            after[j] = 0.5 * (now[j - 1] + now[j + 1]) - a * now[j] - b * before[j]
        before, now = now, after
        lift, lift_before = advance(lift, lift_before, a, b, k + 1, at1), lift
        rest, rest_before = advance(rest, rest_before, a, b, k + 2), rest
        at0, at0_before = -(a * at0) - b * at0_before, at0
        at1, at1_before = (1.0 - a) * at1 - b * at1_before, at1
    scale = 1.0 / at1
    return [x * scale for x in lift], [x * scale for x in rest]


def finish_kernel(gathered, basis, diag, sea, residual, sea_t, residual_t):
    lift, rest = polynomials(gathered[...])
    for i in range(EB):
        for j in range(3):
            here = slice(128 * j, 128 * j + 128)
            c = basis[0, i, :, here]
            a, b = lift[0] * c, rest[0] * c
            for k in range(1, ITERS + 1):
                c = basis[k, i, :, here]
                b = b + rest[k] * c
                if k < ITERS:
                    a = a + lift[k] * c
            sea_t[j, pl.ds(i, 8, EB), :] = a
            residual_t[j, pl.ds(i, 8, EB), :] = diag[i, :, here] * b
    for out, by_tile in ((sea, sea_t), (residual, residual_t)):
        out[:, 0:128] = by_tile[0, :H, :]
        out[:, 128:256] = by_tile[1, :H, :]
        out[:, 256:W] = by_tile[2, :H, : W - 256]


def finish_part(gathered, basis, diag):
    vmem = pl.BlockSpec(memory_space=pltpu.VMEM)
    shape = jax.ShapeDtypeStruct
    return pl.pallas_call(
        finish_kernel,
        out_shape=[shape((H, W), F32), shape((H, W), F32)],
        in_specs=[vmem] * 3,
        out_specs=[vmem] * 2,
        scratch_shapes=[pltpu.VMEM((3, EH, 128), F32)] * 2,
        compiler_params=pltpu.CompilerParams(vmem_limit_bytes=VMEM_LIMIT),
        name="finish",
    )(gathered, basis, diag)


def edges_kernel(partial, flux_e, flux_w, dst, level, sem):
    def store(k):
        return pltpu.make_async_copy(level.at[k], dst.at[k], sem.at[k])

    lane = lanes((8, 128))
    lane_e = lanes((8, W - 256))
    for k in range(KL):
        for r in range(0, H, 8):
            here = slice(r, r + 8)
            at_w = jnp.where(lane == 0, roll(flux_w[here, :], -TR0 - k, 1), 0.0)
            at_e = roll(flux_e[here, :], W - 257 - TR0 - k, 1)[:, : W - 256]
            at_e = jnp.where(lane_e == W - 257, at_e, 0.0)
            level[k, here, :128] = partial[k, here, :128] - at_w
            level[k, here, 128:256] = partial[k, here, 128:256]
            level[k, here, 256:W] = partial[k, here, 256:W] + at_e
        store(k).start()
    for k in range(KL):
        store(k).wait()


def edges_part(partial, flux_e, flux_w):
    vmem = pl.BlockSpec(memory_space=pltpu.VMEM)
    hbm = pl.BlockSpec(memory_space=pltpu.HBM)
    return pl.pallas_call(
        edges_kernel,
        out_shape=jax.ShapeDtypeStruct((KL, H, W), F32),
        in_specs=[vmem] * 3,
        out_specs=hbm,
        scratch_shapes=[pltpu.VMEM((KL, H, W), F32), pltpu.SemaphoreType.DMA((KL,))],
        compiler_params=pltpu.CompilerParams(vmem_limit_bytes=VMEM_LIMIT),
        name="edges",
    )(partial, flux_e, flux_w)


def shards(tracer, east_velocity, north_velocity, kmt, block_mask, surface_forcing):
    nx, ny = lax.axis_size("gx"), lax.axis_size("gy")
    *fields, lev, min_e, min_n, msg_e, msg_w, out_e, out_w, row_n, row_s = outer_part(
        block_mask, kmt, surface_forcing, tracer, east_velocity, north_velocity
    )
    from_w = lax.ppermute(out_e, "gx", [(i, (i + 1) % nx) for i in range(nx)])
    from_e = lax.ppermute(out_w, "gx", [((i + 1) % nx, i) for i in range(nx)])
    partial, rhs = tracer_part(*fields, lev, min_e, min_n)
    rhs_x, lev_x, msg_n, msg_s, flux_e, flux_w = sides_part(
        from_w, from_e, msg_e, msg_w, rhs, lev, row_n, row_s
    )
    from_s = lax.ppermute(msg_n, "gy", [(i, (i + 1) % ny) for i in range(ny)])
    from_n = lax.ppermute(msg_s, "gy", [((i + 1) % ny, i) for i in range(ny)])
    partial = edges_part(partial, flux_e, flux_w)
    basis, diag, sums, updated = basis_part(
        from_s, from_n, msg_n, msg_s, rhs_x, lev_x, partial, nx * ny
    )
    gathered = lax.all_to_all(sums, ("gx", "gy"), 0, 0, tiled=True)
    sea_level, residual = finish_part(gathered, basis, diag)
    return (updated, sea_level, residual)


def solution(mesh):
    in_specs = (
        P(None, "gy", "gx"),
        P(None, "gy", "gx"),
        P(None, "gy", "gx"),
        P("gy", "gx"),
        P("gy", "gx"),
        P("gy", "gx"),
    )
    out_specs = (P(None, "gy", "gx"), P("gy", "gx"), P("gy", "gx"))
    return jax.shard_map(shards, mesh=mesh, in_specs=in_specs, out_specs=out_specs, check_vma=False)
```
